32 devices in a mesh: sec: 2 (over x), gx: 8 (over z, y), gy: 2 (over core).
Axes of the slice: x: 2, y: 2, z: 4, core: 2. Of those that a mesh axis runs over, the one named last changes fastest.
Arguments:
- velocity: float32 [2, 3, 32, 64, 256], P('sec', None, None, 'gx', 'gy'), may hold values from -6 to 6
- turbine_cells: int32 [64, 3], replicated, may hold values from 0 to 255, as said below
- fringe_bounds: int32 [2], replicated, may hold values from 48 to 64, as said below
Outputs:
- velocity_next: float32 [2, 3, 32, 64, 256], P('sec', None, 'gx', None, 'gy')
- pressure: float32 [2, 32, 64, 256], P('sec', 'gx', None, 'gy')
The draws below stay inside these ranges and needn't reach their ends.
Inputs may be any that keep to these rules, and one draw needn't show every extreme that they name: `turbine_cells`: each turbine's streamwise index is below 32 and its vertical index lies from 4 to 27. fringe_bounds[0] < fringe_bounds[1] = 64; the fringe lies in the last quarter of the streamwise columns.
All inputs are finite; a program needn't handle non-finite values.
Results may differ from the reference program's by a relative error of at most 0.00018.
Values sent between devices are 32-bit elements; how exact they have to be, the bound alone decides.
No kernel may reach another device: no remote copies, remote signals or barrier semaphores. Data moves between devices by JAX's collectives and lax.ppermute only.
A program may use at most 64 MiB of HBM per device.

```python
import jax
import jax.numpy as jnp
from jax import lax

NZ = 32
TURB = 64
RADIUS = 4
NX = 64
NY = 256


def draw_turbine_cells(key, part):
    subkeys = jax.random.split(jax.random.fold_in(key, 11), 3)
    streamwise = jax.random.randint(subkeys[0], (TURB,), 0, NX // 2)
    across = jax.random.randint(subkeys[1], (TURB,), 0, NY)
    height = jax.random.randint(subkeys[2], (TURB,), RADIUS, NZ - RADIUS)
    return jnp.stack([streamwise, across, height], axis=1).astype(jnp.int32)


def draw_fringe_bounds(key, part):
    subkeys = jax.random.split(jax.random.fold_in(key, 23), 1)
    first_column = jax.random.randint(subkeys[0], (), NX * 3 // 4, NX * 7 // 8 + 1)
    last_column = jnp.zeros((), jnp.int32) + NX
    return jnp.stack([first_column, last_column]).astype(jnp.int32)


def block_scale(stream_key, shape, pieces, low, largest):
    factor_of = 1.0
    for dim, shards_of in pieces:
        heights = jax.random.uniform(jax.random.fold_in(jax.random.fold_in(stream_key, 6), dim), (shards_of,), jnp.float32, low / len(pieces), largest / len(pieces))
        factor_of = factor_of * jnp.repeat(jnp.exp(heights), shape[dim] // shards_of).reshape((-1,) + (1,) * (len(shape) - 1 - dim))
    return factor_of


def scatter_about(rng, extent, deviation, reach, shards=(), held_as=jnp.bfloat16):
    gain = block_scale(rng, extent, shards, -0.22, 0.18) if shards else 1.0
    entries = jax.random.normal(rng, extent, jnp.float32) * deviation * gain
    return jnp.minimum(jnp.maximum(entries, -reach), reach).astype(held_as)


def setup_inputs(seed: int = 0) -> dict:
    splits = jax.random.split(jax.random.key(seed), 4)
    velocity = scatter_about(splits[0], (2, 3, NZ, NX, NY), 1.0, 6.0, ((0, 2), (3, 8), (4, 2)), jnp.float32)
    turbine_cells = draw_turbine_cells(jax.random.fold_in(splits[3], 71), 0)
    fringe_bounds = draw_fringe_bounds(jax.random.fold_in(splits[3], 71), 0)
    return {"velocity": velocity, "turbine_cells": turbine_cells, "fringe_bounds": fringe_bounds}


TIME_STEP = 0.05
SMAG_COEFF = 0.1
THRUST_COEFF = 4.0
DRIVING_FORCE = 0.1
FRINGE_BLEND = 0.5
HIGHEST = lax.Precision.HIGHEST

def cas_table(row_index, column_index, length):
    product = row_index[:, None] * column_index[None, :] % length
    angle = product.astype(jnp.float32) * (2.0 * jnp.pi / length)
    return jnp.cos(angle) + jnp.sin(angle)

def shift_up(values):
    zeros = jnp.zeros_like(values[..., :1, :, :])
    return jnp.concatenate([values[..., 1:, :, :], zeros], axis=-3)

def shift_down(values):
    zeros = jnp.zeros_like(values[..., :1, :, :])
    return jnp.concatenate([zeros, values[..., :-1, :, :]], axis=-3)

def thomas(right_side, eigen_value):
    length = right_side.shape[0]
    inverses = []
    reduced = []
    for level_index in range(length):
        if level_index == 0:
            diagonal = eigen_value - 1.0
        elif level_index == length - 1:
            diagonal = eigen_value - 3.0
        else:
            diagonal = eigen_value - 2.0
        if level_index == 0:
            pivot_now = diagonal
            current = right_side[0] / pivot_now
        else:
            pivot_now = diagonal - inverses[-1]
            current = (right_side[level_index] - reduced[-1]) / pivot_now
        inverses.append(1.0 / pivot_now)
        reduced.append(current)
    solution = [reduced[-1]]
    for level_index in range(length - 2, -1, -1):
        solution.append(reduced[level_index] - inverses[level_index] * solution[-1])
    return jnp.stack(solution[::-1])

def disk_weights(turbine_cells):
    along_x = jnp.arange(NX, dtype=jnp.int32)
    along_y = jnp.arange(NY, dtype=jnp.int32)
    along_z = jnp.arange(NZ, dtype=jnp.int32)
    matches = (along_x[:, None] == turbine_cells[None, :, 0]).astype(jnp.float32)
    offset_y = (along_y[None, :] - turbine_cells[:, 1:2] + NY // 2) % NY - NY // 2
    offset_z = along_z[None, :] - turbine_cells[:, 2:3]
    distance = offset_z[:, :, None] * offset_z[:, :, None] + offset_y[:, None, :] * offset_y[:, None, :]
    inside = (distance <= RADIUS * RADIUS).astype(jnp.float32)
    return jnp.einsum('xt,tzy->zxy', matches, inside, precision=HIGHEST)

def tendency(velocity_now, farm_flag, disk_weight):
    plus_x = jnp.roll(velocity_now, -1, axis=-2)
    minus_x = jnp.roll(velocity_now, 1, axis=-2)
    plus_y = jnp.roll(velocity_now, -1, axis=-1)
    minus_y = jnp.roll(velocity_now, 1, axis=-1)
    plus_z = shift_up(velocity_now)
    minus_z = shift_down(velocity_now)
    gradients = [0.5 * (plus_x - minus_x), 0.5 * (plus_y - minus_y), 0.5 * (plus_z - minus_z)]
    strain_squares = jnp.zeros_like(velocity_now[0])
    for component in range(3):
        strain_squares = strain_squares + gradients[component][component] * gradients[component][component]
        for direction in range(component + 1, 3):
            shear = 0.5 * (gradients[direction][component] + gradients[component][direction])
            strain_squares = strain_squares + 2.0 * shear * shear
    viscosity = SMAG_COEFF * jnp.sqrt(2.0 * strain_squares)
    visc_plus_x = jnp.roll(viscosity, -1, axis=-2)
    visc_minus_x = jnp.roll(viscosity, 1, axis=-2)
    visc_plus_y = jnp.roll(viscosity, -1, axis=-1)
    visc_minus_y = jnp.roll(viscosity, 1, axis=-1)
    visc_plus_z = shift_up(viscosity)
    visc_minus_z = shift_down(viscosity)
    advection = 0.5 * (plus_x[0] * plus_x - minus_x[0] * minus_x)
    advection = advection + 0.5 * (plus_y[1] * plus_y - minus_y[1] * minus_y)
    advection = advection + 0.5 * (plus_z[2] * plus_z - minus_z[2] * minus_z)
    diffusion = 0.5 * (viscosity + visc_plus_x) * (plus_x - velocity_now) - 0.5 * (viscosity + visc_minus_x) * (velocity_now - minus_x)
    diffusion = diffusion + 0.5 * (viscosity + visc_plus_y) * (plus_y - velocity_now) - 0.5 * (viscosity + visc_minus_y) * (velocity_now - minus_y)
    diffusion = diffusion + 0.5 * (viscosity + visc_plus_z) * (plus_z - velocity_now) - 0.5 * (viscosity + visc_minus_z) * (velocity_now - minus_z)
    changes = diffusion - advection
    streamwise = DRIVING_FORCE - THRUST_COEFF * farm_flag * disk_weight * velocity_now[0] * jnp.abs(velocity_now[0])
    return jnp.concatenate([changes[:1] + streamwise[None], changes[1:]], axis=0)

def project(velocity_now):
    divergence = 0.5 * (jnp.roll(velocity_now[0], -1, axis=-2) - jnp.roll(velocity_now[0], 1, axis=-2))
    divergence = divergence + 0.5 * (jnp.roll(velocity_now[1], -1, axis=-1) - jnp.roll(velocity_now[1], 1, axis=-1))
    divergence = divergence + 0.5 * (shift_up(velocity_now[2]) - shift_down(velocity_now[2]))
    index_x = jnp.arange(NX, dtype=jnp.int32)
    index_y = jnp.arange(NY, dtype=jnp.int32)
    table_x = cas_table(index_x, index_x, NX)
    table_y = cas_table(index_y, index_y, NY)
    spectrum = jnp.einsum('kx,zxy->zky', table_x, divergence, precision=HIGHEST)
    spectrum = jnp.einsum('ly,zky->zkl', table_y, spectrum, precision=HIGHEST)
    eigen_value = 2.0 * jnp.cos(index_x.astype(jnp.float32) * (2.0 * jnp.pi / NX))[:, None]
    eigen_value = eigen_value + 2.0 * jnp.cos(index_y.astype(jnp.float32) * (2.0 * jnp.pi / NY))[None, :] - 4.0
    solved = thomas(spectrum, eigen_value)
    pressure = jnp.einsum('xk,zkl->zxl', table_x, solved, precision=HIGHEST) * (1.0 / NX)
    pressure = jnp.einsum('yl,zxl->zxy', table_y, pressure, precision=HIGHEST) * (1.0 / NY)
    gradient_x = 0.5 * (jnp.roll(pressure, -1, axis=1) - jnp.roll(pressure, 1, axis=1))
    gradient_y = 0.5 * (jnp.roll(pressure, -1, axis=2) - jnp.roll(pressure, 1, axis=2))
    above_level = jnp.concatenate([pressure[1:], -pressure[-1:]], axis=0)
    below_level = jnp.concatenate([pressure[:1], pressure[:-1]], axis=0)
    gradient_z = 0.5 * (above_level - below_level)
    return (velocity_now - jnp.stack([gradient_x, gradient_y, gradient_z]), pressure)

def reference(velocity, turbine_cells, fringe_bounds):
    disk_weight = disk_weights(turbine_cells)
    advanced = []
    for section in range(2):
        farm_flag = float(section)
        initial = velocity[section]
        segment_one = initial + TIME_STEP * tendency(initial, farm_flag, disk_weight)
        segment_two = 0.75 * initial + 0.25 * (segment_one + TIME_STEP * tendency(segment_one, farm_flag, disk_weight))
        segment_three = initial / 3.0 + 2.0 / 3.0 * (segment_two + TIME_STEP * tendency(segment_two, farm_flag, disk_weight))
        advanced.append(segment_three)
    along_x = jnp.arange(NX, dtype=jnp.int32)
    inside = ((along_x >= fringe_bounds[0]) & (along_x < fringe_bounds[1])).astype(jnp.float32)
    farm_blended = advanced[1] + FRINGE_BLEND * inside[:, None] * (advanced[0] - advanced[1])
    precursor_next, precursor_pressure = project(advanced[0])
    farm_next, farm_pressure = project(farm_blended)
    return (jnp.stack([precursor_next, farm_next]), jnp.stack([precursor_pressure, farm_pressure]))
```

```python
import functools

import jax
import jax.numpy as jnp
import numpy as np
from jax import lax
from jax.experimental import pallas as pl
from jax.experimental.pallas import tpu as pltpu
from jax.sharding import PartitionSpec as P

RADIUS = 4


TIME_STEP = 0.05
SMAG_COEFF = 0.1
THRUST_COEFF = 4.0
DRIVING_FORCE = 0.1
FRINGE_BLEND = 0.5
HIGHEST = lax.Precision.HIGHEST
STAGES = 3
REACH = 2 * STAGES + 1
LANES = 128
ROWS = 8
VMEM_BYTES = 48 * 1024 * 1024


def extended(x, sides, width):
    for axis, dim in sides:
        count, length = (lax.axis_size(axis), x.shape[dim])
        up = [(i, (i + 1) % count) for i in range(count)]
        down = [(j, i) for i, j in up]
        last = lax.slice_in_dim(x, length - width, length, axis=dim)
        initial = lax.slice_in_dim(x, 0, width, axis=dim)
        before = lax.ppermute(last, axis, up)
        after = lax.ppermute(initial, axis, down)
        x = jnp.concatenate([before, x, after], axis=dim)
    return x


def shifted(block, axis, distance):
    devices = range(lax.axis_size(axis))
    route = [(i - distance, i) for i in devices if i - distance in devices]
    return lax.ppermute(block, axis, route)


def cas_table(row_index, column_index, length):
    product = row_index[:, None] * column_index[None, :] % length
    angle = product.astype(jnp.float32) * (2.0 * jnp.pi / length)
    return jnp.cos(angle) + jnp.sin(angle)


def shift_up(values):
    zeros = jnp.zeros_like(values[..., :1, :, :])
    return jnp.concatenate([values[..., 1:, :, :], zeros], axis=-3)


def shift_down(values):
    zeros = jnp.zeros_like(values[..., :1, :, :])
    return jnp.concatenate([zeros, values[..., :-1, :, :]], axis=-3)


def thomas(right_side, eigen_value):
    length = right_side.shape[0]
    inverses = []
    reduced = []
    for level_index in range(length):
        if level_index == 0:
            diagonal = eigen_value - 1.0
        elif level_index == length - 1:
            diagonal = eigen_value - 3.0
        else:
            diagonal = eigen_value - 2.0
        if level_index == 0:
            pivot_now = diagonal
            current = right_side[0] / pivot_now
        else:
            pivot_now = diagonal - inverses[-1]
            current = (right_side[level_index] - reduced[-1]) / pivot_now
        inverses.append(1.0 / pivot_now)
        reduced.append(current)
    solution = [reduced[-1]]
    for level_index in range(length - 2, -1, -1):
        solution.append(reduced[level_index] - inverses[level_index] * solution[-1])
    return jnp.stack(solution[::-1])


def spanwise_derivative(values, sine_y):
    return -sine_y * jnp.roll(jnp.flip(values, axis=-1), 1, axis=-1)


def widened(values):
    return extended(values, (("gx", 1), ("gy", 2)), 1)


def disk_weights(turbine_cells, along_x, along_y, along_z, total_y):
    matches = (along_x[:, None] == turbine_cells[None, :, 0]).astype(jnp.float32)
    offset_y = (along_y[None, :] - turbine_cells[:, 1:2] + total_y // 2) % total_y - total_y // 2
    offset_z = along_z[None, :] - turbine_cells[:, 2:3]
    distance = (
        offset_z[:, :, None] * offset_z[:, :, None] + offset_y[:, None, :] * offset_y[:, None, :]
    )
    inside = (distance <= RADIUS * RADIUS).astype(jnp.float32)
    return jnp.einsum("xt,tzy->zxy", matches, inside, precision=HIGHEST)


def tendency(velocity_now, farm_flag, disk_weight):
    levels, cells_x, cells_y = (velocity_now.shape[1], velocity_now.shape[2], velocity_now.shape[3])
    border = widened(velocity_now.reshape(3 * levels, cells_x, cells_y)).reshape(
        3, levels, cells_x + 2, cells_y + 2
    )
    plus_x = border[:, :, 2:, 1:-1]
    minus_x = border[:, :, :-2, 1:-1]
    plus_y = border[:, :, 1:-1, 2:]
    minus_y = border[:, :, 1:-1, :-2]
    plus_z = shift_up(velocity_now)
    minus_z = shift_down(velocity_now)
    gradients = [0.5 * (plus_x - minus_x), 0.5 * (plus_y - minus_y), 0.5 * (plus_z - minus_z)]
    strain_squares = jnp.zeros_like(velocity_now[0])
    for component in range(3):
        strain_squares = (
            strain_squares + gradients[component][component] * gradients[component][component]
        )
        for direction in range(component + 1, 3):
            shear = 0.5 * (gradients[direction][component] + gradients[component][direction])
            strain_squares = strain_squares + 2.0 * shear * shear
    viscosity = SMAG_COEFF * jnp.sqrt(2.0 * strain_squares)
    visc_border = widened(viscosity)
    visc_plus_x = visc_border[:, 2:, 1:-1]
    visc_minus_x = visc_border[:, :-2, 1:-1]
    visc_plus_y = visc_border[:, 1:-1, 2:]
    visc_minus_y = visc_border[:, 1:-1, :-2]
    visc_plus_z = shift_up(viscosity)
    visc_minus_z = shift_down(viscosity)
    advection = 0.5 * (plus_x[0] * plus_x - minus_x[0] * minus_x)
    advection = advection + 0.5 * (plus_y[1] * plus_y - minus_y[1] * minus_y)
    advection = advection + 0.5 * (plus_z[2] * plus_z - minus_z[2] * minus_z)
    diffusion = 0.5 * (viscosity + visc_plus_x) * (plus_x - velocity_now) - 0.5 * (
        viscosity + visc_minus_x
    ) * (velocity_now - minus_x)
    diffusion = (
        diffusion
        + 0.5 * (viscosity + visc_plus_y) * (plus_y - velocity_now)
        - 0.5 * (viscosity + visc_minus_y) * (velocity_now - minus_y)
    )
    diffusion = (
        diffusion
        + 0.5 * (viscosity + visc_plus_z) * (plus_z - velocity_now)
        - 0.5 * (viscosity + visc_minus_z) * (velocity_now - minus_z)
    )
    changes = diffusion - advection
    streamwise = DRIVING_FORCE - THRUST_COEFF * farm_flag * disk_weight * velocity_now[0] * jnp.abs(
        velocity_now[0]
    )
    return jnp.concatenate([changes[:1] + streamwise[None], changes[1:]], axis=0)


def general_plan(velocity, turbine_cells, fringe_bounds):
    initial = velocity[0]
    levels, cells_x, cells_y = (initial.shape[1], initial.shape[2], initial.shape[3])
    total_y = cells_y * lax.axis_size("gy")
    x_anchor = lax.axis_index("gx") * cells_x
    y_anchor = lax.axis_index("gy") * cells_y
    farm_flag = lax.axis_index("sec").astype(jnp.float32)
    along_x = x_anchor + jnp.arange(cells_x, dtype=jnp.int32)
    along_y = y_anchor + jnp.arange(cells_y, dtype=jnp.int32)
    along_z = jnp.arange(levels, dtype=jnp.int32)
    disk_weight = disk_weights(turbine_cells, along_x, along_y, along_z, total_y)
    segment_one = initial + TIME_STEP * tendency(initial, farm_flag, disk_weight)
    segment_two = 0.75 * initial + 0.25 * (
        segment_one + TIME_STEP * tendency(segment_one, farm_flag, disk_weight)
    )
    segment_three = initial / 3.0 + 2.0 / 3.0 * (
        segment_two + TIME_STEP * tendency(segment_two, farm_flag, disk_weight)
    )
    regrouped = lax.all_to_all(segment_three, "gx", split_axis=1, concat_axis=2, tiled=True)
    count_x = regrouped.shape[2]
    quarter = count_x // 4
    cut_at = count_x - quarter
    outlet_part = regrouped[:, :, cut_at:, :]
    upstream = shifted(outlet_part, "sec", 1)
    columns = cut_at + jnp.arange(quarter, dtype=jnp.int32)
    inside = ((columns >= fringe_bounds[0]) & (columns < fringe_bounds[1])).astype(jnp.float32)
    weight = FRINGE_BLEND * farm_flag * inside
    blended_part = outlet_part + weight[:, None] * (upstream - outlet_part)
    regrouped = jnp.concatenate([regrouped[:, :, :cut_at, :], blended_part], axis=2)
    index_x = jnp.arange(count_x, dtype=jnp.int32)
    table_x = cas_table(index_x, index_x, count_x)
    gradient_u = 0.5 * (jnp.roll(regrouped[0], -1, axis=1) - jnp.roll(regrouped[0], 1, axis=1))
    fields = jnp.stack([gradient_u, regrouped[1], regrouped[2]])
    spectral_x = jnp.einsum("kx,czxy->czky", table_x, fields, precision=HIGHEST)
    columns_view = lax.all_to_all(
        lax.all_to_all(spectral_x, "gx", split_axis=2, concat_axis=1, tiled=True),
        "gy",
        split_axis=2,
        concat_axis=3,
        tiled=True,
    )
    slice_width = columns_view.shape[2]
    count_y = columns_view.shape[3]
    index_y = jnp.arange(count_y, dtype=jnp.int32)
    table_y = cas_table(index_y, index_y, count_y)
    spectrum = jnp.einsum("ly,czky->czkl", table_y, columns_view, precision=HIGHEST)
    sine_y = jnp.sin(index_y.astype(jnp.float32) * (2.0 * jnp.pi / count_y))
    source = (
        spectrum[0]
        + spanwise_derivative(spectrum[1], sine_y)
        + 0.5 * (shift_up(spectrum[2]) - shift_down(spectrum[2]))
    )
    wave_x = (
        lax.axis_index("gx") * cells_x
        + lax.axis_index("gy") * slice_width
        + jnp.arange(slice_width, dtype=jnp.int32)
    )
    eigen_value = 2.0 * jnp.cos(wave_x.astype(jnp.float32) * (2.0 * jnp.pi / count_x))[:, None]
    eigen_value = (
        eigen_value
        + 2.0 * jnp.cos(index_y.astype(jnp.float32) * (2.0 * jnp.pi / count_y))[None, :]
        - 4.0
    )
    solved = thomas(source, eigen_value)
    above_level = jnp.concatenate([solved[1:], -solved[-1:]], axis=0)
    below_level = jnp.concatenate([solved[:1], solved[:-1]], axis=0)
    coefficients = jnp.stack(
        [solved, spanwise_derivative(solved, sine_y), 0.5 * (above_level - below_level)]
    )
    physical_y = jnp.einsum("yl,czkl->czky", table_y, coefficients, precision=HIGHEST) * (
        1.0 / count_y
    )
    returned = lax.all_to_all(
        lax.all_to_all(physical_y, "gx", split_axis=1, concat_axis=2, tiled=True),
        "gy",
        split_axis=3,
        concat_axis=2,
        tiled=True,
    )
    group_size = count_x // lax.axis_size("gy")
    wave_back = (
        index_x // slice_width % lax.axis_size("gx") * cells_x
        + index_x // group_size * slice_width
        + index_x % slice_width
    )
    inverse_table = cas_table(index_x, wave_back, count_x)
    physical = jnp.einsum("xp,czpy->czxy", inverse_table, returned, precision=HIGHEST) * (
        1.0 / count_x
    )
    pressure = physical[0]
    gradient_p = 0.5 * (jnp.roll(pressure, -1, axis=1) - jnp.roll(pressure, 1, axis=1))
    velocity_next = regrouped - jnp.stack([gradient_p, physical[1], physical[2]])
    return (velocity_next[None], pressure[None])


def dot(left, right):
    return jnp.dot(left, right, precision=HIGHEST, preferred_element_type=jnp.float32)


def swap_blocks(arrays, width):
    arrays = list(arrays)
    block = lax.broadcasted_iota(jnp.int32, arrays[0].shape, 1) // width
    step = 1
    while step < len(arrays):
        low = (block // step) % 2 == 0
        for index in range(len(arrays)):
            if (index // step) % 2 == 0:
                first, second = arrays[index], arrays[index + step]
                arrays[index] = jnp.where(low, first, pltpu.roll(second, step * width, 1))
                arrays[index + step] = jnp.where(
                    low, pltpu.roll(first, LANES - step * width, 1), second
                )
        step *= 2
    return arrays


def advance_kernel(
    total_x,
    meta,
    own_here,
    own_there,
    left_here,
    left_there,
    right_here,
    right_there,
    thrust,
    table_y,
    table_z,
    moved,
    spectra,
    start,
    stage_a,
    stage_b,
    viscosity,
    source,
    columns_out,
    modes,
):
    cells_x, _, levels, half = own_here.shape
    width = 2 * half
    level = lax.broadcasted_iota(jnp.int32, (levels, width), 0)
    top = level == levels - 1
    bottom = level == 0

    for first, here, there in (
        (0, left_here, left_there),
        (REACH, own_here, own_there),
        (REACH + cells_x, right_here, right_there),
    ):
        start[pl.ds(first, here.shape[0]), :, :, :half] = here[...]
        start[pl.ds(first, here.shape[0]), :, :, half:] = there[...]

    def next_y(f):
        return pltpu.roll(f, width - 1, 1)

    def last_y(f):
        return pltpu.roll(f, 1, 1)

    def next_z(f):
        return jnp.where(top, 0.0, pltpu.roll(f, levels - 1, 0))

    def last_z(f):
        return jnp.where(bottom, 0.0, pltpu.roll(f, 1, 0))

    def set_viscosity(now, first, end):
        def column(i, carry):
            here = [now[i, c] for c in range(3)]
            d_x = [now[i + 1, c] - now[i - 1, c] for c in range(3)]
            d_y = [next_y(f) - last_y(f) for f in here]
            d_z = [next_z(f) - last_z(f) for f in here]
            diagonal = d_x[0] * d_x[0] + d_y[1] * d_y[1] + d_z[2] * d_z[2]
            xy = d_x[1] + d_y[0]
            xz = d_x[2] + d_z[0]
            yz = d_y[2] + d_z[1]
            total = (diagonal + diagonal) + (xy * xy + xz * xz + yz * yz)
            viscosity[i] = (0.5 * SMAG_COEFF) * jnp.sqrt(total)
            return carry

        lax.fori_loop(first, end, column, 0)

    def face_x(now, i):
        here = [now[i, c] for c in range(3)]
        after = [now[i + 1, c] for c in range(3)]
        both = viscosity[i] + viscosity[i + 1]
        return [
            both * (after[c] - here[c]) - (here[0] * here[c] + after[0] * after[c])
            for c in range(3)
        ]

    def advance(now, then, first, end, keep, gain):
        def column(i, before):
            here = [now[i, c] for c in range(3)]
            eddy = viscosity[i]
            ahead = face_x(now, i)
            plus_y = [next_y(f) for f in here]
            both_y = eddy + next_y(eddy)
            plus_z = [next_z(f) for f in here]
            both_z = eddy + next_z(eddy)
            for c in range(3):
                flux_y = both_y * (plus_y[c] - here[c]) - (here[1] * here[c] + plus_y[1] * plus_y[c])
                flux_z = both_z * (plus_z[c] - here[c]) - (here[2] * here[c] + plus_z[2] * plus_z[c])
                floor_z = eddy * here[c] - here[2] * here[c]
                below_z = jnp.where(bottom, floor_z, pltpu.roll(flux_z, 1, 0))
                change = 0.5 * (
                    (ahead[c] - before[c]) + (flux_y - last_y(flux_y)) + (flux_z - below_z)
                )
                if c == 0:
                    drag = thrust[i - 2] * here[0] * jnp.abs(here[0])
                    change = change + (DRIVING_FORCE - drag)
                moved_on = here[c] + TIME_STEP * change
                if keep == 0.0:
                    then[i, c] = moved_on
                else:
                    then[i, c] = keep * start[i, c] + gain * moved_on
            return ahead

        lax.fori_loop(first, end, column, face_x(now, first - 1))

    columns = start.shape[0]
    set_viscosity(start, 1, columns - 1)
    advance(start, stage_a, 2, columns - 2, 0.0, 1.0)
    set_viscosity(stage_a, 3, columns - 3)
    advance(stage_a, stage_b, 4, columns - 4, 0.75, 0.25)
    set_viscosity(stage_b, 5, columns - 5)
    advance(stage_b, stage_a, 6, columns - 6, 1.0 / 3.0, 2.0 / 3.0)

    section, anchor, fringe_first, fringe_end = (meta[0], meta[1], meta[2], meta[3])
    is_farm = section == 1

    def weight(offset, dest):
        place = lax.rem(anchor + offset + total_x, total_x)
        inside = jnp.logical_and(place >= fringe_first, place < fringe_end)
        blend = jnp.where(inside, FRINGE_BLEND, 0.0)
        share = jnp.where(is_farm, 1.0 - blend, blend)
        if dest == 0:
            return jnp.where(is_farm, 0.0, 1.0)
        return share

    for x in range(cells_x):
        i = REACH + x
        cross = stage_a[i, 1]
        upright = stage_a[i, 2]
        plane = (next_y(cross) - last_y(cross)) + (next_z(upright) - last_z(upright))
        after, before = stage_a[i + 1, 0], stage_a[i - 1, 0]
        for dest in range(2):
            source[pl.ds((dest * cells_x + x) * levels, levels), :] = 0.5 * (
                weight(x + 1, dest) * after - weight(x - 1, dest) * before + weight(x, dest) * plane
            )
        for c in range(3):
            columns_out[pl.ds((x * 3 + c) * levels, levels), :] = stage_a[i, c, :, :half]

    groups = moved.shape[0]
    share = levels // groups
    for c in range(3):
        for z in range(levels):
            row = columns_out[pl.ds(c * levels + z, cells_x, stride=3 * levels), :]
            moved[z // share, c, z % share] = row

    along_y = dot(source[...], table_y[...])
    for n in range(2 * cells_x):
        modes[pl.ds(n * levels, levels), :] = dot(
            table_z[...], along_y[n * levels : (n + 1) * levels]
        )
    lane_width = LANES // groups
    for dest in range(2):
        for a in range(levels // groups):
            picked = [
                modes[pl.ds(dest * cells_x * levels + a * groups + b, cells_x, stride=levels), :]
                for b in range(groups)
            ]
            for g, block in enumerate(swap_blocks(picked, lane_width)):
                spectra[dest, g, a] = block


def pencil_kernel(meta, received, inverse, table_x, spread_z, moved, upstream, packed):
    groups, parts, cells_x, lanes = received.shape[1:]
    total_x = groups * cells_x
    lane_width = lanes // groups
    pieces = []
    for a in range(parts):
        spectrum = (received[0, :, a] + received[1, :, a]).reshape(total_x, lanes)
        solved = dot(table_x[...], spectrum) * inverse[a]
        pieces.append(dot(table_x[...], solved))
    field = dot(jnp.concatenate(pieces, axis=1), spread_z[...])
    halves = [field[:, a * lanes : (a + 1) * lanes] for a in range(parts)]
    lane = lax.broadcasted_iota(jnp.int32, (total_x, lanes), 1)
    quarter = 2 * lane_width
    for g in range(groups):
        a = g * parts // groups
        if g % 2 == 0:
            edge = pltpu.roll(halves[max(a - 1, 0)], quarter, 1)
            packed[g, :total_x] = jnp.where(lane < quarter, edge, pltpu.roll(halves[a], quarter, 1))
        else:
            edge = pltpu.roll(halves[min(a + 1, parts - 1)], lanes - quarter, 1)
            packed[g, :total_x] = jnp.where(
                lane < lanes - quarter, pltpu.roll(halves[a], lanes - quarter, 1), edge
            )
    section, anchor, fringe_first, fringe_end = (meta[0], meta[1], meta[2], meta[3])
    place = anchor + lax.broadcasted_iota(jnp.int32, (cells_x, lanes), 0)
    inside = jnp.logical_and(place >= fringe_first, place < fringe_end)
    inside = jnp.logical_and(inside, section == 1)
    blend = jnp.where(inside, FRINGE_BLEND, 0.0)[None, None]
    for g in range(groups):
        own = moved[g]
        mixed = own + blend * (upstream[g] - own)
        packed[g, total_x:] = mixed.reshape(-1, lanes)


def project_kernel(meta, received, partner, table_y, velocity_next, pressure):
    groups = received.shape[0]
    total_x, lanes = partner.shape[1:]
    share = pressure.shape[0]
    cells_x = total_x // groups
    here = swap_blocks([received[s, :total_x] for s in range(groups)], lanes // groups)
    there = swap_blocks([partner[s] for s in range(groups)], lanes // groups)
    place = meta[4]
    fields = []
    for n in range(share + 2):
        both = jnp.concatenate([here[n + 1], there[n + 1]], axis=1)
        fields.append(dot(both, table_y[...]))
    values = [f[:, :lanes] for f in fields]
    values[0] = jnp.where(place == 0, values[1], values[0])
    values[-1] = jnp.where(place == groups - 1, -values[-2], values[-1])
    for z in range(share):
        now = values[z + 1]
        pressure[z] = now
        slopes = [
            0.5 * (pltpu.roll(now, total_x - 1, 0) - pltpu.roll(now, 1, 0)),
            fields[z + 1][:, lanes:],
            0.5 * (values[z + 2] - values[z]),
        ]
        for c in range(3):
            rows = total_x + (c * share + z) * cells_x
            blended = received[:, rows : rows + cells_x].reshape(total_x, lanes)
            velocity_next[c, z] = blended - slopes[c]


def cas(rows, columns, length):
    angle = (np.outer(rows, columns) % length) * (2.0 * np.pi / length)
    return np.cos(angle) + np.sin(angle)


def tables(levels, total_x, total_y, groups):
    half = total_y // 2
    lane_width = LANES // groups
    every_x = np.arange(total_x)
    every_y = np.arange(total_y)
    table_x = cas(every_x, every_x, total_x)
    table_y = cas(every_y, every_y, total_y)
    slope_y = 0.5 * (np.roll(table_y, -1, axis=1) - np.roll(table_y, 1, axis=1))
    level = np.arange(levels) + 0.5
    table_z = np.cos(np.outer(level, level) * (np.pi / levels))
    spread_z = np.kron(table_z, np.eye(lane_width))
    forward, backward = [], []
    for core in range(2):
        order = np.roll(every_y, -core * half)
        here = slice(core * half, (core + 1) * half)
        forward.append(table_y[order, here])
        backward.append(np.concatenate([table_y[order, here], slope_y[order, here]], axis=1))
    eigen = (
        (2.0 * np.cos(level * (np.pi / levels)) - 2.0)[:, None, None]
        + (2.0 * np.cos(every_x * (2.0 * np.pi / total_x)) - 2.0)[None, :, None]
        + (2.0 * np.cos(every_y * (2.0 * np.pi / total_y)) - 2.0)[None, None, :]
    )
    inverse = (2.0 / levels) / (total_x * total_y) / eigen
    inverse = inverse.reshape(levels // groups, groups, total_x, 2, groups, lane_width)
    inverse = inverse.transpose(4, 3, 0, 2, 1, 5).reshape(
        groups, 2, levels // groups, total_x, LANES
    )
    return [
        np.asarray(t, np.float32)
        for t in (table_x, np.stack(forward), np.stack(backward), table_z, spread_z, inverse)
    ]


def call(kernel, out_shapes, scratch, *operands):
    in_specs = [pl.BlockSpec(memory_space=pltpu.SMEM)]
    in_specs += [pl.BlockSpec(memory_space=pltpu.VMEM)] * (len(operands) - 1)
    return pl.pallas_call(
        kernel,
        out_shape=out_shapes,
        in_specs=in_specs,
        out_specs=jax.tree.map(lambda _: pl.BlockSpec(memory_space=pltpu.VMEM), out_shapes),
        scratch_shapes=scratch,
        compiler_params=pltpu.CompilerParams(vmem_limit_bytes=VMEM_BYTES),
    )(*operands)


def thrust_weights(turbine_cells, along_x, along_y, along_z, total_y, strength):
    matches = (along_x[:, None] == turbine_cells[None, :, 0]).astype(jnp.bfloat16)
    offset_y = (along_y[None, :] - turbine_cells[:, 1:2] + total_y // 2) % total_y - total_y // 2
    offset_z = along_z[None, :] - turbine_cells[:, 2:3]
    distance = (
        offset_z[:, :, None] * offset_z[:, :, None] + offset_y[:, None, :] * offset_y[:, None, :]
    )
    inside = (distance <= RADIUS * RADIUS).astype(jnp.bfloat16)
    count = jnp.einsum("xt,tzy->xzy", matches, inside, preferred_element_type=jnp.float32)
    return strength * count


def paired_plan(velocity, turbine_cells, fringe_bounds):
    groups = lax.axis_size("gx")
    initial = velocity[0]
    _, levels, cells_x, cells_y = initial.shape
    total_x, total_y = cells_x * groups, 2 * cells_y
    width = total_y
    share = levels // groups
    section, place, core = (lax.axis_index("sec"), lax.axis_index("gx"), lax.axis_index("gy"))
    table_x, forward, backward, table_z, spread_z, inverse = tables(
        levels, total_x, total_y, groups
    )
    meta = jnp.stack([section, place * cells_x, fringe_bounds[0], fringe_bounds[1], place])
    meta = meta.astype(jnp.int32)

    up = [(i, (i + 1) % groups) for i in range(groups)]
    down = [(j, i) for i, j in up]
    swap = [(0, 1), (1, 0)]
    own = jnp.transpose(initial, (2, 0, 1, 3))
    left = lax.ppermute(own[cells_x - REACH :], "gx", up)
    right = lax.ppermute(own[:REACH], "gx", down)
    own_there = lax.ppermute(own, "gy", swap)
    left_there = lax.ppermute(left, "gy", swap)
    right_there = lax.ppermute(right, "gy", swap)

    along_x = (place * cells_x + jnp.arange(-REACH + 2, cells_x + REACH - 2)) % total_x
    along_y = (core * cells_y + jnp.arange(total_y)) % total_y
    strength = THRUST_COEFF * section.astype(jnp.float32)
    thrust = thrust_weights(
        turbine_cells, along_x, along_y, jnp.arange(levels), total_y, strength
    )
    table_forward = lax.dynamic_index_in_dim(jnp.asarray(forward), core, 0, keepdims=False)
    table_backward = lax.dynamic_index_in_dim(jnp.asarray(backward), core, 0, keepdims=False)
    own_inverse = lax.dynamic_slice(
        jnp.asarray(inverse), (place, core, 0, 0, 0), (1, 1) + inverse.shape[2:]
    )[0, 0]

    columns = cells_x + 2 * REACH
    parts = levels // groups
    f32 = jnp.float32
    moved, spectra = call(
        functools.partial(advance_kernel, total_x),
        (
            jax.ShapeDtypeStruct((groups, 3, share, cells_x, cells_y), f32),
            jax.ShapeDtypeStruct((2, groups, parts, cells_x, LANES), f32),
        ),
        [
            pltpu.VMEM((columns, 3, levels, width), f32),
            pltpu.VMEM((columns, 3, levels, width), f32),
            pltpu.VMEM((columns, 3, levels, width), f32),
            pltpu.VMEM((columns, levels, width), f32),
            pltpu.VMEM((2 * cells_x * levels, width), f32),
            pltpu.VMEM((cells_x * 3 * levels, cells_y), f32),
            pltpu.VMEM((2 * cells_x * levels, LANES), f32),
        ],
        meta,
        own,
        own_there,
        left,
        left_there,
        right,
        right_there,
        thrust,
        table_forward,
        jnp.asarray(table_z),
    )
    fringe = [(g, groups + g) for g in range(groups - groups // 4, groups)]
    upstream = lax.ppermute(moved, ("sec", "gx"), fringe)
    received = lax.all_to_all(
        spectra.reshape(2 * groups, parts, cells_x, LANES), ("sec", "gx"), 0, 0, tiled=True
    ).reshape(2, groups, parts, cells_x, LANES)
    rows = total_x + 3 * share * cells_x
    packed = call(
        pencil_kernel,
        jax.ShapeDtypeStruct((groups, rows, LANES), f32),
        [],
        meta,
        received,
        own_inverse,
        jnp.asarray(table_x),
        jnp.asarray(spread_z),
        moved,
        upstream,
    )
    returned = lax.all_to_all(packed, "gx", 0, 0, tiled=True)
    partner = lax.ppermute(returned[:, :total_x], "gy", swap)
    velocity_next, pressure = call(
        project_kernel,
        (
            jax.ShapeDtypeStruct((3, share, total_x, cells_y), f32),
            jax.ShapeDtypeStruct((share, total_x, cells_y), f32),
        ),
        [],
        meta,
        returned,
        partner,
        table_backward,
    )
    return (velocity_next[None], pressure[None])


def on_device(velocity, turbine_cells, fringe_bounds):
    groups = lax.axis_size("gx")
    _, _, levels, cells_x, cells_y = velocity.shape
    paired = (
        lax.axis_size("gy") == 2
        and lax.axis_size("sec") == 2
        and cells_y == LANES
        and cells_x == ROWS
        and groups == ROWS
        and 2 * levels == groups * groups
    )
    plan = paired_plan if paired else general_plan
    return plan(velocity, turbine_cells, fringe_bounds)


def solution(mesh):
    return jax.shard_map(
        on_device,
        mesh=mesh,
        in_specs=(P("sec", None, None, "gx", "gy"), P(), P()),
        out_specs=(P("sec", None, "gx", None, "gy"), P("sec", "gx", None, "gy")),
        check_vma=False,
    )
```

```python
import functools

import jax
import jax.numpy as jnp
import numpy as np
from jax import lax
from jax.experimental import pallas as pl
from jax.experimental.pallas import tpu as pltpu
from jax.sharding import PartitionSpec as P

RADIUS = 4


TIME_STEP = 0.05
SMAG_COEFF = 0.1
THRUST_COEFF = 4.0
DRIVING_FORCE = 0.1
FRINGE_BLEND = 0.5
HIGHEST = lax.Precision.HIGHEST
STAGES = 3
REACH = 2 * STAGES + 1
LANES = 128
SMALLEST = float(np.finfo(np.float32).tiny)
ROWS = 8
VMEM_BYTES = 48 * 1024 * 1024


def extended(x, sides, width):
    for axis, dim in sides:
        count, length = (lax.axis_size(axis), x.shape[dim])
        up = [(i, (i + 1) % count) for i in range(count)]
        down = [(j, i) for i, j in up]
        last = lax.slice_in_dim(x, length - width, length, axis=dim)
        initial = lax.slice_in_dim(x, 0, width, axis=dim)
        before = lax.ppermute(last, axis, up)
        after = lax.ppermute(initial, axis, down)
        x = jnp.concatenate([before, x, after], axis=dim)
    return x


def shifted(block, axis, distance):
    devices = range(lax.axis_size(axis))
    route = [(i - distance, i) for i in devices if i - distance in devices]
    return lax.ppermute(block, axis, route)


def cas_table(row_index, column_index, length):
    product = row_index[:, None] * column_index[None, :] % length
    angle = product.astype(jnp.float32) * (2.0 * jnp.pi / length)
    return jnp.cos(angle) + jnp.sin(angle)


def shift_up(values):
    zeros = jnp.zeros_like(values[..., :1, :, :])
    return jnp.concatenate([values[..., 1:, :, :], zeros], axis=-3)


def shift_down(values):
    zeros = jnp.zeros_like(values[..., :1, :, :])
    return jnp.concatenate([zeros, values[..., :-1, :, :]], axis=-3)


def thomas(right_side, eigen_value):
    length = right_side.shape[0]
    inverses = []
    reduced = []
    for level_index in range(length):
        if level_index == 0:
            diagonal = eigen_value - 1.0
        elif level_index == length - 1:
            diagonal = eigen_value - 3.0
        else:
            diagonal = eigen_value - 2.0
        if level_index == 0:
            pivot_now = diagonal
            current = right_side[0] / pivot_now
        else:
            pivot_now = diagonal - inverses[-1]
            current = (right_side[level_index] - reduced[-1]) / pivot_now
        inverses.append(1.0 / pivot_now)
        reduced.append(current)
    solution = [reduced[-1]]
    for level_index in range(length - 2, -1, -1):
        solution.append(reduced[level_index] - inverses[level_index] * solution[-1])
    return jnp.stack(solution[::-1])


def spanwise_derivative(values, sine_y):
    return -sine_y * jnp.roll(jnp.flip(values, axis=-1), 1, axis=-1)


def widened(values):
    return extended(values, (("gx", 1), ("gy", 2)), 1)


def disk_weights(turbine_cells, along_x, along_y, along_z, total_y):
    matches = (along_x[:, None] == turbine_cells[None, :, 0]).astype(jnp.float32)
    offset_y = (along_y[None, :] - turbine_cells[:, 1:2] + total_y // 2) % total_y - total_y // 2
    offset_z = along_z[None, :] - turbine_cells[:, 2:3]
    distance = (
        offset_z[:, :, None] * offset_z[:, :, None] + offset_y[:, None, :] * offset_y[:, None, :]
    )
    inside = (distance <= RADIUS * RADIUS).astype(jnp.float32)
    return jnp.einsum("xt,tzy->zxy", matches, inside, precision=HIGHEST)


def tendency(velocity_now, farm_flag, disk_weight):
    levels, cells_x, cells_y = (velocity_now.shape[1], velocity_now.shape[2], velocity_now.shape[3])
    border = widened(velocity_now.reshape(3 * levels, cells_x, cells_y)).reshape(
        3, levels, cells_x + 2, cells_y + 2
    )
    plus_x = border[:, :, 2:, 1:-1]
    minus_x = border[:, :, :-2, 1:-1]
    plus_y = border[:, :, 1:-1, 2:]
    minus_y = border[:, :, 1:-1, :-2]
    plus_z = shift_up(velocity_now)
    minus_z = shift_down(velocity_now)
    gradients = [0.5 * (plus_x - minus_x), 0.5 * (plus_y - minus_y), 0.5 * (plus_z - minus_z)]
    strain_squares = jnp.zeros_like(velocity_now[0])
    for component in range(3):
        strain_squares = (
            strain_squares + gradients[component][component] * gradients[component][component]
        )
        for direction in range(component + 1, 3):
            shear = 0.5 * (gradients[direction][component] + gradients[component][direction])
            strain_squares = strain_squares + 2.0 * shear * shear
    viscosity = SMAG_COEFF * jnp.sqrt(2.0 * strain_squares)
    visc_border = widened(viscosity)
    visc_plus_x = visc_border[:, 2:, 1:-1]
    visc_minus_x = visc_border[:, :-2, 1:-1]
    visc_plus_y = visc_border[:, 1:-1, 2:]
    visc_minus_y = visc_border[:, 1:-1, :-2]
    visc_plus_z = shift_up(viscosity)
    visc_minus_z = shift_down(viscosity)
    advection = 0.5 * (plus_x[0] * plus_x - minus_x[0] * minus_x)
    advection = advection + 0.5 * (plus_y[1] * plus_y - minus_y[1] * minus_y)
    advection = advection + 0.5 * (plus_z[2] * plus_z - minus_z[2] * minus_z)
    diffusion = 0.5 * (viscosity + visc_plus_x) * (plus_x - velocity_now) - 0.5 * (
        viscosity + visc_minus_x
    ) * (velocity_now - minus_x)
    diffusion = (
        diffusion
        + 0.5 * (viscosity + visc_plus_y) * (plus_y - velocity_now)
        - 0.5 * (viscosity + visc_minus_y) * (velocity_now - minus_y)
    )
    diffusion = (
        diffusion
        + 0.5 * (viscosity + visc_plus_z) * (plus_z - velocity_now)
        - 0.5 * (viscosity + visc_minus_z) * (velocity_now - minus_z)
    )
    changes = diffusion - advection
    streamwise = DRIVING_FORCE - THRUST_COEFF * farm_flag * disk_weight * velocity_now[0] * jnp.abs(
        velocity_now[0]
    )
    return jnp.concatenate([changes[:1] + streamwise[None], changes[1:]], axis=0)


def general_plan(velocity, turbine_cells, fringe_bounds):
    initial = velocity[0]
    levels, cells_x, cells_y = (initial.shape[1], initial.shape[2], initial.shape[3])
    total_y = cells_y * lax.axis_size("gy")
    x_anchor = lax.axis_index("gx") * cells_x
    y_anchor = lax.axis_index("gy") * cells_y
    farm_flag = lax.axis_index("sec").astype(jnp.float32)
    along_x = x_anchor + jnp.arange(cells_x, dtype=jnp.int32)
    along_y = y_anchor + jnp.arange(cells_y, dtype=jnp.int32)
    along_z = jnp.arange(levels, dtype=jnp.int32)
    disk_weight = disk_weights(turbine_cells, along_x, along_y, along_z, total_y)
    segment_one = initial + TIME_STEP * tendency(initial, farm_flag, disk_weight)
    segment_two = 0.75 * initial + 0.25 * (
        segment_one + TIME_STEP * tendency(segment_one, farm_flag, disk_weight)
    )
    segment_three = initial / 3.0 + 2.0 / 3.0 * (
        segment_two + TIME_STEP * tendency(segment_two, farm_flag, disk_weight)
    )
    regrouped = lax.all_to_all(segment_three, "gx", split_axis=1, concat_axis=2, tiled=True)
    count_x = regrouped.shape[2]
    quarter = count_x // 4
    cut_at = count_x - quarter
    outlet_part = regrouped[:, :, cut_at:, :]
    upstream = shifted(outlet_part, "sec", 1)
    columns = cut_at + jnp.arange(quarter, dtype=jnp.int32)
    inside = ((columns >= fringe_bounds[0]) & (columns < fringe_bounds[1])).astype(jnp.float32)
    weight = FRINGE_BLEND * farm_flag * inside
    blended_part = outlet_part + weight[:, None] * (upstream - outlet_part)
    regrouped = jnp.concatenate([regrouped[:, :, :cut_at, :], blended_part], axis=2)
    index_x = jnp.arange(count_x, dtype=jnp.int32)
    table_x = cas_table(index_x, index_x, count_x)
    gradient_u = 0.5 * (jnp.roll(regrouped[0], -1, axis=1) - jnp.roll(regrouped[0], 1, axis=1))
    fields = jnp.stack([gradient_u, regrouped[1], regrouped[2]])
    spectral_x = jnp.einsum("kx,czxy->czky", table_x, fields, precision=HIGHEST)
    columns_view = lax.all_to_all(
        lax.all_to_all(spectral_x, "gx", split_axis=2, concat_axis=1, tiled=True),
        "gy",
        split_axis=2,
        concat_axis=3,
        tiled=True,
    )
    slice_width = columns_view.shape[2]
    count_y = columns_view.shape[3]
    index_y = jnp.arange(count_y, dtype=jnp.int32)
    table_y = cas_table(index_y, index_y, count_y)
    spectrum = jnp.einsum("ly,czky->czkl", table_y, columns_view, precision=HIGHEST)
    sine_y = jnp.sin(index_y.astype(jnp.float32) * (2.0 * jnp.pi / count_y))
    source = (
        spectrum[0]
        + spanwise_derivative(spectrum[1], sine_y)
        + 0.5 * (shift_up(spectrum[2]) - shift_down(spectrum[2]))
    )
    wave_x = (
        lax.axis_index("gx") * cells_x
        + lax.axis_index("gy") * slice_width
        + jnp.arange(slice_width, dtype=jnp.int32)
    )
    eigen_value = 2.0 * jnp.cos(wave_x.astype(jnp.float32) * (2.0 * jnp.pi / count_x))[:, None]
    eigen_value = (
        eigen_value
        + 2.0 * jnp.cos(index_y.astype(jnp.float32) * (2.0 * jnp.pi / count_y))[None, :]
        - 4.0
    )
    solved = thomas(source, eigen_value)
    above_level = jnp.concatenate([solved[1:], -solved[-1:]], axis=0)
    below_level = jnp.concatenate([solved[:1], solved[:-1]], axis=0)
    coefficients = jnp.stack(
        [solved, spanwise_derivative(solved, sine_y), 0.5 * (above_level - below_level)]
    )
    physical_y = jnp.einsum("yl,czkl->czky", table_y, coefficients, precision=HIGHEST) * (
        1.0 / count_y
    )
    returned = lax.all_to_all(
        lax.all_to_all(physical_y, "gx", split_axis=1, concat_axis=2, tiled=True),
        "gy",
        split_axis=3,
        concat_axis=2,
        tiled=True,
    )
    group_size = count_x // lax.axis_size("gy")
    wave_back = (
        index_x // slice_width % lax.axis_size("gx") * cells_x
        + index_x // group_size * slice_width
        + index_x % slice_width
    )
    inverse_table = cas_table(index_x, wave_back, count_x)
    physical = jnp.einsum("xp,czpy->czxy", inverse_table, returned, precision=HIGHEST) * (
        1.0 / count_x
    )
    pressure = physical[0]
    gradient_p = 0.5 * (jnp.roll(pressure, -1, axis=1) - jnp.roll(pressure, 1, axis=1))
    velocity_next = regrouped - jnp.stack([gradient_p, physical[1], physical[2]])
    return (velocity_next[None], pressure[None])


def dot(left, right):
    return jnp.dot(left, right, precision=HIGHEST, preferred_element_type=jnp.float32)


def swap_blocks(arrays, width):
    arrays = list(arrays)
    block = lax.broadcasted_iota(jnp.int32, arrays[0].shape, 1) // width
    step = 1
    while step < len(arrays):
        low = (block // step) % 2 == 0
        for index in range(len(arrays)):
            if (index // step) % 2 == 0:
                first, second = arrays[index], arrays[index + step]
                arrays[index] = jnp.where(low, first, pltpu.roll(second, step * width, 1))
                arrays[index + step] = jnp.where(
                    low, pltpu.roll(first, LANES - step * width, 1), second
                )
        step *= 2
    return arrays


def advance_kernel(
    total_x,
    meta,
    own_here,
    own_there,
    left_here,
    left_there,
    right_here,
    right_there,
    thrust,
    table_y,
    table_z,
    moved,
    spectra,
    start,
    stage_a,
    stage_b,
    viscosity,
    faces,
    source,
    columns_out,
    modes,
):
    cells_x, _, tiles, rows, half = own_here.shape
    levels = tiles * rows
    width = 2 * half
    row = lax.broadcasted_iota(jnp.int32, (rows, width), 0)
    top = row == rows - 1
    bottom = row == 0

    for first, here, there in (
        (0, left_here, left_there),
        (REACH, own_here, own_there),
        (REACH + cells_x, right_here, right_there),
    ):
        start[pl.ds(first, here.shape[0]), :, :, :, :half] = here[...]
        start[pl.ds(first, here.shape[0]), :, :, :, half:] = there[...]

    def next_y(f):
        return pltpu.roll(f, width - 1, 1)

    def last_y(f):
        return pltpu.roll(f, 1, 1)

    def next_z(parts, t):
        if t < tiles - 1:
            return parts[t + 1]
        return jnp.where(top, 0.0, pltpu.roll(parts[0], rows - 1, 0))

    def last_z(parts, t):
        if t > 0:
            return parts[t - 1]
        return jnp.where(bottom, 0.0, pltpu.roll(parts[tiles - 1], 1, 0))

    def set_viscosity(now, first, end):
        def column(i, carry):
            here = [[now[i, c, t] for t in range(tiles)] for c in range(3)]
            found = []
            for t in range(tiles):
                d_x = [now[i + 1, c, t] - now[i - 1, c, t] for c in range(3)]
                d_y = [next_y(f[t]) - last_y(f[t]) for f in here]
                d_z = [next_z(f, t) - last_z(f, t) for f in here]
                diagonal = d_x[0] * d_x[0] + d_y[1] * d_y[1] + d_z[2] * d_z[2]
                xy = d_x[1] + d_y[0]
                xz = d_x[2] + d_z[0]
                yz = d_y[2] + d_z[1]
                total = (diagonal + diagonal) + (xy * xy + xz * xz + yz * yz)
                root = total * lax.rsqrt(jnp.maximum(total, SMALLEST))
                found.append((0.5 * SMAG_COEFF) * root)
            for t in range(tiles):
                viscosity[i, t] = found[t]
            return carry

        lax.fori_loop(first, end, column, 0, unroll=4)

    def face(both, here, after, lead):
        low = both + here[lead]
        high = both - after[lead]
        return [after[c] * high - here[c] * low for c in range(3)]

    def face_x(now, i, t):
        here = [now[i, c, t] for c in range(3)]
        after = [now[i + 1, c, t] for c in range(3)]
        return face(viscosity[i, t] + viscosity[i + 1, t], here, after, 0)

    def advance(now, then, first, end, keep, gain):
        scale = 0.5 * TIME_STEP * gain
        for t in range(tiles):
            for c, f in enumerate(face_x(now, first - 1, t)):
                faces[c, t] = f

        def column(i, carry):
            eddy = [viscosity[i, t] for t in range(tiles)]
            field = [[now[i, c, t] for t in range(tiles)] for c in range(3)]

            def face_z(t):
                here = [f[t] for f in field]
                after = [next_z(f, t) for f in field]
                return face(eddy[t] + next_z(eddy, t), here, after, 2)

            last = face_z(tiles - 1)
            floor = eddy[0] - field[2][0]
            below = [
                jnp.where(bottom, field[c][0] * floor, pltpu.roll(last[c], 1, 0)) for c in range(3)
            ]
            ahead_of = [face_x(now, i, t) for t in range(tiles)]
            before_of = [[faces[c, t] for c in range(3)] for t in range(tiles)]
            found = []
            for t in range(tiles):
                here = [f[t] for f in field]
                above = last if t == tiles - 1 else face_z(t)
                ahead, before = ahead_of[t], before_of[t]
                side = face(eddy[t] + next_y(eddy[t]), here, [next_y(f) for f in here], 1)
                for c in range(3):
                    change = (
                        (ahead[c] - before[c]) + (side[c] - last_y(side[c])) + (above[c] - below[c])
                    )
                    if c == 0:
                        drag = thrust[i - 2, t] * here[0] * jnp.abs(here[0])
                        change = change + (2.0 * DRIVING_FORCE - drag)
                    if keep == 0.0:
                        found.append(here[c] + scale * change)
                    else:
                        found.append(keep * start[i, c, t] + gain * here[c] + scale * change)
                below = above
            for t in range(tiles):
                for c in range(3):
                    then[i, c, t] = found[3 * t + c]
                    faces[c, t] = ahead_of[t][c]
            return carry

        lax.fori_loop(first, end, column, 0, unroll=2)

    columns = start.shape[0]
    set_viscosity(start, 1, columns - 1)
    advance(start, stage_a, 2, columns - 2, 0.0, 1.0)
    set_viscosity(stage_a, 3, columns - 3)
    advance(stage_a, stage_b, 4, columns - 4, 0.75, 0.25)
    set_viscosity(stage_b, 5, columns - 5)
    advance(stage_b, stage_a, 6, columns - 6, 1.0 / 3.0, 2.0 / 3.0)

    section, anchor, fringe_first, fringe_end = (meta[0], meta[1], meta[2], meta[3])
    is_farm = section == 1

    def weight(offset, dest):
        place = lax.rem(anchor + offset + total_x, total_x)
        inside = jnp.logical_and(place >= fringe_first, place < fringe_end)
        blend = jnp.where(inside, FRINGE_BLEND, 0.0)
        share = jnp.where(is_farm, 1.0 - blend, blend)
        if dest == 0:
            share = jnp.where(is_farm, 0.0, 1.0)
        return 0.5 * share

    for x in range(cells_x):
        i = REACH + x
        upright = [stage_a[i, 2, t] for t in range(tiles)]
        for t in range(tiles):
            cross = stage_a[i, 1, t]
            plane = (next_y(cross) - last_y(cross)) + (next_z(upright, t) - last_z(upright, t))
            after, before = stage_a[i + 1, 0, t], stage_a[i - 1, 0, t]
            for dest in range(2):
                source[pl.ds(((dest * cells_x + x) * tiles + t) * rows, rows), :] = (
                    weight(x + 1, dest) * after
                    - weight(x - 1, dest) * before
                    + weight(x, dest) * plane
                )
            for c in range(3):
                columns_out[pl.ds(((x * 3 + c) * tiles + t) * rows, rows), :] = stage_a[
                    i, c, t, :, :half
                ]

    for c in range(3):
        for t in range(tiles):
            for s in range(rows):
                moved[s, c, t] = columns_out[
                    pl.ds((c * tiles + t) * rows + s, cells_x, stride=3 * levels), :
                ]

    along_y = dot(source[...], table_y[...])
    for n in range(2 * cells_x):
        modes[pl.ds(n * levels, levels), :] = dot(
            table_z[...], along_y[n * levels : (n + 1) * levels]
        )
    groups = moved.shape[0]
    lane_width = LANES // groups
    for dest in range(2):
        for a in range(levels // groups):
            picked = [
                modes[pl.ds(dest * cells_x * levels + a * groups + b, cells_x, stride=levels), :]
                for b in range(groups)
            ]
            for g, block in enumerate(swap_blocks(picked, lane_width)):
                spectra[dest, g, a] = block


def pencil_kernel(meta, received, inverse, table_x, spread_z, moved, upstream, packed):
    groups, parts, cells_x, lanes = received.shape[1:]
    total_x = groups * cells_x
    lane_width = lanes // groups
    pieces = []
    for a in range(parts):
        spectrum = (received[0, :, a] + received[1, :, a]).reshape(total_x, lanes)
        solved = dot(table_x[...], spectrum) * inverse[a]
        pieces.append(dot(table_x[...], solved))
    field = dot(jnp.concatenate(pieces, axis=1), spread_z[...])
    halves = [field[:, a * lanes : (a + 1) * lanes] for a in range(parts)]
    lane = lax.broadcasted_iota(jnp.int32, (total_x, lanes), 1)
    quarter = 2 * lane_width
    for g in range(groups):
        a = g * parts // groups
        if g % 2 == 0:
            edge = pltpu.roll(halves[max(a - 1, 0)], quarter, 1)
            packed[g, :total_x] = jnp.where(lane < quarter, edge, pltpu.roll(halves[a], quarter, 1))
        else:
            edge = pltpu.roll(halves[min(a + 1, parts - 1)], lanes - quarter, 1)
            packed[g, :total_x] = jnp.where(
                lane < lanes - quarter, pltpu.roll(halves[a], lanes - quarter, 1), edge
            )
    section, anchor, fringe_first, fringe_end = (meta[0], meta[1], meta[2], meta[3])
    place = anchor + lax.broadcasted_iota(jnp.int32, (cells_x, lanes), 0)
    inside = jnp.logical_and(place >= fringe_first, place < fringe_end)
    inside = jnp.logical_and(inside, section == 1)
    blend = jnp.where(inside, FRINGE_BLEND, 0.0)[None, None]
    for g in range(groups):
        own = moved[g]
        mixed = own + blend * (upstream[g] - own)
        packed[g, total_x:] = mixed.reshape(-1, lanes)


def project_kernel(meta, received, partner, table_y, velocity_next, pressure):
    groups = received.shape[0]
    total_x, lanes = partner.shape[1:]
    share = pressure.shape[0]
    cells_x = total_x // groups
    here = swap_blocks([received[s, :total_x] for s in range(groups)], lanes // groups)
    there = swap_blocks([partner[s] for s in range(groups)], lanes // groups)
    place = meta[4]
    fields = []
    for n in range(share + 2):
        both = jnp.concatenate([here[n + 1], there[n + 1]], axis=1)
        fields.append(dot(both, table_y[...]))
    values = [f[:, :lanes] for f in fields]
    values[0] = jnp.where(place == 0, values[1], values[0])
    values[-1] = jnp.where(place == groups - 1, -values[-2], values[-1])
    for z in range(share):
        now = values[z + 1]
        pressure[z] = now
        slopes = [
            0.5 * (pltpu.roll(now, total_x - 1, 0) - pltpu.roll(now, 1, 0)),
            fields[z + 1][:, lanes:],
            0.5 * (values[z + 2] - values[z]),
        ]
        for c in range(3):
            rows = total_x + (c * share + z) * cells_x
            blended = received[:, rows : rows + cells_x].reshape(total_x, lanes)
            velocity_next[c, z] = blended - slopes[c]


def cas(rows, columns, length):
    angle = (np.outer(rows, columns) % length) * (2.0 * np.pi / length)
    return np.cos(angle) + np.sin(angle)


def tables(levels, total_x, total_y, groups):
    half = total_y // 2
    lane_width = LANES // groups
    every_x = np.arange(total_x)
    every_y = np.arange(total_y)
    table_x = cas(every_x, every_x, total_x)
    table_y = cas(every_y, every_y, total_y)
    slope_y = 0.5 * (np.roll(table_y, -1, axis=1) - np.roll(table_y, 1, axis=1))
    level = np.arange(levels) + 0.5
    table_z = np.cos(np.outer(level, level) * (np.pi / levels))
    spread_z = np.kron(table_z, np.eye(lane_width))
    forward, backward = [], []
    for core in range(2):
        order = np.roll(every_y, -core * half)
        here = slice(core * half, (core + 1) * half)
        forward.append(table_y[order, here])
        backward.append(np.concatenate([table_y[order, here], slope_y[order, here]], axis=1))
    eigen = (
        (2.0 * np.cos(level * (np.pi / levels)) - 2.0)[:, None, None]
        + (2.0 * np.cos(every_x * (2.0 * np.pi / total_x)) - 2.0)[None, :, None]
        + (2.0 * np.cos(every_y * (2.0 * np.pi / total_y)) - 2.0)[None, None, :]
    )
    inverse = (2.0 / levels) / (total_x * total_y) / eigen
    inverse = inverse.reshape(levels // groups, groups, total_x, 2, groups, lane_width)
    inverse = inverse.transpose(4, 3, 0, 2, 1, 5).reshape(
        groups, 2, levels // groups, total_x, LANES
    )
    return [
        np.asarray(t, np.float32)
        for t in (table_x, np.stack(forward), np.stack(backward), table_z, spread_z, inverse)
    ]


def call(kernel, out_shapes, scratch, *operands):
    in_specs = [pl.BlockSpec(memory_space=pltpu.SMEM)]
    in_specs += [pl.BlockSpec(memory_space=pltpu.VMEM)] * (len(operands) - 1)
    return pl.pallas_call(
        kernel,
        out_shape=out_shapes,
        in_specs=in_specs,
        out_specs=jax.tree.map(lambda _: pl.BlockSpec(memory_space=pltpu.VMEM), out_shapes),
        scratch_shapes=scratch,
        compiler_params=pltpu.CompilerParams(vmem_limit_bytes=VMEM_BYTES),
    )(*operands)


def thrust_weights(turbine_cells, along_x, along_y, along_z, total_y, strength):
    matches = (along_x[:, None] == turbine_cells[None, :, 0]).astype(jnp.bfloat16)
    offset_y = (along_y[None, :] - turbine_cells[:, 1:2] + total_y // 2) % total_y - total_y // 2
    offset_z = along_z[None, :] - turbine_cells[:, 2:3]
    distance = (
        offset_z[:, :, None] * offset_z[:, :, None] + offset_y[:, None, :] * offset_y[:, None, :]
    )
    inside = (distance <= RADIUS * RADIUS).astype(jnp.bfloat16)
    count = jnp.einsum("xt,tzy->xzy", matches, inside, preferred_element_type=jnp.float32)
    return strength * count


def paired_plan(velocity, turbine_cells, fringe_bounds):
    groups = lax.axis_size("gx")
    initial = velocity[0]
    _, levels, cells_x, cells_y = initial.shape
    total_x, total_y = cells_x * groups, 2 * cells_y
    width = total_y
    share = levels // groups
    section, place, core = (lax.axis_index("sec"), lax.axis_index("gx"), lax.axis_index("gy"))
    table_x, forward, backward, table_z, spread_z, inverse = tables(
        levels, total_x, total_y, groups
    )
    meta = jnp.stack([section, place * cells_x, fringe_bounds[0], fringe_bounds[1], place])
    meta = meta.astype(jnp.int32)

    up = [(i, (i + 1) % groups) for i in range(groups)]
    down = [(j, i) for i, j in up]
    swap = [(0, 1), (1, 0)]
    own = jnp.transpose(
        initial.reshape(3, ROWS, share, cells_x, cells_y), (3, 0, 2, 1, 4)
    )
    left = lax.ppermute(own[cells_x - REACH :], "gx", up)
    right = lax.ppermute(own[:REACH], "gx", down)
    own_there = lax.ppermute(own, "gy", swap)
    left_there = lax.ppermute(left, "gy", swap)
    right_there = lax.ppermute(right, "gy", swap)

    along_x = (place * cells_x + jnp.arange(-REACH + 2, cells_x + REACH - 2)) % total_x
    along_y = (core * cells_y + jnp.arange(total_y)) % total_y
    strength = 2.0 * THRUST_COEFF * section.astype(jnp.float32)
    thrust = thrust_weights(
        turbine_cells,
        along_x,
        along_y,
        jnp.arange(levels).reshape(ROWS, share).T.reshape(levels),
        total_y,
        strength,
    ).reshape(along_x.shape[0], share, ROWS, total_y)
    table_forward = lax.dynamic_index_in_dim(jnp.asarray(forward), core, 0, keepdims=False)
    table_backward = lax.dynamic_index_in_dim(jnp.asarray(backward), core, 0, keepdims=False)
    own_inverse = lax.dynamic_slice(
        jnp.asarray(inverse), (place, core, 0, 0, 0), (1, 1) + inverse.shape[2:]
    )[0, 0]

    columns = cells_x + 2 * REACH
    parts = levels // groups
    f32 = jnp.float32
    moved, spectra = call(
        functools.partial(advance_kernel, total_x),
        (
            jax.ShapeDtypeStruct((groups, 3, share, cells_x, cells_y), f32),
            jax.ShapeDtypeStruct((2, groups, parts, cells_x, LANES), f32),
        ),
        [
            pltpu.VMEM((columns, 3, share, ROWS, width), f32),
            pltpu.VMEM((columns, 3, share, ROWS, width), f32),
            pltpu.VMEM((columns, 3, share, ROWS, width), f32),
            pltpu.VMEM((columns, share, ROWS, width), f32),
            pltpu.VMEM((3, share, ROWS, width), f32),
            pltpu.VMEM((2 * cells_x * levels, width), f32),
            pltpu.VMEM((cells_x * 3 * levels, cells_y), f32),
            pltpu.VMEM((2 * cells_x * levels, LANES), f32),
        ],
        meta,
        own,
        own_there,
        left,
        left_there,
        right,
        right_there,
        thrust,
        table_forward,
        jnp.asarray(table_z.reshape(levels, ROWS, share).transpose(0, 2, 1).reshape(levels, levels)),
    )
    fringe = [(g, groups + g) for g in range(groups - groups // 4, groups)]
    upstream = lax.ppermute(moved, ("sec", "gx"), fringe)
    received = lax.all_to_all(
        spectra.reshape(2 * groups, parts, cells_x, LANES), ("sec", "gx"), 0, 0, tiled=True
    ).reshape(2, groups, parts, cells_x, LANES)
    rows = total_x + 3 * share * cells_x
    packed = call(
        pencil_kernel,
        jax.ShapeDtypeStruct((groups, rows, LANES), f32),
        [],
        meta,
        received,
        own_inverse,
        jnp.asarray(table_x),
        jnp.asarray(spread_z),
        moved,
        upstream,
    )
    returned = lax.all_to_all(packed, "gx", 0, 0, tiled=True)
    partner = lax.ppermute(returned[:, :total_x], "gy", swap)
    velocity_next, pressure = call(
        project_kernel,
        (
            jax.ShapeDtypeStruct((3, share, total_x, cells_y), f32),
            jax.ShapeDtypeStruct((share, total_x, cells_y), f32),
        ),
        [],
        meta,
        returned,
        partner,
        table_backward,
    )
    return (velocity_next[None], pressure[None])


def on_device(velocity, turbine_cells, fringe_bounds):
    groups = lax.axis_size("gx")
    _, _, levels, cells_x, cells_y = velocity.shape
    paired = (
        lax.axis_size("gy") == 2
        and lax.axis_size("sec") == 2
        and cells_y == LANES
        and cells_x == ROWS
        and groups == ROWS
        and 2 * levels == groups * groups
    )
    plan = paired_plan if paired else general_plan
    return plan(velocity, turbine_cells, fringe_bounds)


def solution(mesh):
    return jax.shard_map(
        on_device,
        mesh=mesh,
        in_specs=(P("sec", None, None, "gx", "gy"), P(), P()),
        out_specs=(P("sec", None, "gx", None, "gy"), P("sec", "gx", None, "gy")),
        check_vma=False,
    )
```

```python
import functools

import jax
import jax.numpy as jnp
import numpy as np
from jax import lax
from jax.experimental import pallas as pl
from jax.experimental.pallas import tpu as pltpu
from jax.sharding import PartitionSpec as P

RADIUS = 4


TIME_STEP = 0.05
SMAG_COEFF = 0.1
THRUST_COEFF = 4.0
DRIVING_FORCE = 0.1
FRINGE_BLEND = 0.5
HIGHEST = lax.Precision.HIGHEST
STAGES = 3
REACH = 2 * STAGES + 1
LANES = 128
SMALLEST = float(np.finfo(np.float32).tiny)
ROWS = 8
VMEM_BYTES = 20 * 1024 * 1024


def extended(x, sides, width):
    for axis, dim in sides:
        count, length = (lax.axis_size(axis), x.shape[dim])
        up = [(i, (i + 1) % count) for i in range(count)]
        down = [(j, i) for i, j in up]
        last = lax.slice_in_dim(x, length - width, length, axis=dim)
        initial = lax.slice_in_dim(x, 0, width, axis=dim)
        before = lax.ppermute(last, axis, up)
        after = lax.ppermute(initial, axis, down)
        x = jnp.concatenate([before, x, after], axis=dim)
    return x


def shifted(block, axis, distance):
    devices = range(lax.axis_size(axis))
    route = [(i - distance, i) for i in devices if i - distance in devices]
    return lax.ppermute(block, axis, route)


def cas_table(row_index, column_index, length):
    product = row_index[:, None] * column_index[None, :] % length
    angle = product.astype(jnp.float32) * (2.0 * jnp.pi / length)
    return jnp.cos(angle) + jnp.sin(angle)


def shift_up(values):
    zeros = jnp.zeros_like(values[..., :1, :, :])
    return jnp.concatenate([values[..., 1:, :, :], zeros], axis=-3)


def shift_down(values):
    zeros = jnp.zeros_like(values[..., :1, :, :])
    return jnp.concatenate([zeros, values[..., :-1, :, :]], axis=-3)


def thomas(right_side, eigen_value):
    length = right_side.shape[0]
    inverses = []
    reduced = []
    for level_index in range(length):
        if level_index == 0:
            diagonal = eigen_value - 1.0
        elif level_index == length - 1:
            diagonal = eigen_value - 3.0
        else:
            diagonal = eigen_value - 2.0
        if level_index == 0:
            pivot_now = diagonal
            current = right_side[0] / pivot_now
        else:
            pivot_now = diagonal - inverses[-1]
            current = (right_side[level_index] - reduced[-1]) / pivot_now
        inverses.append(1.0 / pivot_now)
        reduced.append(current)
    solution = [reduced[-1]]
    for level_index in range(length - 2, -1, -1):
        solution.append(reduced[level_index] - inverses[level_index] * solution[-1])
    return jnp.stack(solution[::-1])


def spanwise_derivative(values, sine_y):
    return -sine_y * jnp.roll(jnp.flip(values, axis=-1), 1, axis=-1)


def widened(values):
    return extended(values, (("gx", 1), ("gy", 2)), 1)


def disk_weights(turbine_cells, along_x, along_y, along_z, total_y):
    matches = (along_x[:, None] == turbine_cells[None, :, 0]).astype(jnp.float32)
    offset_y = (along_y[None, :] - turbine_cells[:, 1:2] + total_y // 2) % total_y - total_y // 2
    offset_z = along_z[None, :] - turbine_cells[:, 2:3]
    distance = (
        offset_z[:, :, None] * offset_z[:, :, None] + offset_y[:, None, :] * offset_y[:, None, :]
    )
    inside = (distance <= RADIUS * RADIUS).astype(jnp.float32)
    return jnp.einsum("xt,tzy->zxy", matches, inside, precision=HIGHEST)


def tendency(velocity_now, farm_flag, disk_weight):
    levels, cells_x, cells_y = (velocity_now.shape[1], velocity_now.shape[2], velocity_now.shape[3])
    border = widened(velocity_now.reshape(3 * levels, cells_x, cells_y)).reshape(
        3, levels, cells_x + 2, cells_y + 2
    )
    plus_x = border[:, :, 2:, 1:-1]
    minus_x = border[:, :, :-2, 1:-1]
    plus_y = border[:, :, 1:-1, 2:]
    minus_y = border[:, :, 1:-1, :-2]
    plus_z = shift_up(velocity_now)
    minus_z = shift_down(velocity_now)
    gradients = [0.5 * (plus_x - minus_x), 0.5 * (plus_y - minus_y), 0.5 * (plus_z - minus_z)]
    strain_squares = jnp.zeros_like(velocity_now[0])
    for component in range(3):
        strain_squares = (
            strain_squares + gradients[component][component] * gradients[component][component]
        )
        for direction in range(component + 1, 3):
            shear = 0.5 * (gradients[direction][component] + gradients[component][direction])
            strain_squares = strain_squares + 2.0 * shear * shear
    viscosity = SMAG_COEFF * jnp.sqrt(2.0 * strain_squares)
    visc_border = widened(viscosity)
    visc_plus_x = visc_border[:, 2:, 1:-1]
    visc_minus_x = visc_border[:, :-2, 1:-1]
    visc_plus_y = visc_border[:, 1:-1, 2:]
    visc_minus_y = visc_border[:, 1:-1, :-2]
    visc_plus_z = shift_up(viscosity)
    visc_minus_z = shift_down(viscosity)
    advection = 0.5 * (plus_x[0] * plus_x - minus_x[0] * minus_x)
    advection = advection + 0.5 * (plus_y[1] * plus_y - minus_y[1] * minus_y)
    advection = advection + 0.5 * (plus_z[2] * plus_z - minus_z[2] * minus_z)
    diffusion = 0.5 * (viscosity + visc_plus_x) * (plus_x - velocity_now) - 0.5 * (
        viscosity + visc_minus_x
    ) * (velocity_now - minus_x)
    diffusion = (
        diffusion
        + 0.5 * (viscosity + visc_plus_y) * (plus_y - velocity_now)
        - 0.5 * (viscosity + visc_minus_y) * (velocity_now - minus_y)
    )
    diffusion = (
        diffusion
        + 0.5 * (viscosity + visc_plus_z) * (plus_z - velocity_now)
        - 0.5 * (viscosity + visc_minus_z) * (velocity_now - minus_z)
    )
    changes = diffusion - advection
    streamwise = DRIVING_FORCE - THRUST_COEFF * farm_flag * disk_weight * velocity_now[0] * jnp.abs(
        velocity_now[0]
    )
    return jnp.concatenate([changes[:1] + streamwise[None], changes[1:]], axis=0)


def general_plan(velocity, turbine_cells, fringe_bounds):
    initial = velocity[0]
    levels, cells_x, cells_y = (initial.shape[1], initial.shape[2], initial.shape[3])
    total_y = cells_y * lax.axis_size("gy")
    x_anchor = lax.axis_index("gx") * cells_x
    y_anchor = lax.axis_index("gy") * cells_y
    farm_flag = lax.axis_index("sec").astype(jnp.float32)
    along_x = x_anchor + jnp.arange(cells_x, dtype=jnp.int32)
    along_y = y_anchor + jnp.arange(cells_y, dtype=jnp.int32)
    along_z = jnp.arange(levels, dtype=jnp.int32)
    disk_weight = disk_weights(turbine_cells, along_x, along_y, along_z, total_y)
    segment_one = initial + TIME_STEP * tendency(initial, farm_flag, disk_weight)
    segment_two = 0.75 * initial + 0.25 * (
        segment_one + TIME_STEP * tendency(segment_one, farm_flag, disk_weight)
    )
    segment_three = initial / 3.0 + 2.0 / 3.0 * (
        segment_two + TIME_STEP * tendency(segment_two, farm_flag, disk_weight)
    )
    regrouped = lax.all_to_all(segment_three, "gx", split_axis=1, concat_axis=2, tiled=True)
    count_x = regrouped.shape[2]
    quarter = count_x // 4
    cut_at = count_x - quarter
    outlet_part = regrouped[:, :, cut_at:, :]
    upstream = shifted(outlet_part, "sec", 1)
    columns = cut_at + jnp.arange(quarter, dtype=jnp.int32)
    inside = ((columns >= fringe_bounds[0]) & (columns < fringe_bounds[1])).astype(jnp.float32)
    weight = FRINGE_BLEND * farm_flag * inside
    blended_part = outlet_part + weight[:, None] * (upstream - outlet_part)
    regrouped = jnp.concatenate([regrouped[:, :, :cut_at, :], blended_part], axis=2)
    index_x = jnp.arange(count_x, dtype=jnp.int32)
    table_x = cas_table(index_x, index_x, count_x)
    gradient_u = 0.5 * (jnp.roll(regrouped[0], -1, axis=1) - jnp.roll(regrouped[0], 1, axis=1))
    fields = jnp.stack([gradient_u, regrouped[1], regrouped[2]])
    spectral_x = jnp.einsum("kx,czxy->czky", table_x, fields, precision=HIGHEST)
    columns_view = lax.all_to_all(
        lax.all_to_all(spectral_x, "gx", split_axis=2, concat_axis=1, tiled=True),
        "gy",
        split_axis=2,
        concat_axis=3,
        tiled=True,
    )
    slice_width = columns_view.shape[2]
    count_y = columns_view.shape[3]
    index_y = jnp.arange(count_y, dtype=jnp.int32)
    table_y = cas_table(index_y, index_y, count_y)
    spectrum = jnp.einsum("ly,czky->czkl", table_y, columns_view, precision=HIGHEST)
    sine_y = jnp.sin(index_y.astype(jnp.float32) * (2.0 * jnp.pi / count_y))
    source = (
        spectrum[0]
        + spanwise_derivative(spectrum[1], sine_y)
        + 0.5 * (shift_up(spectrum[2]) - shift_down(spectrum[2]))
    )
    wave_x = (
        lax.axis_index("gx") * cells_x
        + lax.axis_index("gy") * slice_width
        + jnp.arange(slice_width, dtype=jnp.int32)
    )
    eigen_value = 2.0 * jnp.cos(wave_x.astype(jnp.float32) * (2.0 * jnp.pi / count_x))[:, None]
    eigen_value = (
        eigen_value
        + 2.0 * jnp.cos(index_y.astype(jnp.float32) * (2.0 * jnp.pi / count_y))[None, :]
        - 4.0
    )
    solved = thomas(source, eigen_value)
    above_level = jnp.concatenate([solved[1:], -solved[-1:]], axis=0)
    below_level = jnp.concatenate([solved[:1], solved[:-1]], axis=0)
    coefficients = jnp.stack(
        [solved, spanwise_derivative(solved, sine_y), 0.5 * (above_level - below_level)]
    )
    physical_y = jnp.einsum("yl,czkl->czky", table_y, coefficients, precision=HIGHEST) * (
        1.0 / count_y
    )
    returned = lax.all_to_all(
        lax.all_to_all(physical_y, "gx", split_axis=1, concat_axis=2, tiled=True),
        "gy",
        split_axis=3,
        concat_axis=2,
        tiled=True,
    )
    group_size = count_x // lax.axis_size("gy")
    wave_back = (
        index_x // slice_width % lax.axis_size("gx") * cells_x
        + index_x // group_size * slice_width
        + index_x % slice_width
    )
    inverse_table = cas_table(index_x, wave_back, count_x)
    physical = jnp.einsum("xp,czpy->czxy", inverse_table, returned, precision=HIGHEST) * (
        1.0 / count_x
    )
    pressure = physical[0]
    gradient_p = 0.5 * (jnp.roll(pressure, -1, axis=1) - jnp.roll(pressure, 1, axis=1))
    velocity_next = regrouped - jnp.stack([gradient_p, physical[1], physical[2]])
    return (velocity_next[None], pressure[None])


def split(values):
    high = values.astype(jnp.bfloat16)
    low = values - high.astype(jnp.float32)
    return high, low.astype(jnp.bfloat16)


def dot(left, right):
    (a, da), (b, db) = split(left), split(right)

    def product(x, y):
        return jnp.dot(x, y, preferred_element_type=jnp.float32)

    return product(a, b) + (product(a, db) + product(da, b))


def swap_blocks(arrays, width):
    arrays = list(arrays)
    block = lax.broadcasted_iota(jnp.int32, arrays[0].shape, 1) // width
    step = 1
    while step < len(arrays):
        low = (block // step) % 2 == 0
        for index in range(len(arrays)):
            if (index // step) % 2 == 0:
                first, second = arrays[index], arrays[index + step]
                arrays[index] = jnp.where(low, first, pltpu.roll(second, step * width, 1))
                arrays[index + step] = jnp.where(
                    low, pltpu.roll(first, LANES - step * width, 1), second
                )
        step *= 2
    return arrays


class Stencil:
    def __init__(self, tiles, rows, width, viscosity, faces, thrust, start):
        self.tiles, self.rows, self.width = (tiles, rows, width)
        self.viscosity, self.faces, self.thrust, self.start = (viscosity, faces, thrust, start)
        row = lax.broadcasted_iota(jnp.int32, (rows, width), 0)
        self.top = row == rows - 1
        self.bottom = row == 0

    def next_y(self, f):
        return pltpu.roll(f, self.width - 1, 1)

    def last_y(self, f):
        return pltpu.roll(f, 1, 1)

    def next_z(self, parts, t):
        if t < self.tiles - 1:
            return parts[t + 1]
        return jnp.where(self.top, 0.0, pltpu.roll(parts[0], self.rows - 1, 0))

    def last_z(self, parts, t):
        if t > 0:
            return parts[t - 1]
        return jnp.where(self.bottom, 0.0, pltpu.roll(parts[self.tiles - 1], 1, 0))

    def set_viscosity(self, now, first, count):
        tiles = self.tiles

        def column(n, carry):
            i = first + n
            here = [[now[i, c, t] for t in range(tiles)] for c in range(3)]
            found = []
            for t in range(tiles):
                d_x = [now[i + 1, c, t] - now[i - 1, c, t] for c in range(3)]
                d_y = [self.next_y(f[t]) - self.last_y(f[t]) for f in here]
                d_z = [self.next_z(f, t) - self.last_z(f, t) for f in here]
                diagonal = d_x[0] * d_x[0] + d_y[1] * d_y[1] + d_z[2] * d_z[2]
                xy = d_x[1] + d_y[0]
                xz = d_x[2] + d_z[0]
                yz = d_y[2] + d_z[1]
                total = (diagonal + diagonal) + (xy * xy + xz * xz + yz * yz)
                root = total * lax.rsqrt(jnp.maximum(total, SMALLEST))
                found.append((0.5 * SMAG_COEFF) * root)
            for t in range(tiles):
                self.viscosity[i, t] = found[t]
            return carry

        lax.fori_loop(0, count, column, 0, unroll=4 if count % 4 == 0 else 6)

    def face(self, both, here, after, lead):
        low = both + here[lead]
        high = both - after[lead]
        return [after[c] * high - here[c] * low for c in range(3)]

    def face_x(self, now, i, t):
        here = [now[i, c, t] for c in range(3)]
        after = [now[i + 1, c, t] for c in range(3)]
        return self.face(self.viscosity[i, t] + self.viscosity[i + 1, t], here, after, 0)

    def advance(self, now, then, first, count, keep, gain):
        tiles, scale = self.tiles, 0.5 * TIME_STEP * gain
        for t in range(tiles):
            for c, f in enumerate(self.face_x(now, first - 1, t)):
                self.faces[c, t] = f

        def column(n, carry):
            i = first + n
            eddy = [self.viscosity[i, t] for t in range(tiles)]
            field = [[now[i, c, t] for t in range(tiles)] for c in range(3)]

            def face_z(t):
                here = [f[t] for f in field]
                after = [self.next_z(f, t) for f in field]
                return self.face(eddy[t] + self.next_z(eddy, t), here, after, 2)

            last = face_z(tiles - 1)
            floor = eddy[0] - field[2][0]
            below = [
                jnp.where(self.bottom, field[c][0] * floor, pltpu.roll(last[c], 1, 0))
                for c in range(3)
            ]
            ahead_of = [self.face_x(now, i, t) for t in range(tiles)]
            before_of = [[self.faces[c, t] for c in range(3)] for t in range(tiles)]
            found = []
            for t in range(tiles):
                here = [f[t] for f in field]
                above = last if t == tiles - 1 else face_z(t)
                ahead, before = ahead_of[t], before_of[t]
                beside = [self.next_y(f) for f in here]
                side = self.face(eddy[t] + self.next_y(eddy[t]), here, beside, 1)
                for c in range(3):
                    change = (
                        (ahead[c] - before[c])
                        + (side[c] - self.last_y(side[c]))
                        + (above[c] - below[c])
                    )
                    if c == 0:
                        drag = self.thrust[i - 2, t] * here[0] * jnp.abs(here[0])
                        change = change + (2.0 * DRIVING_FORCE - drag)
                    if keep == 0.0:
                        found.append(here[c] + scale * change)
                    else:
                        found.append(keep * self.start[i, c, t] + gain * here[c] + scale * change)
                below = above
            for t in range(tiles):
                for c in range(3):
                    then[i, c, t] = found[3 * t + c]
                    self.faces[c, t] = ahead_of[t][c]
            return carry

        lax.fori_loop(0, count, column, 0, unroll=2)

    def stage(self, number, now, then, first, count):
        keep, gain = ((0.0, 1.0), (0.75, 0.25), (1.0 / 3.0, 2.0 / 3.0))[number]
        self.set_viscosity(now, first - 1, count + 2)
        self.advance(now, then, first, count, keep, gain)


def place_columns(start, core, runs):
    half = start.shape[-1] // 2

    def copy(low_is_here):
        for first, here, there, begin, count in runs:
            low, high = (here, there) if low_is_here else (there, here)
            start[pl.ds(first, count), :, :, :, :half] = low[pl.ds(begin, count)]
            start[pl.ds(first, count), :, :, :, half:] = high[pl.ds(begin, count)]

    pl.when(core == 0)(lambda: copy(True))
    pl.when(core == 1)(lambda: copy(False))


def near_kernel(
    own_here,
    own_there,
    left_here,
    left_there,
    right_here,
    right_there,
    thrust,
    first,
    second,
    third,
    start,
    stage_a,
    stage_b,
    viscosity,
    faces,
):
    cells_x = own_here.shape[0]
    near = left_here.shape[0]
    _, _, tiles, rows, width = start.shape
    core = lax.axis_index("gy")
    place_columns(
        start,
        core,
        (
            (0, left_here, left_there, 0, near),
            (near, own_here, own_there, 0, cells_x),
            (near + cells_x, right_here, right_there, 0, near),
        ),
    )
    stencil = Stencil(tiles, rows, width, viscosity, faces, thrust, start)
    columns = start.shape[0]
    stencil.stage(0, start, stage_a, 2, columns - 4)
    stencil.stage(1, stage_a, stage_b, 4, columns - 8)
    first[...] = stage_a[pl.ds(2 + core * (columns - 8), 4)]
    second[...] = stage_b[pl.ds(4 + core * (columns - 12), 4)]
    stencil.stage(2, stage_b, stage_a, 6, columns - 12)
    third[...] = stage_a[pl.ds(6, columns - 12)]


def far_kernel(
    total_x,
    fringe,
    own_here,
    own_there,
    left_here,
    left_there,
    right_here,
    right_there,
    far_here,
    far_there,
    first,
    second,
    third,
    thrust,
    pieces,
    source,
    start,
    stage_a,
    stage_b,
    stage_c,
    viscosity,
    faces,
    columns_here,
    columns_there,
):
    cells_x = own_here.shape[0]
    near, far = left_here.shape[0], far_here.shape[0]
    _, _, tiles, rows, width = start.shape
    half = width // 2
    share_x = cells_x // 2
    inner = share_x + 1
    core = lax.axis_index("gy")

    @pl.when(core == 0)
    def _():
        place_columns(
            start,
            core,
            (
                (0, far_here, far_there, 0, far),
                (far, left_here, left_there, 0, near),
                (far + near, own_here, own_there, 0, inner),
            ),
        )

    @pl.when(core == 1)
    def _():
        place_columns(
            start,
            core,
            (
                (0, own_here, own_there, cells_x - inner, inner),
                (inner, right_here, right_there, 0, near),
                (inner + near, far_here, far_there, 0, far),
            ),
        )

    stencil = Stencil(tiles, rows, width, viscosity, faces, thrust, start)
    stencil.stage(0, start, stage_a, 2 + 4 * core, 4)
    stage_a[pl.ds(6 - 4 * core, 4)] = first[...]
    stencil.stage(1, stage_a, stage_b, 4, 4)
    stage_b[pl.ds(8 - 8 * core, 4)] = second[...]
    stencil.stage(2, stage_b, stage_c, 6 - 4 * core, 4)
    stage_c[pl.ds(10 - 10 * core, 2)] = third[...]

    origin = REACH - core * (REACH - 1)
    pairs = 3 * tiles // 2
    for x in range(share_x):
        for c in range(3):
            for t in range(tiles):
                n = c * tiles + t
                field = stage_c[origin + x, c, t]
                low, high = field[:, :half], field[:, half:]
                spot = pl.ds((((n % 2) * share_x + x) * pairs + n // 2) * rows, rows)
                columns_here[spot, :] = jnp.where(core == 0, low, high)
                columns_there[spot, :] = jnp.where(core == 0, high, low)
    for s in range(rows):
        for m in range(pairs):
            spot = pl.ds(m * rows + s, 2 * share_x, stride=pairs * rows)
            pieces[0, s, m] = columns_here[spot, :]
            pieces[1, s, m] = columns_there[spot, :]

    is_farm = lax.axis_index("sec") == 1
    corner = lax.axis_index("gx") * cells_x + core * share_x

    def weight(offset, dest):
        place = lax.rem(corner + offset + total_x, total_x)
        inside = jnp.logical_and(place >= fringe[0], place < fringe[1])
        blend = jnp.where(inside, FRINGE_BLEND, 0.0)
        share = jnp.where(is_farm, 1.0 - blend, blend)
        if dest == 0:
            share = jnp.where(is_farm, 0.0, 1.0)
        return 0.5 * share

    for x in range(share_x):
        i = origin + x
        upright = [stage_c[i, 2, t] for t in range(tiles)]
        for t in range(tiles):
            cross = stage_c[i, 1, t]
            plane = (stencil.next_y(cross) - stencil.last_y(cross)) + (
                stencil.next_z(upright, t) - stencil.last_z(upright, t)
            )
            after, before = stage_c[i + 1, 0, t], stage_c[i - 1, 0, t]
            for dest in range(2):
                source[pl.ds(((dest * share_x + x) * tiles + t) * rows, rows), :] = (
                    weight(x + 1, dest) * after
                    - weight(x - 1, dest) * before
                    + weight(x, dest) * plane
                )


def spectra_kernel(source, table_y, table_z, spectra, modes):
    _, groups, _, parts, rows, lanes = spectra.shape
    levels = table_z.shape[0]
    count, total_y = source.shape
    columns = count // levels
    along_y = dot(source[...], table_y[...])
    beside = [along_y[n * levels : (n + 1) * levels] for n in range(columns)]
    both = dot(table_z[...], jnp.concatenate(beside, axis=1))
    for n in range(columns):
        for h in range(2):
            first = n * total_y + h * lanes
            modes[h, pl.ds(n * levels, levels), :] = both[:, first : first + lanes]
    for dest in range(2):
        for h in range(2):
            for p in range(parts):
                first = dest * count // 2 + p * groups
                picked = [
                    modes[h, pl.ds(first + b, rows, stride=levels // 2), :] for b in range(groups)
                ]
                for g, block in enumerate(swap_blocks(picked, lanes // groups)):
                    spectra[dest, g, h, p] = block


def blend_kernel(fringe, pieces, upstream, blended_here, blended_there):
    _, groups, pairs, rows, lanes = pieces.shape
    half = rows // 2
    corner = lax.axis_index("gx") * rows + lax.axis_index("gy") * half
    place = corner + lax.broadcasted_iota(jnp.int32, (rows, lanes), 0) % half
    inside = jnp.logical_and(place >= fringe[0], place < fringe[1])
    inside = jnp.logical_and(inside, lax.axis_index("sec") == 1)
    weight = jnp.where(inside, FRINGE_BLEND, 0.0)[None, None]
    for n, blended in enumerate((blended_here, blended_there)):
        own = pieces[n]
        blended[...] = own + weight * (upstream[n] - own)


def pencil_kernel(received, inverse, table, blended_here, blended_there, packed):
    _, groups, cores, parts, rows, lanes = received.shape
    _, pairs, _, _ = blended_here.shape
    total_x = groups * rows
    lane_width = lanes // groups
    wave, base = 2 * total_x, table.shape[1]
    spread_z = table[:base]
    pair_x = table[base : base + wave, :wave]
    table_x = table[base : base + total_x, wave : wave + total_x]
    spectrum = jnp.concatenate(
        [(received[0, :, :, p] + received[1, :, :, p]).reshape(-1, lanes) for p in range(parts)],
        axis=1,
    )
    solved = dot(pair_x, spectrum)
    pieces = []
    for a in range(2 * parts):
        p, side = a % parts, a // parts
        block = solved[side * total_x : (side + 1) * total_x, p * lanes : (p + 1) * lanes]
        pieces.append(block * inverse[a])
    field = dot(dot(table_x, jnp.concatenate(pieces, axis=1)), spread_z)
    levels_of = [field[:, a * lanes : (a + 1) * lanes] for a in range(2 * parts)]
    wide = lax.broadcasted_iota(jnp.int32, (total_x // 2, lanes), 1)
    left = wide < lanes // 2
    quarter = total_x // 4
    block = lax.broadcasted_iota(jnp.int32, (quarter, lanes), 1) // lane_width
    low = lax.broadcasted_iota(jnp.int32, (rows, lanes), 0) < rows // 2
    is_first = lax.axis_index("gy") == 0
    for g in range(groups):
        a, odd = divmod(g, 2)
        now = levels_of[a]
        front, rear = now[: total_x // 2], now[total_x // 2 :]
        if odd:
            main = jnp.where(left, pltpu.roll(front, lanes // 2, 1), rear)
            lower, lower_lane = now, lanes // 2 - lane_width
            upper, upper_lane = levels_of[min(a + 1, 2 * parts - 1)], 0
        else:
            main = jnp.where(left, front, pltpu.roll(rear, lanes // 2, 1))
            lower, lower_lane = levels_of[max(a - 1, 0)], lanes - lane_width
            upper, upper_lane = now, lanes // 2
        edge = None
        for q in range(4):
            for n, (whole, lane) in enumerate(((lower, lower_lane), (upper, upper_lane))):
                spot = 2 * q + n
                move = (spot * lane_width - lane) % lanes
                rolled = whole[q * quarter : (q + 1) * quarter]
                if move:
                    rolled = pltpu.roll(rolled, move, 1)
                edge = rolled if edge is None else jnp.where(block == spot, rolled, edge)
        packed[g, : total_x // 2] = main
        packed[g, total_x // 2 : 3 * quarter] = edge
        for m in range(pairs):
            here, there = blended_here[g, m], blended_there[g, m]
            before = jnp.where(is_first, here, there)
            after = jnp.where(is_first, there, here)
            first = 3 * quarter + 2 * m * rows
            packed[g, first : first + rows] = jnp.where(
                low, before, pltpu.roll(after, rows // 2, 0)
            )
            packed[g, first + rows : first + 2 * rows] = jnp.where(
                low, pltpu.roll(before, rows // 2, 0), after
            )


def project_kernel(received, partner, table_y, velocity_next, pressure):
    groups = received.shape[0]
    share, total_x, lanes = pressure.shape
    cells_x = total_x // groups
    width = lanes // groups
    place, core = lax.axis_index("gx"), lax.axis_index("gy")
    main_rows = total_x // 2
    rows = partner.shape[1]

    def levels_in(arrays):
        main = swap_blocks([arrays[s, :main_rows] for s in range(groups)], width)
        edge = swap_blocks([arrays[s, main_rows:rows] for s in range(groups)], width)
        inner = [jnp.concatenate([main[n], main[share + n]], axis=0) for n in range(share)]
        outer = [jnp.concatenate([edge[2 * q + n] for q in range(4)], axis=0) for n in range(2)]
        return [outer[0]] + inner + [outer[1]]

    here, there = levels_in(received), levels_in(partner)
    here, there = jnp.concatenate(here, axis=0), jnp.concatenate(there, axis=0)
    low = jnp.where(core == 0, here, there)
    high = jnp.where(core == 0, there, here)
    both = dot(jnp.concatenate([low, high], axis=1), table_y[core])
    fields = [both[n * total_x : (n + 1) * total_x] for n in range(share + 2)]
    values = [f[:, :lanes] for f in fields]
    values[0] = jnp.where(place == 0, values[1], values[0])
    values[-1] = jnp.where(place == groups - 1, -values[-2], values[-1])
    for z in range(share):
        now = values[z + 1]
        pressure[z] = now
        slopes = [
            0.5 * (pltpu.roll(now, total_x - 1, 0) - pltpu.roll(now, 1, 0)),
            fields[z + 1][:, lanes:],
            0.5 * (values[z + 2] - values[z]),
        ]
        for c in range(3):
            first = rows + (c * share + z) * cells_x
            blended = received[:, first : first + cells_x].reshape(total_x, lanes)
            velocity_next[c, z] = blended - slopes[c]


def cas(rows, columns, length):
    angle = (np.outer(rows, columns) % length) * (2.0 * np.pi / length)
    return np.cos(angle) + np.sin(angle)


def tables(levels, total_x, total_y, groups):
    half = total_y // 2
    lane_width = LANES // groups
    every_x = np.arange(total_x)
    every_y = np.arange(total_y)
    table_x = cas(every_x, every_x, total_x)
    table_y = cas(every_y, every_y, total_y)
    slope_y = 0.5 * (np.roll(table_y, -1, axis=1) - np.roll(table_y, 1, axis=1))
    level = np.arange(levels) + 0.5
    table_z = np.cos(np.outer(level, level) * (np.pi / levels))
    spread_z = np.kron(table_z, np.eye(lane_width))
    order = np.arange(levels).reshape(ROWS, levels // ROWS).T.reshape(levels)
    backward = [
        np.concatenate([table_y[:, here], slope_y[:, here]], axis=1)
        for here in (slice(0, half), slice(half, total_y))
    ]
    pair_x = np.einsum("kx,ab->akxb", table_x, np.eye(2)).reshape(2 * total_x, 2 * total_x)
    eigen = (
        (2.0 * np.cos(level * (np.pi / levels)) - 2.0)[:, None, None]
        + (2.0 * np.cos(every_x * (2.0 * np.pi / total_x)) - 2.0)[None, :, None]
        + (2.0 * np.cos(every_y * (2.0 * np.pi / total_y)) - 2.0)[None, None, :]
    )
    inverse = (2.0 / levels) / (total_x * total_y) / eigen
    inverse = inverse.reshape(levels // groups, groups, total_x, 2, groups, lane_width)
    inverse = inverse.transpose(4, 3, 0, 2, 1, 5).reshape(
        groups, 2, levels // groups, total_x, LANES
    )
    pencil = np.zeros((spread_z.shape[0] + 2 * total_x, spread_z.shape[1]))
    pencil[: spread_z.shape[0]] = spread_z
    pencil[spread_z.shape[0] :, : 2 * total_x] = pair_x
    pencil[spread_z.shape[0] : -total_x, 2 * total_x : 3 * total_x] = table_x
    return [
        jnp.asarray(t, jnp.float32)
        for t in (
            pencil,
            table_y,
            np.stack(backward),
            table_z[:, order],
            inverse,
        )
    ]


def call(kernel, out_shapes, scratch, *operands):
    in_specs = [
        pl.BlockSpec(memory_space=pltpu.SMEM if o.dtype == jnp.int32 else pltpu.VMEM)
        for o in operands
    ]
    return pl.pallas_call(
        kernel,
        out_shape=out_shapes,
        in_specs=in_specs,
        out_specs=jax.tree.map(lambda _: pl.BlockSpec(memory_space=pltpu.VMEM), out_shapes),
        scratch_shapes=scratch,
        compiler_params=pltpu.CompilerParams(vmem_limit_bytes=VMEM_BYTES),
    )(*operands)


def thrust_weights(turbine_cells, along_x, along_y, along_z, total_y, strength):
    matches = (along_x[:, None] == turbine_cells[None, :, 0]).astype(jnp.bfloat16)
    offset_y = (along_y[None, :] - turbine_cells[:, 1:2] + total_y // 2) % total_y - total_y // 2
    offset_z = along_z[None, :] - turbine_cells[:, 2:3]
    distance = (
        offset_z[:, :, None] * offset_z[:, :, None] + offset_y[:, None, :] * offset_y[:, None, :]
    )
    inside = (distance <= RADIUS * RADIUS).astype(jnp.bfloat16)
    count = jnp.einsum("xt,tzy->xzy", matches, inside, preferred_element_type=jnp.float32)
    return strength * count


def paired_plan(velocity, turbine_cells, fringe_bounds):
    groups = lax.axis_size("gx")
    initial = velocity[0]
    _, levels, cells_x, cells_y = initial.shape
    total_x, total_y = cells_x * groups, 2 * cells_y
    share, share_x = levels // ROWS, cells_x // 2
    section, place, core = (lax.axis_index("sec"), lax.axis_index("gx"), lax.axis_index("gy"))
    pencil, table_y, backward, table_z, inverse = tables(levels, total_x, total_y, groups)

    near, far = REACH - 4, 4
    up = [(i, (i + 1) % groups) for i in range(groups)]
    down = [(j, i) for i, j in up]
    swap = [(0, 1), (1, 0)]
    straight = [(2 * i, 2 * j) for i, j in up] + [(2 * j + 1, 2 * i + 1) for i, j in up]
    crossed = [(2 * i + 1, 2 * j) for i, j in up] + [(2 * j, 2 * i + 1) for i, j in up]
    own = jnp.transpose(initial.reshape(3, ROWS, share, cells_x, cells_y), (3, 0, 2, 1, 4))
    left = lax.ppermute(own[cells_x - near :], "gx", up)
    right = lax.ppermute(own[:near], "gx", down)
    tail, head = cells_x - REACH, near
    same = lax.dynamic_slice_in_dim(own, jnp.where(core == 0, tail, head), far, 0)
    other = lax.dynamic_slice_in_dim(own, jnp.where(core == 0, head, tail), far, 0)
    far_here = lax.ppermute(same, ("gx", "gy"), straight)
    far_there = lax.ppermute(other, ("gx", "gy"), crossed)
    own_there = lax.ppermute(own, "gy", swap)
    left_there = lax.ppermute(left, "gy", swap)
    right_there = lax.ppermute(right, "gy", swap)

    strength = 2.0 * THRUST_COEFF * section.astype(jnp.float32)
    along_z = jnp.arange(levels).reshape(ROWS, share).T.reshape(levels)

    def thrust_on(offset, count):
        along_x = (place * cells_x + offset + jnp.arange(count) + total_x) % total_x
        weights = thrust_weights(
            turbine_cells, along_x, jnp.arange(total_y), along_z, total_y, strength
        )
        return weights.reshape(count, share, ROWS, total_y)

    near_thrust = thrust_on(2 - near, cells_x + 2 * near - 4)
    far_thrust = thrust_on((2 - REACH) * (1 - core) + (share_x + 1) * core, far + near + share_x - 3)
    own_inverse = lax.dynamic_slice(
        inverse, (place, core, 0, 0, 0), (1, 1) + inverse.shape[2:]
    )[0, 0]

    f32 = jnp.float32
    body = (3, share, ROWS, total_y)

    def columns(count):
        return pltpu.VMEM((count,) + body, f32)

    reached = cells_x + 2 * near
    shapes = [jax.ShapeDtypeStruct((n,) + body, f32) for n in (4, 4, reached - 12)]
    first, second, third = call(
        near_kernel,
        shapes,
        [columns(reached)] * 3
        + [pltpu.VMEM((reached,) + body[1:], f32), pltpu.VMEM(body, f32)],
        own,
        own_there,
        left,
        left_there,
        right,
        right_there,
        near_thrust,
    )
    window = far + near + share_x + 1
    pairs = 3 * share // 2
    piece = jax.ShapeDtypeStruct((ROWS, pairs, 2 * share_x, cells_y), f32)
    parts = levels // (2 * groups)
    pieces, source = call(
        functools.partial(far_kernel, total_x),
        [
            jax.ShapeDtypeStruct((2,) + piece.shape, f32),
            jax.ShapeDtypeStruct((2 * share_x * levels, total_y), f32),
        ],
        [columns(window)] * 4
        + [
            pltpu.VMEM((window,) + body[1:], f32),
            pltpu.VMEM(body, f32),
            pltpu.VMEM((share_x * 3 * levels, cells_y), f32),
            pltpu.VMEM((share_x * 3 * levels, cells_y), f32),
        ],
        fringe_bounds,
        own,
        own_there,
        left,
        left_there,
        right,
        right_there,
        far_here,
        far_there,
        first,
        second,
        third,
        far_thrust,
    )
    outlet = [(g, groups + g) for g in range(groups - groups // 4, groups)]
    upstream = lax.ppermute(pieces, ("sec", "gx"), outlet)
    spectra = call(
        spectra_kernel,
        jax.ShapeDtypeStruct((2, groups, 2, parts, 2 * share_x, LANES), f32),
        [pltpu.VMEM((2, 2 * share_x * levels, LANES), f32)],
        source,
        table_y,
        table_z,
    )
    received = lax.all_to_all(
        spectra.reshape((4 * groups,) + spectra.shape[3:]), ("sec", "gx", "gy"), 0, 0, tiled=True
    ).reshape(spectra.shape)
    blended_here, blended_send = call(
        blend_kernel, [piece, piece], [], fringe_bounds, pieces, upstream
    )
    blended_there = lax.ppermute(blended_send, "gy", swap)
    pressure_rows = 3 * total_x // 4
    packed = call(
        pencil_kernel,
        jax.ShapeDtypeStruct((groups, pressure_rows + 3 * share * cells_x, LANES), f32),
        [],
        received,
        own_inverse,
        pencil,
        blended_here,
        blended_there,
    )
    returned = lax.all_to_all(packed, "gx", 0, 0, tiled=True)
    partner = lax.ppermute(returned[:, :pressure_rows], "gy", swap)
    velocity_next, pressure = call(
        project_kernel,
        [
            jax.ShapeDtypeStruct((3, share, total_x, cells_y), f32),
            jax.ShapeDtypeStruct((share, total_x, cells_y), f32),
        ],
        [],
        returned,
        partner,
        backward,
    )
    return (velocity_next[None], pressure[None])


def on_device(velocity, turbine_cells, fringe_bounds):
    groups = lax.axis_size("gx")
    _, _, levels, cells_x, cells_y = velocity.shape
    paired = (
        lax.axis_size("gy") == 2
        and lax.axis_size("sec") == 2
        and cells_y == LANES
        and cells_x == ROWS
        and groups == ROWS
        and 2 * levels == groups * groups
    )
    plan = paired_plan if paired else general_plan
    return plan(velocity, turbine_cells, fringe_bounds)


def solution(mesh):
    return jax.shard_map(
        on_device,
        mesh=mesh,
        in_specs=(P("sec", None, None, "gx", "gy"), P(), P()),
        out_specs=(P("sec", None, "gx", None, "gy"), P("sec", "gx", None, "gy")),
        check_vma=False,
    )
```

```python
import functools

import jax
import jax.numpy as jnp
import numpy as np
from jax import lax
from jax.experimental import pallas as pl
from jax.experimental.pallas import tpu as pltpu
from jax.sharding import PartitionSpec as P

RADIUS = 4


TIME_STEP = 0.05
SMAG_COEFF = 0.1
THRUST_COEFF = 4.0
DRIVING_FORCE = 0.1
FRINGE_BLEND = 0.5
HIGHEST = lax.Precision.HIGHEST
STAGES = 3
REACH = 2 * STAGES + 1
LANES = 128
SMALLEST = float(np.finfo(np.float32).tiny)
ROWS = 8
VMEM_BYTES = 20 * 1024 * 1024


def extended(x, sides, width):
    for axis, dim in sides:
        count, length = (lax.axis_size(axis), x.shape[dim])
        up = [(i, (i + 1) % count) for i in range(count)]
        down = [(j, i) for i, j in up]
        last = lax.slice_in_dim(x, length - width, length, axis=dim)
        initial = lax.slice_in_dim(x, 0, width, axis=dim)
        before = lax.ppermute(last, axis, up)
        after = lax.ppermute(initial, axis, down)
        x = jnp.concatenate([before, x, after], axis=dim)
    return x


def shifted(block, axis, distance):
    devices = range(lax.axis_size(axis))
    route = [(i - distance, i) for i in devices if i - distance in devices]
    return lax.ppermute(block, axis, route)


def cas_table(row_index, column_index, length):
    product = row_index[:, None] * column_index[None, :] % length
    angle = product.astype(jnp.float32) * (2.0 * jnp.pi / length)
    return jnp.cos(angle) + jnp.sin(angle)


def shift_up(values):
    zeros = jnp.zeros_like(values[..., :1, :, :])
    return jnp.concatenate([values[..., 1:, :, :], zeros], axis=-3)


def shift_down(values):
    zeros = jnp.zeros_like(values[..., :1, :, :])
    return jnp.concatenate([zeros, values[..., :-1, :, :]], axis=-3)


def thomas(right_side, eigen_value):
    length = right_side.shape[0]
    inverses = []
    reduced = []
    for level_index in range(length):
        if level_index == 0:
            diagonal = eigen_value - 1.0
        elif level_index == length - 1:
            diagonal = eigen_value - 3.0
        else:
            diagonal = eigen_value - 2.0
        if level_index == 0:
            pivot_now = diagonal
            current = right_side[0] / pivot_now
        else:
            pivot_now = diagonal - inverses[-1]
            current = (right_side[level_index] - reduced[-1]) / pivot_now
        inverses.append(1.0 / pivot_now)
        reduced.append(current)
    solution = [reduced[-1]]
    for level_index in range(length - 2, -1, -1):
        solution.append(reduced[level_index] - inverses[level_index] * solution[-1])
    return jnp.stack(solution[::-1])


def spanwise_derivative(values, sine_y):
    return -sine_y * jnp.roll(jnp.flip(values, axis=-1), 1, axis=-1)


def widened(values):
    return extended(values, (("gx", 1), ("gy", 2)), 1)


def disk_weights(turbine_cells, along_x, along_y, along_z, total_y):
    matches = (along_x[:, None] == turbine_cells[None, :, 0]).astype(jnp.float32)
    offset_y = (along_y[None, :] - turbine_cells[:, 1:2] + total_y // 2) % total_y - total_y // 2
    offset_z = along_z[None, :] - turbine_cells[:, 2:3]
    distance = (
        offset_z[:, :, None] * offset_z[:, :, None] + offset_y[:, None, :] * offset_y[:, None, :]
    )
    inside = (distance <= RADIUS * RADIUS).astype(jnp.float32)
    return jnp.einsum("xt,tzy->zxy", matches, inside, precision=HIGHEST)


def tendency(velocity_now, farm_flag, disk_weight):
    levels, cells_x, cells_y = (velocity_now.shape[1], velocity_now.shape[2], velocity_now.shape[3])
    border = widened(velocity_now.reshape(3 * levels, cells_x, cells_y)).reshape(
        3, levels, cells_x + 2, cells_y + 2
    )
    plus_x = border[:, :, 2:, 1:-1]
    minus_x = border[:, :, :-2, 1:-1]
    plus_y = border[:, :, 1:-1, 2:]
    minus_y = border[:, :, 1:-1, :-2]
    plus_z = shift_up(velocity_now)
    minus_z = shift_down(velocity_now)
    gradients = [0.5 * (plus_x - minus_x), 0.5 * (plus_y - minus_y), 0.5 * (plus_z - minus_z)]
    strain_squares = jnp.zeros_like(velocity_now[0])
    for component in range(3):
        strain_squares = (
            strain_squares + gradients[component][component] * gradients[component][component]
        )
        for direction in range(component + 1, 3):
            shear = 0.5 * (gradients[direction][component] + gradients[component][direction])
            strain_squares = strain_squares + 2.0 * shear * shear
    viscosity = SMAG_COEFF * jnp.sqrt(2.0 * strain_squares)
    visc_border = widened(viscosity)
    visc_plus_x = visc_border[:, 2:, 1:-1]
    visc_minus_x = visc_border[:, :-2, 1:-1]
    visc_plus_y = visc_border[:, 1:-1, 2:]
    visc_minus_y = visc_border[:, 1:-1, :-2]
    visc_plus_z = shift_up(viscosity)
    visc_minus_z = shift_down(viscosity)
    advection = 0.5 * (plus_x[0] * plus_x - minus_x[0] * minus_x)
    advection = advection + 0.5 * (plus_y[1] * plus_y - minus_y[1] * minus_y)
    advection = advection + 0.5 * (plus_z[2] * plus_z - minus_z[2] * minus_z)
    diffusion = 0.5 * (viscosity + visc_plus_x) * (plus_x - velocity_now) - 0.5 * (
        viscosity + visc_minus_x
    ) * (velocity_now - minus_x)
    diffusion = (
        diffusion
        + 0.5 * (viscosity + visc_plus_y) * (plus_y - velocity_now)
        - 0.5 * (viscosity + visc_minus_y) * (velocity_now - minus_y)
    )
    diffusion = (
        diffusion
        + 0.5 * (viscosity + visc_plus_z) * (plus_z - velocity_now)
        - 0.5 * (viscosity + visc_minus_z) * (velocity_now - minus_z)
    )
    changes = diffusion - advection
    streamwise = DRIVING_FORCE - THRUST_COEFF * farm_flag * disk_weight * velocity_now[0] * jnp.abs(
        velocity_now[0]
    )
    return jnp.concatenate([changes[:1] + streamwise[None], changes[1:]], axis=0)


def general_plan(velocity, turbine_cells, fringe_bounds):
    initial = velocity[0]
    levels, cells_x, cells_y = (initial.shape[1], initial.shape[2], initial.shape[3])
    total_y = cells_y * lax.axis_size("gy")
    x_anchor = lax.axis_index("gx") * cells_x
    y_anchor = lax.axis_index("gy") * cells_y
    farm_flag = lax.axis_index("sec").astype(jnp.float32)
    along_x = x_anchor + jnp.arange(cells_x, dtype=jnp.int32)
    along_y = y_anchor + jnp.arange(cells_y, dtype=jnp.int32)
    along_z = jnp.arange(levels, dtype=jnp.int32)
    disk_weight = disk_weights(turbine_cells, along_x, along_y, along_z, total_y)
    segment_one = initial + TIME_STEP * tendency(initial, farm_flag, disk_weight)
    segment_two = 0.75 * initial + 0.25 * (
        segment_one + TIME_STEP * tendency(segment_one, farm_flag, disk_weight)
    )
    segment_three = initial / 3.0 + 2.0 / 3.0 * (
        segment_two + TIME_STEP * tendency(segment_two, farm_flag, disk_weight)
    )
    regrouped = lax.all_to_all(segment_three, "gx", split_axis=1, concat_axis=2, tiled=True)
    count_x = regrouped.shape[2]
    quarter = count_x // 4
    cut_at = count_x - quarter
    outlet_part = regrouped[:, :, cut_at:, :]
    upstream = shifted(outlet_part, "sec", 1)
    columns = cut_at + jnp.arange(quarter, dtype=jnp.int32)
    inside = ((columns >= fringe_bounds[0]) & (columns < fringe_bounds[1])).astype(jnp.float32)
    weight = FRINGE_BLEND * farm_flag * inside
    blended_part = outlet_part + weight[:, None] * (upstream - outlet_part)
    regrouped = jnp.concatenate([regrouped[:, :, :cut_at, :], blended_part], axis=2)
    index_x = jnp.arange(count_x, dtype=jnp.int32)
    table_x = cas_table(index_x, index_x, count_x)
    gradient_u = 0.5 * (jnp.roll(regrouped[0], -1, axis=1) - jnp.roll(regrouped[0], 1, axis=1))
    fields = jnp.stack([gradient_u, regrouped[1], regrouped[2]])
    spectral_x = jnp.einsum("kx,czxy->czky", table_x, fields, precision=HIGHEST)
    columns_view = lax.all_to_all(
        lax.all_to_all(spectral_x, "gx", split_axis=2, concat_axis=1, tiled=True),
        "gy",
        split_axis=2,
        concat_axis=3,
        tiled=True,
    )
    slice_width = columns_view.shape[2]
    count_y = columns_view.shape[3]
    index_y = jnp.arange(count_y, dtype=jnp.int32)
    table_y = cas_table(index_y, index_y, count_y)
    spectrum = jnp.einsum("ly,czky->czkl", table_y, columns_view, precision=HIGHEST)
    sine_y = jnp.sin(index_y.astype(jnp.float32) * (2.0 * jnp.pi / count_y))
    source = (
        spectrum[0]
        + spanwise_derivative(spectrum[1], sine_y)
        + 0.5 * (shift_up(spectrum[2]) - shift_down(spectrum[2]))
    )
    wave_x = (
        lax.axis_index("gx") * cells_x
        + lax.axis_index("gy") * slice_width
        + jnp.arange(slice_width, dtype=jnp.int32)
    )
    eigen_value = 2.0 * jnp.cos(wave_x.astype(jnp.float32) * (2.0 * jnp.pi / count_x))[:, None]
    eigen_value = (
        eigen_value
        + 2.0 * jnp.cos(index_y.astype(jnp.float32) * (2.0 * jnp.pi / count_y))[None, :]
        - 4.0
    )
    solved = thomas(source, eigen_value)
    above_level = jnp.concatenate([solved[1:], -solved[-1:]], axis=0)
    below_level = jnp.concatenate([solved[:1], solved[:-1]], axis=0)
    coefficients = jnp.stack(
        [solved, spanwise_derivative(solved, sine_y), 0.5 * (above_level - below_level)]
    )
    physical_y = jnp.einsum("yl,czkl->czky", table_y, coefficients, precision=HIGHEST) * (
        1.0 / count_y
    )
    returned = lax.all_to_all(
        lax.all_to_all(physical_y, "gx", split_axis=1, concat_axis=2, tiled=True),
        "gy",
        split_axis=3,
        concat_axis=2,
        tiled=True,
    )
    group_size = count_x // lax.axis_size("gy")
    wave_back = (
        index_x // slice_width % lax.axis_size("gx") * cells_x
        + index_x // group_size * slice_width
        + index_x % slice_width
    )
    inverse_table = cas_table(index_x, wave_back, count_x)
    physical = jnp.einsum("xp,czpy->czxy", inverse_table, returned, precision=HIGHEST) * (
        1.0 / count_x
    )
    pressure = physical[0]
    gradient_p = 0.5 * (jnp.roll(pressure, -1, axis=1) - jnp.roll(pressure, 1, axis=1))
    velocity_next = regrouped - jnp.stack([gradient_p, physical[1], physical[2]])
    return (velocity_next[None], pressure[None])


def split(values):
    high = values.astype(jnp.bfloat16)
    low = values - high.astype(jnp.float32)
    return high, low.astype(jnp.bfloat16)


def dot(left, right):
    (a, da), (b, db) = split(left), split(right)

    def product(x, y):
        return jnp.dot(x, y, preferred_element_type=jnp.float32)

    return product(a, b) + (product(a, db) + product(da, b))


def swap_blocks(arrays, width):
    arrays = list(arrays)
    block = lax.broadcasted_iota(jnp.int32, arrays[0].shape, 1) // width
    step = 1
    while step < len(arrays):
        low = (block // step) % 2 == 0
        for index in range(len(arrays)):
            if (index // step) % 2 == 0:
                first, second = arrays[index], arrays[index + step]
                arrays[index] = jnp.where(low, first, pltpu.roll(second, step * width, 1))
                arrays[index + step] = jnp.where(
                    low, pltpu.roll(first, LANES - step * width, 1), second
                )
        step *= 2
    return arrays


class Stencil:
    def __init__(self, tiles, rows, width, viscosity, faces, thrust, start, beside):
        self.tiles, self.rows, self.width, self.beside = (tiles, rows, width, beside)
        self.viscosity, self.faces, self.thrust, self.start = (viscosity, faces, thrust, start)
        row = lax.broadcasted_iota(jnp.int32, (rows, width), 0)
        self.top = row == rows - 1
        self.bottom = row == 0

    def next_y(self, f):
        return pltpu.roll(f, self.width - 1, 1)

    def last_y(self, f):
        return pltpu.roll(f, 1, 1)

    def next_z(self, parts, t):
        if t < self.tiles - 1:
            return parts[t + 1]
        return jnp.where(self.top, 0.0, pltpu.roll(parts[0], self.rows - 1, 0))

    def last_z(self, parts, t):
        if t > 0:
            return parts[t - 1]
        return jnp.where(self.bottom, 0.0, pltpu.roll(parts[self.tiles - 1], 1, 0))

    def set_viscosity(self, now, first, count):
        tiles = self.tiles

        def column(n, carry):
            i = first + n
            here = [[now[i, c, t] for t in range(tiles)] for c in range(3)]
            found, sides = [], []
            for t in range(tiles):
                d_x = [now[i + 1, c, t] - now[i - 1, c, t] for c in range(3)]
                after_y = [self.next_y(f[t]) for f in here]
                sides.append(after_y)
                d_y = [a - self.last_y(f[t]) for a, f in zip(after_y, here)]
                d_z = [self.next_z(f, t) - self.last_z(f, t) for f in here]
                diagonal = d_x[0] * d_x[0] + d_y[1] * d_y[1] + d_z[2] * d_z[2]
                xy = d_x[1] + d_y[0]
                xz = d_x[2] + d_z[0]
                yz = d_y[2] + d_z[1]
                total = (diagonal + diagonal) + (xy * xy + xz * xz + yz * yz)
                root = total * lax.rsqrt(jnp.maximum(total, SMALLEST))
                found.append((0.5 * SMAG_COEFF) * root)
            for t in range(tiles):
                self.viscosity[i, t] = found[t]
                for c in range(3):
                    self.beside[i, c, t] = sides[t][c]
            return carry

        lax.fori_loop(0, count, column, 0, unroll=4 if count % 4 == 0 else 6)

    def face(self, both, here, after, lead):
        low = both + here[lead]
        high = both - after[lead]
        return [after[c] * high - here[c] * low for c in range(3)]

    def face_x(self, now, i, t):
        here = [now[i, c, t] for c in range(3)]
        after = [now[i + 1, c, t] for c in range(3)]
        return self.face(self.viscosity[i, t] + self.viscosity[i + 1, t], here, after, 0)

    def advance(self, now, then, first, count, keep, gain):
        tiles, scale = self.tiles, 0.5 * TIME_STEP * gain
        for t in range(tiles):
            for c, f in enumerate(self.face_x(now, first - 1, t)):
                self.faces[c, t] = f

        def column(n, carry):
            i = first + n
            eddy = [self.viscosity[i, t] for t in range(tiles)]
            field = [[now[i, c, t] for t in range(tiles)] for c in range(3)]

            def face_z(t):
                here = [f[t] for f in field]
                after = [self.next_z(f, t) for f in field]
                return self.face(eddy[t] + self.next_z(eddy, t), here, after, 2)

            last = face_z(tiles - 1)
            floor = eddy[0] - field[2][0]
            below = [
                jnp.where(self.bottom, field[c][0] * floor, pltpu.roll(last[c], 1, 0))
                for c in range(3)
            ]
            ahead_of = [self.face_x(now, i, t) for t in range(tiles)]
            before_of = [[self.faces[c, t] for c in range(3)] for t in range(tiles)]
            found = []
            for t in range(tiles):
                here = [f[t] for f in field]
                above = last if t == tiles - 1 else face_z(t)
                ahead, before = ahead_of[t], before_of[t]
                beside = [self.beside[i, c, t] for c in range(3)]
                side = self.face(eddy[t] + self.next_y(eddy[t]), here, beside, 1)
                for c in range(3):
                    change = (
                        (ahead[c] - before[c])
                        + (side[c] - self.last_y(side[c]))
                        + (above[c] - below[c])
                    )
                    if c == 0:
                        drag = self.thrust[i - 2, t] * here[0] * jnp.abs(here[0])
                        change = change + (2.0 * DRIVING_FORCE - drag)
                    if keep == 0.0:
                        found.append(here[c] + scale * change)
                    else:
                        found.append(keep * self.start[i, c, t] + gain * here[c] + scale * change)
                below = above
            for t in range(tiles):
                for c in range(3):
                    then[i, c, t] = found[3 * t + c]
                    self.faces[c, t] = ahead_of[t][c]
            return carry

        lax.fori_loop(0, count, column, 0, unroll=2)

    def stage(self, number, now, then, first, count):
        keep, gain = ((0.0, 1.0), (0.75, 0.25), (1.0 / 3.0, 2.0 / 3.0))[number]
        self.set_viscosity(now, first - 1, count + 2)
        self.advance(now, then, first, count, keep, gain)


def place_columns(start, core, runs):
    half = start.shape[-1] // 2

    def copy(low_is_here):
        for first, here, there, begin, count in runs:
            low, high = (here, there) if low_is_here else (there, here)
            start[pl.ds(first, count), :, :, :, :half] = low[pl.ds(begin, count)]
            start[pl.ds(first, count), :, :, :, half:] = high[pl.ds(begin, count)]

    pl.when(core == 0)(lambda: copy(True))
    pl.when(core == 1)(lambda: copy(False))


def near_kernel(
    own_here,
    own_there,
    left_here,
    left_there,
    right_here,
    right_there,
    thrust,
    first,
    second,
    third,
    start,
    stage_a,
    stage_b,
    viscosity,
    faces,
    beside,
):
    cells_x = own_here.shape[0]
    near = left_here.shape[0]
    _, _, tiles, rows, width = start.shape
    core = lax.axis_index("gy")
    place_columns(
        start,
        core,
        (
            (0, left_here, left_there, 0, near),
            (near, own_here, own_there, 0, cells_x),
            (near + cells_x, right_here, right_there, 0, near),
        ),
    )
    stencil = Stencil(tiles, rows, width, viscosity, faces, thrust, start, beside)
    columns = start.shape[0]
    stencil.stage(0, start, stage_a, 2, columns - 4)
    stencil.stage(1, stage_a, stage_b, 4, columns - 8)
    first[...] = stage_a[pl.ds(2 + core * (columns - 8), 4)]
    second[...] = stage_b[pl.ds(4 + core * (columns - 12), 4)]
    stencil.stage(2, stage_b, stage_a, 6, columns - 12)
    third[...] = stage_a[pl.ds(6, columns - 12)]


def far_kernel(
    total_x,
    fringe,
    own_here,
    own_there,
    left_here,
    left_there,
    right_here,
    right_there,
    far_here,
    far_there,
    first,
    second,
    third,
    thrust,
    pieces,
    source,
    start,
    stage_a,
    stage_b,
    stage_c,
    viscosity,
    faces,
    beside,
    columns_here,
    columns_there,
):
    cells_x = own_here.shape[0]
    near, far = left_here.shape[0], far_here.shape[0]
    _, _, tiles, rows, width = start.shape
    half = width // 2
    share_x = cells_x // 2
    inner = share_x + 1
    core = lax.axis_index("gy")

    @pl.when(core == 0)
    def _():
        place_columns(
            start,
            core,
            (
                (0, far_here, far_there, 0, far),
                (far, left_here, left_there, 0, near),
                (far + near, own_here, own_there, 0, inner),
            ),
        )

    @pl.when(core == 1)
    def _():
        place_columns(
            start,
            core,
            (
                (0, own_here, own_there, cells_x - inner, inner),
                (inner, right_here, right_there, 0, near),
                (inner + near, far_here, far_there, 0, far),
            ),
        )

    stencil = Stencil(tiles, rows, width, viscosity, faces, thrust, start, beside)
    stencil.stage(0, start, stage_a, 2 + 4 * core, 4)
    stage_a[pl.ds(6 - 4 * core, 4)] = first[...]
    stencil.stage(1, stage_a, stage_b, 4, 4)
    stage_b[pl.ds(8 - 8 * core, 4)] = second[...]
    stencil.stage(2, stage_b, stage_c, 6 - 4 * core, 4)
    stage_c[pl.ds(10 - 10 * core, 2)] = third[...]

    origin = REACH - core * (REACH - 1)
    pairs = 3 * tiles // 2
    for x in range(share_x):
        for c in range(3):
            for t in range(tiles):
                n = c * tiles + t
                field = stage_c[origin + x, c, t]
                low, high = field[:, :half], field[:, half:]
                spot = pl.ds((((n % 2) * share_x + x) * pairs + n // 2) * rows, rows)
                columns_here[spot, :] = jnp.where(core == 0, low, high)
                columns_there[spot, :] = jnp.where(core == 0, high, low)
    for s in range(rows):
        for m in range(pairs):
            spot = pl.ds(m * rows + s, 2 * share_x, stride=pairs * rows)
            pieces[0, s, m] = columns_here[spot, :]
            pieces[1, s, m] = columns_there[spot, :]

    is_farm = lax.axis_index("sec") == 1
    corner = lax.axis_index("gx") * cells_x + core * share_x

    def weight(offset, dest):
        place = lax.rem(corner + offset + total_x, total_x)
        inside = jnp.logical_and(place >= fringe[0], place < fringe[1])
        blend = jnp.where(inside, FRINGE_BLEND, 0.0)
        share = jnp.where(is_farm, 1.0 - blend, blend)
        if dest == 0:
            share = jnp.where(is_farm, 0.0, 1.0)
        return 0.5 * share

    for x in range(share_x):
        i = origin + x
        upright = [stage_c[i, 2, t] for t in range(tiles)]
        for t in range(tiles):
            cross = stage_c[i, 1, t]
            plane = (stencil.next_y(cross) - stencil.last_y(cross)) + (
                stencil.next_z(upright, t) - stencil.last_z(upright, t)
            )
            after, before = stage_c[i + 1, 0, t], stage_c[i - 1, 0, t]
            for dest in range(2):
                source[pl.ds(((dest * share_x + x) * tiles + t) * rows, rows), :] = (
                    weight(x + 1, dest) * after
                    - weight(x - 1, dest) * before
                    + weight(x, dest) * plane
                )


def fill_spectra(source, table_y, table_z, spectra, modes):
    _, groups, _, parts, rows, lanes = spectra.shape
    levels = table_z.shape[0]
    count, total_y = source.shape
    columns = count // levels
    along_y = dot(source[...], table_y[...])
    beside = [along_y[n * levels : (n + 1) * levels] for n in range(columns)]
    both = dot(table_z[...], jnp.concatenate(beside, axis=1))
    for n in range(columns):
        for h in range(2):
            first = n * total_y + h * lanes
            modes[h, pl.ds(n * levels, levels), :] = both[:, first : first + lanes]
    for dest in range(2):
        for h in range(2):
            for p in range(parts):
                first = dest * count // 2 + p * groups
                picked = [
                    modes[h, pl.ds(first + b, rows, stride=levels // 2), :] for b in range(groups)
                ]
                for g, block in enumerate(swap_blocks(picked, lanes // groups)):
                    spectra[dest, g, h, p] = block


def precursor_kernel(source, table_y, table_z, spectra, modes):
    @pl.when(lax.axis_index("sec") == 0)
    def _():
        fill_spectra(source, table_y, table_z, spectra, modes)


def farm_kernel(source, table_y, table_z, earlier, spectra, modes):
    @pl.when(lax.axis_index("sec") == 0)
    def _():
        spectra[...] = earlier[...]

    @pl.when(lax.axis_index("sec") == 1)
    def _():
        fill_spectra(source, table_y, table_z, spectra, modes)


def blend_kernel(fringe, pieces, upstream, blended_here, blended_there):
    _, groups, pairs, rows, lanes = pieces.shape
    half = rows // 2
    corner = lax.axis_index("gx") * rows + lax.axis_index("gy") * half
    place = corner + lax.broadcasted_iota(jnp.int32, (rows, lanes), 0) % half
    inside = jnp.logical_and(place >= fringe[0], place < fringe[1])
    inside = jnp.logical_and(inside, lax.axis_index("sec") == 1)
    weight = jnp.where(inside, FRINGE_BLEND, 0.0)[None, None]
    for n, blended in enumerate((blended_here, blended_there)):
        own = pieces[n]
        blended[...] = own + weight * (upstream[n] - own)


def pencil_kernel(received, inverse, table, blended_here, blended_there, packed):
    _, groups, cores, parts, rows, lanes = received.shape
    _, pairs, _, _ = blended_here.shape
    total_x = groups * rows
    lane_width = lanes // groups
    wave, base = 2 * total_x, table.shape[1]
    spread_z = table[:base]
    pair_x = table[base : base + wave, :wave]
    table_x = table[base : base + total_x, wave : wave + total_x]
    spectrum = jnp.concatenate(
        [(received[0, :, :, p] + received[1, :, :, p]).reshape(-1, lanes) for p in range(parts)],
        axis=1,
    )
    solved = dot(pair_x, spectrum)
    pieces = []
    for a in range(2 * parts):
        p, side = a % parts, a // parts
        block = solved[side * total_x : (side + 1) * total_x, p * lanes : (p + 1) * lanes]
        pieces.append(block * inverse[a])
    field = dot(dot(table_x, jnp.concatenate(pieces, axis=1)), spread_z)
    levels_of = [field[:, a * lanes : (a + 1) * lanes] for a in range(2 * parts)]
    wide = lax.broadcasted_iota(jnp.int32, (total_x // 2, lanes), 1)
    left = wide < lanes // 2
    quarter = total_x // 4
    block = lax.broadcasted_iota(jnp.int32, (quarter, lanes), 1) // lane_width
    low = lax.broadcasted_iota(jnp.int32, (rows, lanes), 0) < rows // 2
    is_first = lax.axis_index("gy") == 0
    for g in range(groups):
        a, odd = divmod(g, 2)
        now = levels_of[a]
        front, rear = now[: total_x // 2], now[total_x // 2 :]
        if odd:
            main = jnp.where(left, pltpu.roll(front, lanes // 2, 1), rear)
            lower, lower_lane = now, lanes // 2 - lane_width
            upper, upper_lane = levels_of[min(a + 1, 2 * parts - 1)], 0
        else:
            main = jnp.where(left, front, pltpu.roll(rear, lanes // 2, 1))
            lower, lower_lane = levels_of[max(a - 1, 0)], lanes - lane_width
            upper, upper_lane = now, lanes // 2
        edge = None
        for q in range(4):
            for n, (whole, lane) in enumerate(((lower, lower_lane), (upper, upper_lane))):
                spot = 2 * q + n
                move = (spot * lane_width - lane) % lanes
                rolled = whole[q * quarter : (q + 1) * quarter]
                if move:
                    rolled = pltpu.roll(rolled, move, 1)
                edge = rolled if edge is None else jnp.where(block == spot, rolled, edge)
        packed[g, : total_x // 2] = main
        packed[g, total_x // 2 : 3 * quarter] = edge
        for m in range(pairs):
            here, there = blended_here[g, m], blended_there[g, m]
            before = jnp.where(is_first, here, there)
            after = jnp.where(is_first, there, here)
            first = 3 * quarter + 2 * m * rows
            packed[g, first : first + rows] = jnp.where(
                low, before, pltpu.roll(after, rows // 2, 0)
            )
            packed[g, first + rows : first + 2 * rows] = jnp.where(
                low, pltpu.roll(before, rows // 2, 0), after
            )


def project_kernel(received, partner, table_y, velocity_next, pressure):
    groups = received.shape[0]
    share, total_x, lanes = pressure.shape
    cells_x = total_x // groups
    width = lanes // groups
    place, core = lax.axis_index("gx"), lax.axis_index("gy")
    main_rows = total_x // 2
    rows = partner.shape[1]

    def levels_in(arrays):
        main = swap_blocks([arrays[s, :main_rows] for s in range(groups)], width)
        edge = swap_blocks([arrays[s, main_rows:rows] for s in range(groups)], width)
        inner = [jnp.concatenate([main[n], main[share + n]], axis=0) for n in range(share)]
        outer = [jnp.concatenate([edge[2 * q + n] for q in range(4)], axis=0) for n in range(2)]
        return [outer[0]] + inner + [outer[1]]

    here, there = levels_in(received), levels_in(partner)
    here, there = jnp.concatenate(here, axis=0), jnp.concatenate(there, axis=0)
    low = jnp.where(core == 0, here, there)
    high = jnp.where(core == 0, there, here)
    both = dot(jnp.concatenate([low, high], axis=1), table_y[core])
    fields = [both[n * total_x : (n + 1) * total_x] for n in range(share + 2)]
    values = [f[:, :lanes] for f in fields]
    values[0] = jnp.where(place == 0, values[1], values[0])
    values[-1] = jnp.where(place == groups - 1, -values[-2], values[-1])
    for z in range(share):
        now = values[z + 1]
        pressure[z] = now
        slopes = [
            0.5 * (pltpu.roll(now, total_x - 1, 0) - pltpu.roll(now, 1, 0)),
            fields[z + 1][:, lanes:],
            0.5 * (values[z + 2] - values[z]),
        ]
        for c in range(3):
            first = rows + (c * share + z) * cells_x
            blended = received[:, first : first + cells_x].reshape(total_x, lanes)
            velocity_next[c, z] = blended - slopes[c]


def cas(rows, columns, length):
    angle = (np.outer(rows, columns) % length) * (2.0 * np.pi / length)
    return np.cos(angle) + np.sin(angle)


def tables(levels, total_x, total_y, groups):
    half = total_y // 2
    lane_width = LANES // groups
    every_x = np.arange(total_x)
    every_y = np.arange(total_y)
    table_x = cas(every_x, every_x, total_x)
    table_y = cas(every_y, every_y, total_y)
    slope_y = 0.5 * (np.roll(table_y, -1, axis=1) - np.roll(table_y, 1, axis=1))
    level = np.arange(levels) + 0.5
    table_z = np.cos(np.outer(level, level) * (np.pi / levels))
    spread_z = np.kron(table_z, np.eye(lane_width))
    order = np.arange(levels).reshape(ROWS, levels // ROWS).T.reshape(levels)
    backward = [
        np.concatenate([table_y[:, here], slope_y[:, here]], axis=1)
        for here in (slice(0, half), slice(half, total_y))
    ]
    pair_x = np.einsum("kx,ab->akxb", table_x, np.eye(2)).reshape(2 * total_x, 2 * total_x)
    eigen = (
        (2.0 * np.cos(level * (np.pi / levels)) - 2.0)[:, None, None]
        + (2.0 * np.cos(every_x * (2.0 * np.pi / total_x)) - 2.0)[None, :, None]
        + (2.0 * np.cos(every_y * (2.0 * np.pi / total_y)) - 2.0)[None, None, :]
    )
    inverse = (2.0 / levels) / (total_x * total_y) / eigen
    inverse = inverse.reshape(levels // groups, groups, total_x, 2, groups, lane_width)
    inverse = inverse.transpose(4, 3, 0, 2, 1, 5).reshape(
        groups, 2, levels // groups, total_x, LANES
    )
    pencil = np.zeros((spread_z.shape[0] + 2 * total_x, spread_z.shape[1]))
    pencil[: spread_z.shape[0]] = spread_z
    pencil[spread_z.shape[0] :, : 2 * total_x] = pair_x
    pencil[spread_z.shape[0] : -total_x, 2 * total_x : 3 * total_x] = table_x
    return [
        jnp.asarray(t, jnp.float32)
        for t in (
            pencil,
            table_y,
            np.stack(backward),
            table_z[:, order],
            inverse,
        )
    ]


def call(kernel, out_shapes, scratch, *operands):
    in_specs = [
        pl.BlockSpec(memory_space=pltpu.SMEM if o.dtype == jnp.int32 else pltpu.VMEM)
        for o in operands
    ]
    return pl.pallas_call(
        kernel,
        out_shape=out_shapes,
        in_specs=in_specs,
        out_specs=jax.tree.map(lambda _: pl.BlockSpec(memory_space=pltpu.VMEM), out_shapes),
        scratch_shapes=scratch,
        compiler_params=pltpu.CompilerParams(vmem_limit_bytes=VMEM_BYTES),
    )(*operands)


def thrust_weights(turbine_cells, along_x, along_y, along_z, total_y, strength):
    matches = (along_x[:, None] == turbine_cells[None, :, 0]).astype(jnp.bfloat16)
    offset_y = (along_y[None, :] - turbine_cells[:, 1:2] + total_y // 2) % total_y - total_y // 2
    offset_z = along_z[None, :] - turbine_cells[:, 2:3]
    distance = (
        offset_z[:, :, None] * offset_z[:, :, None] + offset_y[:, None, :] * offset_y[:, None, :]
    )
    inside = (distance <= RADIUS * RADIUS).astype(jnp.bfloat16)
    count = jnp.einsum("xt,tzy->xzy", matches, inside, preferred_element_type=jnp.float32)
    return strength * count


def paired_plan(velocity, turbine_cells, fringe_bounds):
    groups = lax.axis_size("gx")
    initial = velocity[0]
    _, levels, cells_x, cells_y = initial.shape
    total_x, total_y = cells_x * groups, 2 * cells_y
    share, share_x = levels // ROWS, cells_x // 2
    section, place, core = (lax.axis_index("sec"), lax.axis_index("gx"), lax.axis_index("gy"))
    pencil, table_y, backward, table_z, inverse = tables(levels, total_x, total_y, groups)

    near, far = REACH - 4, 4
    up = [(i, (i + 1) % groups) for i in range(groups)]
    down = [(j, i) for i, j in up]
    swap = [(0, 1), (1, 0)]
    straight = [(2 * i, 2 * j) for i, j in up] + [(2 * j + 1, 2 * i + 1) for i, j in up]
    crossed = [(2 * i + 1, 2 * j) for i, j in up] + [(2 * j, 2 * i + 1) for i, j in up]
    own = jnp.transpose(initial.reshape(3, ROWS, share, cells_x, cells_y), (3, 0, 2, 1, 4))
    left = lax.ppermute(own[cells_x - near :], "gx", up)
    right = lax.ppermute(own[:near], "gx", down)
    tail, head = cells_x - REACH, near
    same = lax.dynamic_slice_in_dim(own, jnp.where(core == 0, tail, head), far, 0)
    other = lax.dynamic_slice_in_dim(own, jnp.where(core == 0, head, tail), far, 0)
    own_there = lax.ppermute(own, "gy", swap)
    other, left = lax.optimization_barrier((other, left))
    far_there = lax.ppermute(other, ("gx", "gy"), crossed)
    left_there = lax.ppermute(left, "gy", swap)
    right_there = lax.ppermute(right, "gy", swap)

    strength = 2.0 * THRUST_COEFF * section.astype(jnp.float32)
    along_z = jnp.arange(levels).reshape(ROWS, share).T.reshape(levels)

    def thrust_on(offset, count):
        along_x = (place * cells_x + offset + jnp.arange(count) + total_x) % total_x
        weights = thrust_weights(
            turbine_cells, along_x, jnp.arange(total_y), along_z, total_y, strength
        )
        return weights.reshape(count, share, ROWS, total_y)

    near_thrust = thrust_on(2 - near, cells_x + 2 * near - 4)
    far_thrust = thrust_on((2 - REACH) * (1 - core) + (share_x + 1) * core, far + near + share_x - 3)
    same, near_thrust, far_thrust = lax.optimization_barrier((same, near_thrust, far_thrust))
    far_here = lax.ppermute(same, ("gx", "gy"), straight)
    own_inverse = lax.dynamic_slice(
        inverse, (place, core, 0, 0, 0), (1, 1) + inverse.shape[2:]
    )[0, 0]

    f32 = jnp.float32
    body = (3, share, ROWS, total_y)

    def columns(count):
        return pltpu.VMEM((count,) + body, f32)

    reached = cells_x + 2 * near
    shapes = [jax.ShapeDtypeStruct((n,) + body, f32) for n in (4, 4, reached - 12)]
    first, second, third = call(
        near_kernel,
        shapes,
        [columns(reached)] * 3
        + [pltpu.VMEM((reached,) + body[1:], f32), pltpu.VMEM(body, f32), columns(reached)],
        own,
        own_there,
        left,
        left_there,
        right,
        right_there,
        near_thrust,
    )
    window = far + near + share_x + 1
    pairs = 3 * share // 2
    piece = jax.ShapeDtypeStruct((ROWS, pairs, 2 * share_x, cells_y), f32)
    parts = levels // (2 * groups)
    pieces, source = call(
        functools.partial(far_kernel, total_x),
        [
            jax.ShapeDtypeStruct((2,) + piece.shape, f32),
            jax.ShapeDtypeStruct((2 * share_x * levels, total_y), f32),
        ],
        [columns(window)] * 4
        + [
            pltpu.VMEM((window,) + body[1:], f32),
            pltpu.VMEM(body, f32),
            columns(window),
            pltpu.VMEM((share_x * 3 * levels, cells_y), f32),
            pltpu.VMEM((share_x * 3 * levels, cells_y), f32),
        ],
        fringe_bounds,
        own,
        own_there,
        left,
        left_there,
        right,
        right_there,
        far_here,
        far_there,
        first,
        second,
        third,
        far_thrust,
    )
    outlet = [(g, groups + g) for g in range(groups - groups // 4, groups)]
    spectra_shape = jax.ShapeDtypeStruct((2, groups, 2, parts, 2 * share_x, LANES), f32)
    modes = [pltpu.VMEM((2, 2 * share_x * levels, LANES), f32)]
    earlier = call(precursor_kernel, spectra_shape, modes, source, table_y, table_z)
    earlier, pieces = lax.optimization_barrier((earlier, pieces))
    upstream = lax.ppermute(pieces, ("sec", "gx"), outlet)
    spectra = call(farm_kernel, spectra_shape, modes, source, table_y, table_z, earlier)
    received = lax.all_to_all(
        spectra.reshape((4 * groups,) + spectra.shape[3:]), ("sec", "gx", "gy"), 0, 0, tiled=True
    ).reshape(spectra.shape)
    blended_here, blended_send = call(
        blend_kernel, [piece, piece], [], fringe_bounds, pieces, upstream
    )
    blended_there = lax.ppermute(blended_send, "gy", swap)
    pressure_rows = 3 * total_x // 4
    packed = call(
        pencil_kernel,
        jax.ShapeDtypeStruct((groups, pressure_rows + 3 * share * cells_x, LANES), f32),
        [],
        received,
        own_inverse,
        pencil,
        blended_here,
        blended_there,
    )
    returned = lax.all_to_all(packed, "gx", 0, 0, tiled=True)
    partner = lax.ppermute(returned[:, :pressure_rows], "gy", swap)
    velocity_next, pressure = call(
        project_kernel,
        [
            jax.ShapeDtypeStruct((3, share, total_x, cells_y), f32),
            jax.ShapeDtypeStruct((share, total_x, cells_y), f32),
        ],
        [],
        returned,
        partner,
        backward,
    )
    return (velocity_next[None], pressure[None])


def on_device(velocity, turbine_cells, fringe_bounds):
    groups = lax.axis_size("gx")
    _, _, levels, cells_x, cells_y = velocity.shape
    paired = (
        lax.axis_size("gy") == 2
        and lax.axis_size("sec") == 2
        and cells_y == LANES
        and cells_x == ROWS
        and groups == ROWS
        and 2 * levels == groups * groups
    )
    plan = paired_plan if paired else general_plan
    return plan(velocity, turbine_cells, fringe_bounds)


def solution(mesh):
    return jax.shard_map(
        on_device,
        mesh=mesh,
        in_specs=(P("sec", None, None, "gx", "gy"), P(), P()),
        out_specs=(P("sec", None, "gx", None, "gy"), P("sec", "gx", None, "gy")),
        check_vma=False,
    )
```

```python
import functools

import jax
import jax.numpy as jnp
import numpy as np
from jax import lax
from jax.experimental import pallas as pl
from jax.experimental.pallas import tpu as pltpu
from jax.sharding import PartitionSpec as P

RADIUS = 4


TIME_STEP = 0.05
SMAG_COEFF = 0.1
THRUST_COEFF = 4.0
DRIVING_FORCE = 0.1
FRINGE_BLEND = 0.5
HIGHEST = lax.Precision.HIGHEST
STAGES = 3
REACH = 2 * STAGES + 1
LANES = 128
SMALLEST = float(np.finfo(np.float32).tiny)
ROWS = 8
VMEM_BYTES = 20 * 1024 * 1024


def extended(x, sides, width):
    for axis, dim in sides:
        count, length = (lax.axis_size(axis), x.shape[dim])
        up = [(i, (i + 1) % count) for i in range(count)]
        down = [(j, i) for i, j in up]
        last = lax.slice_in_dim(x, length - width, length, axis=dim)
        initial = lax.slice_in_dim(x, 0, width, axis=dim)
        before = lax.ppermute(last, axis, up)
        after = lax.ppermute(initial, axis, down)
        x = jnp.concatenate([before, x, after], axis=dim)
    return x


def shifted(block, axis, distance):
    devices = range(lax.axis_size(axis))
    route = [(i - distance, i) for i in devices if i - distance in devices]
    return lax.ppermute(block, axis, route)


def cas_table(row_index, column_index, length):
    product = row_index[:, None] * column_index[None, :] % length
    angle = product.astype(jnp.float32) * (2.0 * jnp.pi / length)
    return jnp.cos(angle) + jnp.sin(angle)


def shift_up(values):
    zeros = jnp.zeros_like(values[..., :1, :, :])
    return jnp.concatenate([values[..., 1:, :, :], zeros], axis=-3)


def shift_down(values):
    zeros = jnp.zeros_like(values[..., :1, :, :])
    return jnp.concatenate([zeros, values[..., :-1, :, :]], axis=-3)


def thomas(right_side, eigen_value):
    length = right_side.shape[0]
    inverses = []
    reduced = []
    for level_index in range(length):
        if level_index == 0:
            diagonal = eigen_value - 1.0
        elif level_index == length - 1:
            diagonal = eigen_value - 3.0
        else:
            diagonal = eigen_value - 2.0
        if level_index == 0:
            pivot_now = diagonal
            current = right_side[0] / pivot_now
        else:
            pivot_now = diagonal - inverses[-1]
            current = (right_side[level_index] - reduced[-1]) / pivot_now
        inverses.append(1.0 / pivot_now)
        reduced.append(current)
    solution = [reduced[-1]]
    for level_index in range(length - 2, -1, -1):
        solution.append(reduced[level_index] - inverses[level_index] * solution[-1])
    return jnp.stack(solution[::-1])


def spanwise_derivative(values, sine_y):
    return -sine_y * jnp.roll(jnp.flip(values, axis=-1), 1, axis=-1)


def widened(values):
    return extended(values, (("gx", 1), ("gy", 2)), 1)


def disk_weights(turbine_cells, along_x, along_y, along_z, total_y):
    matches = (along_x[:, None] == turbine_cells[None, :, 0]).astype(jnp.float32)
    offset_y = (along_y[None, :] - turbine_cells[:, 1:2] + total_y // 2) % total_y - total_y // 2
    offset_z = along_z[None, :] - turbine_cells[:, 2:3]
    distance = (
        offset_z[:, :, None] * offset_z[:, :, None] + offset_y[:, None, :] * offset_y[:, None, :]
    )
    inside = (distance <= RADIUS * RADIUS).astype(jnp.float32)
    return jnp.einsum("xt,tzy->zxy", matches, inside, precision=HIGHEST)


def tendency(velocity_now, farm_flag, disk_weight):
    levels, cells_x, cells_y = (velocity_now.shape[1], velocity_now.shape[2], velocity_now.shape[3])
    border = widened(velocity_now.reshape(3 * levels, cells_x, cells_y)).reshape(
        3, levels, cells_x + 2, cells_y + 2
    )
    plus_x = border[:, :, 2:, 1:-1]
    minus_x = border[:, :, :-2, 1:-1]
    plus_y = border[:, :, 1:-1, 2:]
    minus_y = border[:, :, 1:-1, :-2]
    plus_z = shift_up(velocity_now)
    minus_z = shift_down(velocity_now)
    gradients = [0.5 * (plus_x - minus_x), 0.5 * (plus_y - minus_y), 0.5 * (plus_z - minus_z)]
    strain_squares = jnp.zeros_like(velocity_now[0])
    for component in range(3):
        strain_squares = (
            strain_squares + gradients[component][component] * gradients[component][component]
        )
        for direction in range(component + 1, 3):
            shear = 0.5 * (gradients[direction][component] + gradients[component][direction])
            strain_squares = strain_squares + 2.0 * shear * shear
    viscosity = SMAG_COEFF * jnp.sqrt(2.0 * strain_squares)
    visc_border = widened(viscosity)
    visc_plus_x = visc_border[:, 2:, 1:-1]
    visc_minus_x = visc_border[:, :-2, 1:-1]
    visc_plus_y = visc_border[:, 1:-1, 2:]
    visc_minus_y = visc_border[:, 1:-1, :-2]
    visc_plus_z = shift_up(viscosity)
    visc_minus_z = shift_down(viscosity)
    advection = 0.5 * (plus_x[0] * plus_x - minus_x[0] * minus_x)
    advection = advection + 0.5 * (plus_y[1] * plus_y - minus_y[1] * minus_y)
    advection = advection + 0.5 * (plus_z[2] * plus_z - minus_z[2] * minus_z)
    diffusion = 0.5 * (viscosity + visc_plus_x) * (plus_x - velocity_now) - 0.5 * (
        viscosity + visc_minus_x
    ) * (velocity_now - minus_x)
    diffusion = (
        diffusion
        + 0.5 * (viscosity + visc_plus_y) * (plus_y - velocity_now)
        - 0.5 * (viscosity + visc_minus_y) * (velocity_now - minus_y)
    )
    diffusion = (
        diffusion
        + 0.5 * (viscosity + visc_plus_z) * (plus_z - velocity_now)
        - 0.5 * (viscosity + visc_minus_z) * (velocity_now - minus_z)
    )
    changes = diffusion - advection
    streamwise = DRIVING_FORCE - THRUST_COEFF * farm_flag * disk_weight * velocity_now[0] * jnp.abs(
        velocity_now[0]
    )
    return jnp.concatenate([changes[:1] + streamwise[None], changes[1:]], axis=0)


def general_plan(velocity, turbine_cells, fringe_bounds):
    initial = velocity[0]
    levels, cells_x, cells_y = (initial.shape[1], initial.shape[2], initial.shape[3])
    total_y = cells_y * lax.axis_size("gy")
    x_anchor = lax.axis_index("gx") * cells_x
    y_anchor = lax.axis_index("gy") * cells_y
    farm_flag = lax.axis_index("sec").astype(jnp.float32)
    along_x = x_anchor + jnp.arange(cells_x, dtype=jnp.int32)
    along_y = y_anchor + jnp.arange(cells_y, dtype=jnp.int32)
    along_z = jnp.arange(levels, dtype=jnp.int32)
    disk_weight = disk_weights(turbine_cells, along_x, along_y, along_z, total_y)
    segment_one = initial + TIME_STEP * tendency(initial, farm_flag, disk_weight)
    segment_two = 0.75 * initial + 0.25 * (
        segment_one + TIME_STEP * tendency(segment_one, farm_flag, disk_weight)
    )
    segment_three = initial / 3.0 + 2.0 / 3.0 * (
        segment_two + TIME_STEP * tendency(segment_two, farm_flag, disk_weight)
    )
    regrouped = lax.all_to_all(segment_three, "gx", split_axis=1, concat_axis=2, tiled=True)
    count_x = regrouped.shape[2]
    quarter = count_x // 4
    cut_at = count_x - quarter
    outlet_part = regrouped[:, :, cut_at:, :]
    upstream = shifted(outlet_part, "sec", 1)
    columns = cut_at + jnp.arange(quarter, dtype=jnp.int32)
    inside = ((columns >= fringe_bounds[0]) & (columns < fringe_bounds[1])).astype(jnp.float32)
    weight = FRINGE_BLEND * farm_flag * inside
    blended_part = outlet_part + weight[:, None] * (upstream - outlet_part)
    regrouped = jnp.concatenate([regrouped[:, :, :cut_at, :], blended_part], axis=2)
    index_x = jnp.arange(count_x, dtype=jnp.int32)
    table_x = cas_table(index_x, index_x, count_x)
    gradient_u = 0.5 * (jnp.roll(regrouped[0], -1, axis=1) - jnp.roll(regrouped[0], 1, axis=1))
    fields = jnp.stack([gradient_u, regrouped[1], regrouped[2]])
    spectral_x = jnp.einsum("kx,czxy->czky", table_x, fields, precision=HIGHEST)
    columns_view = lax.all_to_all(
        lax.all_to_all(spectral_x, "gx", split_axis=2, concat_axis=1, tiled=True),
        "gy",
        split_axis=2,
        concat_axis=3,
        tiled=True,
    )
    slice_width = columns_view.shape[2]
    count_y = columns_view.shape[3]
    index_y = jnp.arange(count_y, dtype=jnp.int32)
    table_y = cas_table(index_y, index_y, count_y)
    spectrum = jnp.einsum("ly,czky->czkl", table_y, columns_view, precision=HIGHEST)
    sine_y = jnp.sin(index_y.astype(jnp.float32) * (2.0 * jnp.pi / count_y))
    source = (
        spectrum[0]
        + spanwise_derivative(spectrum[1], sine_y)
        + 0.5 * (shift_up(spectrum[2]) - shift_down(spectrum[2]))
    )
    wave_x = (
        lax.axis_index("gx") * cells_x
        + lax.axis_index("gy") * slice_width
        + jnp.arange(slice_width, dtype=jnp.int32)
    )
    eigen_value = 2.0 * jnp.cos(wave_x.astype(jnp.float32) * (2.0 * jnp.pi / count_x))[:, None]
    eigen_value = (
        eigen_value
        + 2.0 * jnp.cos(index_y.astype(jnp.float32) * (2.0 * jnp.pi / count_y))[None, :]
        - 4.0
    )
    solved = thomas(source, eigen_value)
    above_level = jnp.concatenate([solved[1:], -solved[-1:]], axis=0)
    below_level = jnp.concatenate([solved[:1], solved[:-1]], axis=0)
    coefficients = jnp.stack(
        [solved, spanwise_derivative(solved, sine_y), 0.5 * (above_level - below_level)]
    )
    physical_y = jnp.einsum("yl,czkl->czky", table_y, coefficients, precision=HIGHEST) * (
        1.0 / count_y
    )
    returned = lax.all_to_all(
        lax.all_to_all(physical_y, "gx", split_axis=1, concat_axis=2, tiled=True),
        "gy",
        split_axis=3,
        concat_axis=2,
        tiled=True,
    )
    group_size = count_x // lax.axis_size("gy")
    wave_back = (
        index_x // slice_width % lax.axis_size("gx") * cells_x
        + index_x // group_size * slice_width
        + index_x % slice_width
    )
    inverse_table = cas_table(index_x, wave_back, count_x)
    physical = jnp.einsum("xp,czpy->czxy", inverse_table, returned, precision=HIGHEST) * (
        1.0 / count_x
    )
    pressure = physical[0]
    gradient_p = 0.5 * (jnp.roll(pressure, -1, axis=1) - jnp.roll(pressure, 1, axis=1))
    velocity_next = regrouped - jnp.stack([gradient_p, physical[1], physical[2]])
    return (velocity_next[None], pressure[None])


def split(values):
    high = values.astype(jnp.bfloat16)
    low = values - high.astype(jnp.float32)
    return high, low.astype(jnp.bfloat16)


def dot(left, right):
    (a, da), (b, db) = split(left), split(right)

    def product(x, y):
        return jnp.dot(x, y, preferred_element_type=jnp.float32)

    return product(a, b) + (product(a, db) + product(da, b))


def swap_blocks(arrays, width):
    arrays = list(arrays)
    block = lax.broadcasted_iota(jnp.int32, arrays[0].shape, 1) // width
    step = 1
    while step < len(arrays):
        low = (block // step) % 2 == 0
        for index in range(len(arrays)):
            if (index // step) % 2 == 0:
                first, second = arrays[index], arrays[index + step]
                arrays[index] = jnp.where(low, first, pltpu.roll(second, step * width, 1))
                arrays[index + step] = jnp.where(
                    low, pltpu.roll(first, LANES - step * width, 1), second
                )
        step *= 2
    return arrays


class Stencil:
    def __init__(self, tiles, rows, width, viscosity, faces, thrust, start, beside):
        self.tiles, self.rows, self.width, self.beside = (tiles, rows, width, beside)
        self.viscosity, self.faces, self.thrust, self.start = (viscosity, faces, thrust, start)
        row = lax.broadcasted_iota(jnp.int32, (rows, width), 0)
        self.top = row == rows - 1
        self.bottom = row == 0

    def next_y(self, f):
        return pltpu.roll(f, self.width - 1, 1)

    def last_y(self, f):
        return pltpu.roll(f, 1, 1)

    def next_z(self, parts, t):
        if t < self.tiles - 1:
            return parts[t + 1]
        return jnp.where(self.top, 0.0, pltpu.roll(parts[0], self.rows - 1, 0))

    def last_z(self, parts, t):
        if t > 0:
            return parts[t - 1]
        return jnp.where(self.bottom, 0.0, pltpu.roll(parts[self.tiles - 1], 1, 0))

    def set_viscosity(self, now, first, count):
        tiles = self.tiles

        def column(n, carry):
            i = first + n
            here = [[now[i, c, t] for t in range(tiles)] for c in range(3)]
            found, sides = [], []
            for t in range(tiles):
                d_x = [now[i + 1, c, t] - now[i - 1, c, t] for c in range(3)]
                after_y = [self.next_y(f[t]) for f in here]
                sides.append(after_y)
                d_y = [a - self.last_y(f[t]) for a, f in zip(after_y, here)]
                d_z = [self.next_z(f, t) - self.last_z(f, t) for f in here]
                diagonal = d_x[0] * d_x[0] + d_y[1] * d_y[1] + d_z[2] * d_z[2]
                xy = d_x[1] + d_y[0]
                xz = d_x[2] + d_z[0]
                yz = d_y[2] + d_z[1]
                total = (diagonal + diagonal) + (xy * xy + xz * xz + yz * yz)
                root = total * lax.rsqrt(jnp.maximum(total, SMALLEST))
                found.append((0.5 * SMAG_COEFF) * root)
            for t in range(tiles):
                self.viscosity[i, t] = found[t]
                for c in range(3):
                    self.beside[i, c, t] = sides[t][c]
            return carry

        lax.fori_loop(0, count, column, 0, unroll=4 if count % 4 == 0 else 6)

    def face(self, both, here, after, lead):
        low = both + here[lead]
        high = both - after[lead]
        return [after[c] * high - here[c] * low for c in range(3)]

    def face_x(self, now, i, t):
        here = [now[i, c, t] for c in range(3)]
        after = [now[i + 1, c, t] for c in range(3)]
        return self.face(self.viscosity[i, t] + self.viscosity[i + 1, t], here, after, 0)

    def advance(self, now, then, first, count, keep, gain):
        tiles, scale = self.tiles, 0.5 * TIME_STEP * gain
        for t in range(tiles):
            for c, f in enumerate(self.face_x(now, first - 1, t)):
                self.faces[c, t] = f

        def column(n, carry):
            i = first + n
            eddy = [self.viscosity[i, t] for t in range(tiles)]
            field = [[now[i, c, t] for t in range(tiles)] for c in range(3)]

            def face_z(t):
                here = [f[t] for f in field]
                after = [self.next_z(f, t) for f in field]
                return self.face(eddy[t] + self.next_z(eddy, t), here, after, 2)

            last = face_z(tiles - 1)
            floor = eddy[0] - field[2][0]
            below = [
                jnp.where(self.bottom, field[c][0] * floor, pltpu.roll(last[c], 1, 0))
                for c in range(3)
            ]
            ahead_of = [self.face_x(now, i, t) for t in range(tiles)]
            before_of = [[self.faces[c, t] for c in range(3)] for t in range(tiles)]
            found = []
            for t in range(tiles):
                here = [f[t] for f in field]
                above = last if t == tiles - 1 else face_z(t)
                ahead, before = ahead_of[t], before_of[t]
                beside = [self.beside[i, c, t] for c in range(3)]
                side = self.face(eddy[t] + self.next_y(eddy[t]), here, beside, 1)
                for c in range(3):
                    change = (
                        (ahead[c] - before[c])
                        + (side[c] - self.last_y(side[c]))
                        + (above[c] - below[c])
                    )
                    if c == 0:
                        drag = self.thrust[i - 2, t] * here[0] * jnp.abs(here[0])
                        change = change + (2.0 * DRIVING_FORCE - drag)
                    if keep == 0.0:
                        found.append(here[c] + scale * change)
                    else:
                        found.append(keep * self.start[i, c, t] + gain * here[c] + scale * change)
                below = above
            for t in range(tiles):
                for c in range(3):
                    then[i, c, t] = found[3 * t + c]
                    self.faces[c, t] = ahead_of[t][c]
            return carry

        lax.fori_loop(0, count, column, 0, unroll=2)

    def stage(self, number, now, then, first, count):
        keep, gain = ((0.0, 1.0), (0.75, 0.25), (1.0 / 3.0, 2.0 / 3.0))[number]
        self.set_viscosity(now, first - 1, count + 2)
        self.advance(now, then, first, count, keep, gain)


def place_columns(start, runs_of):
    half = start.shape[-1] // 2
    core = lax.axis_index("gy")
    odd = lax.axis_index("gx") % 2

    def copy(side, parity):
        for first, here, there, begin, count in runs_of(side, parity):
            low, high = (here, there) if side == 0 else (there, here)
            start[pl.ds(first, count), :, :, :, :half] = low[pl.ds(begin, count)]
            start[pl.ds(first, count), :, :, :, half:] = high[pl.ds(begin, count)]

    for side in range(2):
        for parity in range(2):
            chosen = jnp.logical_and(core == side, odd == parity)
            pl.when(chosen)(functools.partial(copy, side, parity))


def near_kernel(
    own_here,
    own_there,
    across_here,
    across_there,
    around_here,
    around_there,
    thrust,
    first,
    second,
    third,
    start,
    stage_a,
    stage_b,
    viscosity,
    faces,
    beside,
):
    cells_x = own_here.shape[0]
    near = across_here.shape[0]
    _, _, tiles, rows, width = start.shape
    core = lax.axis_index("gy")

    def runs_of(side, parity):
        across, around = (across_here, across_there), (around_here, around_there)
        left, right = (around, across) if parity == 0 else (across, around)
        return (
            (0, *left, 0, near),
            (near, own_here, own_there, 0, cells_x),
            (near + cells_x, *right, 0, near),
        )

    place_columns(start, runs_of)
    stencil = Stencil(tiles, rows, width, viscosity, faces, thrust, start, beside)
    columns = start.shape[0]
    stencil.stage(0, start, stage_a, 2, columns - 4)
    stencil.stage(1, stage_a, stage_b, 4, columns - 8)
    first[...] = stage_a[pl.ds(2 + core * (columns - 8), 4)]
    second[...] = stage_b[pl.ds(4 + core * (columns - 12), 4)]
    stencil.stage(2, stage_b, stage_a, 6, columns - 12)
    third[...] = stage_a[pl.ds(6, columns - 12)]


def far_kernel(
    total_x,
    fringe,
    own_here,
    own_there,
    across_here,
    across_there,
    around_here,
    around_there,
    far_here,
    far_there,
    first,
    second,
    third,
    thrust,
    piece_here,
    piece_there,
    source,
    start,
    stage_a,
    stage_b,
    stage_c,
    viscosity,
    faces,
    beside,
    columns_here,
    columns_there,
):
    cells_x = own_here.shape[0]
    near, far = across_here.shape[0], far_here.shape[0]
    _, _, tiles, rows, width = start.shape
    half = width // 2
    share_x = cells_x // 2
    inner = share_x + 1
    core = lax.axis_index("gy")

    def runs_of(side, parity):
        across, around = (across_here, across_there), (around_here, around_there)
        if side == 0:
            return (
                (0, far_here, far_there, 0, far),
                (far, *(around if parity == 0 else across), 0, near),
                (far + near, own_here, own_there, 0, inner),
            )
        return (
            (0, own_here, own_there, cells_x - inner, inner),
            (inner, *(across if parity == 0 else around), 0, near),
            (inner + near, far_here, far_there, 0, far),
        )

    place_columns(start, runs_of)
    stencil = Stencil(tiles, rows, width, viscosity, faces, thrust, start, beside)
    stencil.stage(0, start, stage_a, 2 + 4 * core, 4)
    stage_a[pl.ds(6 - 4 * core, 4)] = first[...]
    stencil.stage(1, stage_a, stage_b, 4, 4)
    stage_b[pl.ds(8 - 8 * core, 4)] = second[...]
    stencil.stage(2, stage_b, stage_c, 6 - 4 * core, 4)
    stage_c[pl.ds(10 - 10 * core, 2)] = third[...]

    origin = REACH - core * (REACH - 1)
    pairs = 3 * tiles // 2
    for x in range(share_x):
        for c in range(3):
            for t in range(tiles):
                n = c * tiles + t
                field = stage_c[origin + x, c, t]
                low, high = field[:, :half], field[:, half:]
                spot = pl.ds((((n % 2) * share_x + x) * pairs + n // 2) * rows, rows)
                columns_here[spot, :] = jnp.where(core == 0, low, high)
                columns_there[spot, :] = jnp.where(core == 0, high, low)
    for s in range(rows):
        for m in range(pairs):
            spot = pl.ds(m * rows + s, 2 * share_x, stride=pairs * rows)
            piece_here[s, m] = columns_here[spot, :]
            piece_there[s, m] = columns_there[spot, :]

    is_farm = lax.axis_index("sec") == 1
    corner = lax.axis_index("gx") * cells_x + core * share_x

    def weight(offset, dest):
        place = lax.rem(corner + offset + total_x, total_x)
        inside = jnp.logical_and(place >= fringe[0], place < fringe[1])
        blend = jnp.where(inside, FRINGE_BLEND, 0.0)
        share = jnp.where(is_farm, 1.0 - blend, blend)
        if dest == 0:
            share = jnp.where(is_farm, 0.0, 1.0)
        return 0.5 * share

    for x in range(share_x):
        i = origin + x
        upright = [stage_c[i, 2, t] for t in range(tiles)]
        for t in range(tiles):
            cross = stage_c[i, 1, t]
            plane = (stencil.next_y(cross) - stencil.last_y(cross)) + (
                stencil.next_z(upright, t) - stencil.last_z(upright, t)
            )
            after, before = stage_c[i + 1, 0, t], stage_c[i - 1, 0, t]
            for dest in range(2):
                source[pl.ds(((dest * share_x + x) * tiles + t) * rows, rows), :] = (
                    weight(x + 1, dest) * after
                    - weight(x - 1, dest) * before
                    + weight(x, dest) * plane
                )


def spectra_kernel(source, table_y, table_z, spectra, modes):
    _, groups, _, parts, rows, lanes = spectra.shape
    levels = table_z.shape[0]
    count, total_y = source.shape
    columns = count // levels
    along_y = dot(source[...], table_y[...])
    beside = [along_y[n * levels : (n + 1) * levels] for n in range(columns)]
    both = dot(table_z[...], jnp.concatenate(beside, axis=1))
    for n in range(columns):
        for h in range(2):
            first = n * total_y + h * lanes
            modes[h, pl.ds(n * levels, levels), :] = both[:, first : first + lanes]
    for dest in range(2):
        for h in range(2):
            for p in range(parts):
                first = dest * count // 2 + p * groups
                picked = [
                    modes[h, pl.ds(first + b, rows, stride=levels // 2), :] for b in range(groups)
                ]
                for g, block in enumerate(swap_blocks(picked, lanes // groups)):
                    spectra[dest, g, h, p] = block


def arrange_kernel(piece_here, piece_there, *blocks):
    groups, pairs, rows, lanes = piece_here.shape
    half = rows // 2
    low = lax.broadcasted_iota(jnp.int32, (rows, lanes), 0) < half
    is_first = lax.axis_index("gy") == 0
    for distance, block in enumerate(blocks):
        g = lax.axis_index("gx") ^ distance
        for m in range(pairs):
            here, there = piece_here[g, m], piece_there[g, m]
            before = jnp.where(is_first, here, there)
            after = jnp.where(is_first, there, here)
            block[2 * m] = jnp.where(low, before, pltpu.roll(after, half, 0))
            block[2 * m + 1] = jnp.where(low, pltpu.roll(before, half, 0), after)


def pencil_kernel(received, waves, table, packed):
    _, groups, cores, parts, rows, lanes = received.shape
    total_x = groups * rows
    lane_width = lanes // groups
    wave, base = 2 * total_x, table.shape[1]
    spread_z = table[:base]
    pair_x = table[base : base + wave, :wave]
    table_x = table[base : base + total_x, wave : wave + total_x]
    along_x = table[base : base + total_x, 2 * wave : 2 * wave + lanes]
    along_zy = waves[lax.axis_index("gx"), lax.axis_index("gy")]
    spectrum = jnp.concatenate(
        [(received[0, :, :, p] + received[1, :, :, p]).reshape(-1, lanes) for p in range(parts)],
        axis=1,
    )
    solved = dot(pair_x, spectrum)
    pieces = []
    for a in range(2 * parts):
        p, side = a % parts, a // parts
        block = solved[side * total_x : (side + 1) * total_x, p * lanes : (p + 1) * lanes]
        pieces.append(block / (along_x + along_zy[a : a + 1]))
    field = dot(dot(table_x, jnp.concatenate(pieces, axis=1)), spread_z)
    levels_of = [field[:, a * lanes : (a + 1) * lanes] for a in range(2 * parts)]
    wide = lax.broadcasted_iota(jnp.int32, (total_x // 2, lanes), 1)
    left = wide < lanes // 2
    quarter = total_x // 4
    block = lax.broadcasted_iota(jnp.int32, (quarter, lanes), 1) // lane_width
    for g in range(groups):
        a, odd = divmod(g, 2)
        now = levels_of[a]
        front, rear = now[: total_x // 2], now[total_x // 2 :]
        if odd:
            main = jnp.where(left, pltpu.roll(front, lanes // 2, 1), rear)
            lower, lower_lane = now, lanes // 2 - lane_width
            upper, upper_lane = levels_of[min(a + 1, 2 * parts - 1)], 0
        else:
            main = jnp.where(left, front, pltpu.roll(rear, lanes // 2, 1))
            lower, lower_lane = levels_of[max(a - 1, 0)], lanes - lane_width
            upper, upper_lane = now, lanes // 2
        edge = None
        for q in range(4):
            for n, (whole, lane) in enumerate(((lower, lower_lane), (upper, upper_lane))):
                spot = 2 * q + n
                move = (spot * lane_width - lane) % lanes
                rolled = whole[q * quarter : (q + 1) * quarter]
                if move:
                    rolled = pltpu.roll(rolled, move, 1)
                edge = rolled if edge is None else jnp.where(block == spot, rolled, edge)
        packed[g, : total_x // 2] = main
        packed[g, total_x // 2 : 3 * quarter] = edge


def project_kernel(fringe, received, partner, table_y, moved, upstream, velocity_next, pressure):
    groups = received.shape[0]
    share, total_x, lanes = pressure.shape
    cells_x = total_x // groups
    width = lanes // groups
    place, core = lax.axis_index("gx"), lax.axis_index("gy")
    main_rows = total_x // 2
    rows = partner.shape[1]

    def levels_in(arrays):
        main = swap_blocks([arrays[s, :main_rows] for s in range(groups)], width)
        edge = swap_blocks([arrays[s, main_rows:rows] for s in range(groups)], width)
        inner = [jnp.concatenate([main[n], main[share + n]], axis=0) for n in range(share)]
        outer = [jnp.concatenate([edge[2 * q + n] for q in range(4)], axis=0) for n in range(2)]
        return [outer[0]] + inner + [outer[1]]

    here, there = levels_in(received), levels_in(partner)
    here, there = jnp.concatenate(here, axis=0), jnp.concatenate(there, axis=0)
    low = jnp.where(core == 0, here, there)
    high = jnp.where(core == 0, there, here)
    both = dot(jnp.concatenate([low, high], axis=1), table_y[core])
    fields = [both[n * total_x : (n + 1) * total_x] for n in range(share + 2)]
    values = [f[:, :lanes] for f in fields]
    values[0] = jnp.where(place == 0, values[1], values[0])
    values[-1] = jnp.where(place == groups - 1, -values[-2], values[-1])
    is_farm = lax.axis_index("sec") == 1
    outlet = upstream.shape[0]
    for z in range(share):
        now = values[z + 1]
        pressure[z] = now
        slopes = [
            0.5 * (pltpu.roll(now, total_x - 1, 0) - pltpu.roll(now, 1, 0)),
            fields[z + 1][:, lanes:],
            0.5 * (values[z + 2] - values[z]),
        ]
        for s in range(groups):
            distance = place ^ s
            columns = s * cells_x + lax.broadcasted_iota(jnp.int32, (cells_x, lanes), 0)
            inside = jnp.logical_and(columns >= fringe[0], columns < fringe[1])
            blend = jnp.where(jnp.logical_and(inside, is_farm), FRINGE_BLEND, 0.0)
            for c in range(3):
                own = moved[distance, c * share + z]
                if s >= groups - outlet:
                    own = own + blend * (upstream[s - groups + outlet, c * share + z] - own)
                spot = slice(s * cells_x, (s + 1) * cells_x)
                velocity_next[c, z, spot] = own - slopes[c][spot]


def cas(rows, columns, length):
    angle = (np.outer(rows, columns) % length) * (2.0 * np.pi / length)
    return np.cos(angle) + np.sin(angle)


def tables(levels, total_x, total_y, groups):
    half = total_y // 2
    lane_width = LANES // groups
    every_x = np.arange(total_x)
    every_y = np.arange(total_y)
    table_x = cas(every_x, every_x, total_x)
    table_y = cas(every_y, every_y, total_y)
    slope_y = 0.5 * (np.roll(table_y, -1, axis=1) - np.roll(table_y, 1, axis=1))
    level = np.arange(levels) + 0.5
    table_z = np.cos(np.outer(level, level) * (np.pi / levels))
    spread_z = np.kron(table_z, np.eye(lane_width))
    order = np.arange(levels).reshape(ROWS, levels // ROWS).T.reshape(levels)
    backward = [
        np.concatenate([table_y[:, here], slope_y[:, here]], axis=1)
        for here in (slice(0, half), slice(half, total_y))
    ]
    pair_x = np.einsum("kx,ab->akxb", table_x, np.eye(2)).reshape(2 * total_x, 2 * total_x)
    norm = levels / 2.0 * total_x * total_y
    wave_x = norm * (2.0 * np.cos(every_x * (2.0 * np.pi / total_x)) - 2.0)
    wave_y = norm * (2.0 * np.cos(every_y * (2.0 * np.pi / total_y)) - 2.0)
    wave_z = norm * (2.0 * np.cos(level * (np.pi / levels)) - 2.0)
    waves = wave_z.reshape(1, 1, -1, groups, 1) + wave_y.reshape(2, groups, 1, 1, lane_width)
    waves = waves.transpose(1, 0, 2, 3, 4).reshape(groups, 2, levels // groups, LANES)
    pencil = np.zeros((spread_z.shape[0] + 2 * total_x, spread_z.shape[1]))
    pencil[: spread_z.shape[0]] = spread_z
    pencil[spread_z.shape[0] :, : 2 * total_x] = pair_x
    pencil[spread_z.shape[0] : -total_x, 2 * total_x : 3 * total_x] = table_x
    pencil[spread_z.shape[0] : -total_x, 4 * total_x : 4 * total_x + LANES] = wave_x[:, None]
    return [
        jnp.asarray(t, jnp.float32)
        for t in (
            pencil,
            table_y,
            np.stack(backward),
            table_z[:, order],
            waves,
        )
    ]


def call(kernel, out_shapes, scratch, *operands):
    in_specs = [
        pl.BlockSpec(memory_space=pltpu.SMEM if o.dtype == jnp.int32 else pltpu.VMEM)
        for o in operands
    ]
    return pl.pallas_call(
        kernel,
        out_shape=out_shapes,
        in_specs=in_specs,
        out_specs=jax.tree.map(lambda _: pl.BlockSpec(memory_space=pltpu.VMEM), out_shapes),
        scratch_shapes=scratch,
        compiler_params=pltpu.CompilerParams(vmem_limit_bytes=VMEM_BYTES),
    )(*operands)


def thrust_weights(turbine_cells, along_x, along_y, along_z, total_y, strength):
    matches = (along_x[:, None] == turbine_cells[None, :, 0]).astype(jnp.bfloat16)
    offset_y = (along_y[None, :] - turbine_cells[:, 1:2] + total_y // 2) % total_y - total_y // 2
    offset_z = along_z[None, :] - turbine_cells[:, 2:3]
    distance = (
        offset_z[:, :, None] * offset_z[:, :, None] + offset_y[:, None, :] * offset_y[:, None, :]
    )
    inside = (distance <= RADIUS * RADIUS).astype(jnp.bfloat16)
    count = jnp.einsum("xt,tzy->xzy", matches, inside, preferred_element_type=jnp.float32)
    return strength * count


def paired_plan(velocity, turbine_cells, fringe_bounds):
    groups = lax.axis_size("gx")
    initial = velocity[0]
    _, levels, cells_x, cells_y = initial.shape
    total_x, total_y = cells_x * groups, 2 * cells_y
    share, share_x = levels // ROWS, cells_x // 2
    section, place, core = (lax.axis_index("sec"), lax.axis_index("gx"), lax.axis_index("gy"))
    pencil, table_y, backward, table_z, waves = tables(levels, total_x, total_y, groups)

    near, far = REACH - 4, 4
    up = [(i, (i + 1) % groups) for i in range(groups)]
    down = [(j, i) for i, j in up]
    swap = [(0, 1), (1, 0)]
    straight = [(2 * i, 2 * j) for i, j in up] + [(2 * j + 1, 2 * i + 1) for i, j in up]
    crossed = [(2 * i + 1, 2 * j) for i, j in up] + [(2 * j, 2 * i + 1) for i, j in up]
    own = jnp.transpose(initial.reshape(3, ROWS, share, cells_x, cells_y), (3, 0, 2, 1, 4))
    even = place % 2 == 0
    pairs_across = [(i, i ^ 1) for i in range(groups)]
    pairs_around = [(i, (i - 1 if i % 2 == 0 else i + 1) % groups) for i in range(groups)]
    upper = lax.dynamic_slice_in_dim(own, jnp.where(even, cells_x - near, 0), near, 0)
    lower = lax.dynamic_slice_in_dim(own, jnp.where(even, 0, cells_x - near), near, 0)
    around = lax.ppermute(lower, "gx", pairs_around)
    across = lax.ppermute(upper, "gx", pairs_across)
    tail, head = cells_x - REACH, near
    same = lax.dynamic_slice_in_dim(own, jnp.where(core == 0, tail, head), far, 0)
    other = lax.dynamic_slice_in_dim(own, jnp.where(core == 0, head, tail), far, 0)
    own_there = lax.ppermute(own, "gy", swap)
    other, across = lax.optimization_barrier((other, across))
    far_there = lax.ppermute(other, ("gx", "gy"), crossed)
    across_there = lax.ppermute(across, "gy", swap)
    around_there = lax.ppermute(around, "gy", swap)

    strength = 2.0 * THRUST_COEFF * section.astype(jnp.float32)
    along_z = jnp.arange(levels).reshape(ROWS, share).T.reshape(levels)

    def thrust_on(offset, count):
        along_x = (place * cells_x + offset + jnp.arange(count) + total_x) % total_x
        weights = thrust_weights(
            turbine_cells, along_x, jnp.arange(total_y), along_z, total_y, strength
        )
        return weights.reshape(count, share, ROWS, total_y)

    near_thrust = thrust_on(2 - near, cells_x + 2 * near - 4)
    far_thrust = thrust_on((2 - REACH) * (1 - core) + (share_x + 1) * core, far + near + share_x - 3)
    same, near_thrust, far_thrust = lax.optimization_barrier((same, near_thrust, far_thrust))
    far_here = lax.ppermute(same, ("gx", "gy"), straight)
    f32 = jnp.float32
    body = (3, share, ROWS, total_y)

    def columns(count):
        return pltpu.VMEM((count,) + body, f32)

    reached = cells_x + 2 * near
    shapes = [jax.ShapeDtypeStruct((n,) + body, f32) for n in (4, 4, reached - 12)]
    first, second, third = call(
        near_kernel,
        shapes,
        [columns(reached)] * 3
        + [pltpu.VMEM((reached,) + body[1:], f32), pltpu.VMEM(body, f32), columns(reached)],
        own,
        own_there,
        across,
        across_there,
        around,
        around_there,
        near_thrust,
    )
    window = far + near + share_x + 1
    pairs = 3 * share // 2
    piece = jax.ShapeDtypeStruct((ROWS, pairs, 2 * share_x, cells_y), f32)
    parts = levels // (2 * groups)
    piece_here, piece_send, source = call(
        functools.partial(far_kernel, total_x),
        [piece, piece, jax.ShapeDtypeStruct((2 * share_x * levels, total_y), f32)],
        [columns(window)] * 4
        + [
            pltpu.VMEM((window,) + body[1:], f32),
            pltpu.VMEM(body, f32),
            columns(window),
            pltpu.VMEM((share_x * 3 * levels, cells_y), f32),
            pltpu.VMEM((share_x * 3 * levels, cells_y), f32),
        ],
        fringe_bounds,
        own,
        own_there,
        across,
        across_there,
        around,
        around_there,
        far_here,
        far_there,
        first,
        second,
        third,
        far_thrust,
    )
    piece_there = lax.ppermute(piece_send, "gy", swap)
    spectra = call(
        spectra_kernel,
        jax.ShapeDtypeStruct((2, groups, 2, parts, 2 * share_x, LANES), f32),
        [pltpu.VMEM((2, 2 * share_x * levels, LANES), f32)],
        source,
        table_y,
        table_z,
    )
    received = lax.all_to_all(
        spectra.reshape((4 * groups,) + spectra.shape[3:]), ("sec", "gx", "gy"), 0, 0, tiled=True
    ).reshape(spectra.shape)
    blocks = call(
        arrange_kernel,
        [jax.ShapeDtypeStruct((3 * share, cells_x, cells_y), f32)] * groups,
        [],
        piece_here,
        piece_there,
    )
    moved = [blocks[0]] + [
        lax.ppermute(block, "gx", [(i, i ^ d) for i in range(groups)])
        for d, block in enumerate(blocks)
        if d
    ]
    packed = call(
        pencil_kernel,
        jax.ShapeDtypeStruct((groups, 3 * total_x // 4, LANES), f32),
        [],
        received,
        waves,
        pencil,
    )
    packed, *moved = lax.optimization_barrier([packed] + moved)
    moved = jnp.stack(moved)
    outlet = groups // 4
    leaving = jnp.stack(
        [
            lax.dynamic_index_in_dim(moved, place ^ s, 0, keepdims=False)
            for s in range(groups - outlet, groups)
        ]
    )
    upstream = lax.ppermute(leaving, "sec", [(0, 1)])
    returned = lax.all_to_all(packed, "gx", 0, 0, tiled=True)
    returned, upstream = lax.optimization_barrier((returned, upstream))
    partner = lax.ppermute(returned, "gy", swap)
    velocity_next, pressure = call(
        project_kernel,
        [
            jax.ShapeDtypeStruct((3, share, total_x, cells_y), f32),
            jax.ShapeDtypeStruct((share, total_x, cells_y), f32),
        ],
        [],
        fringe_bounds,
        returned,
        partner,
        backward,
        moved,
        upstream,
    )
    return (velocity_next[None], pressure[None])


def on_device(velocity, turbine_cells, fringe_bounds):
    groups = lax.axis_size("gx")
    _, _, levels, cells_x, cells_y = velocity.shape
    paired = (
        lax.axis_size("gy") == 2
        and lax.axis_size("sec") == 2
        and cells_y == LANES
        and cells_x == ROWS
        and groups == ROWS
        and 2 * levels == groups * groups
    )
    plan = paired_plan if paired else general_plan
    return plan(velocity, turbine_cells, fringe_bounds)


def solution(mesh):
    return jax.shard_map(
        on_device,
        mesh=mesh,
        in_specs=(P("sec", None, None, "gx", "gy"), P(), P()),
        out_specs=(P("sec", None, "gx", None, "gy"), P("sec", "gx", None, "gy")),
        check_vma=False,
    )
```

```python
import functools

import jax
import jax.numpy as jnp
import numpy as np
from jax import lax
from jax.experimental import pallas as pl
from jax.experimental.pallas import tpu as pltpu
from jax.sharding import PartitionSpec as P

RADIUS = 4


TIME_STEP = 0.05
SMAG_COEFF = 0.1
THRUST_COEFF = 4.0
DRIVING_FORCE = 0.1
FRINGE_BLEND = 0.5
HIGHEST = lax.Precision.HIGHEST
STAGES = 3
REACH = 2 * STAGES + 1
LANES = 128
SMALLEST = float(np.finfo(np.float32).tiny)
ROWS = 8
VMEM_BYTES = 20 * 1024 * 1024


def extended(x, sides, width):
    for axis, dim in sides:
        count, length = (lax.axis_size(axis), x.shape[dim])
        up = [(i, (i + 1) % count) for i in range(count)]
        down = [(j, i) for i, j in up]
        last = lax.slice_in_dim(x, length - width, length, axis=dim)
        initial = lax.slice_in_dim(x, 0, width, axis=dim)
        before = lax.ppermute(last, axis, up)
        after = lax.ppermute(initial, axis, down)
        x = jnp.concatenate([before, x, after], axis=dim)
    return x


def shifted(block, axis, distance):
    devices = range(lax.axis_size(axis))
    route = [(i - distance, i) for i in devices if i - distance in devices]
    return lax.ppermute(block, axis, route)


def cas_table(row_index, column_index, length):
    product = row_index[:, None] * column_index[None, :] % length
    angle = product.astype(jnp.float32) * (2.0 * jnp.pi / length)
    return jnp.cos(angle) + jnp.sin(angle)


def shift_up(values):
    zeros = jnp.zeros_like(values[..., :1, :, :])
    return jnp.concatenate([values[..., 1:, :, :], zeros], axis=-3)


def shift_down(values):
    zeros = jnp.zeros_like(values[..., :1, :, :])
    return jnp.concatenate([zeros, values[..., :-1, :, :]], axis=-3)


def thomas(right_side, eigen_value):
    length = right_side.shape[0]
    inverses = []
    reduced = []
    for level_index in range(length):
        if level_index == 0:
            diagonal = eigen_value - 1.0
        elif level_index == length - 1:
            diagonal = eigen_value - 3.0
        else:
            diagonal = eigen_value - 2.0
        if level_index == 0:
            pivot_now = diagonal
            current = right_side[0] / pivot_now
        else:
            pivot_now = diagonal - inverses[-1]
            current = (right_side[level_index] - reduced[-1]) / pivot_now
        inverses.append(1.0 / pivot_now)
        reduced.append(current)
    solution = [reduced[-1]]
    for level_index in range(length - 2, -1, -1):
        solution.append(reduced[level_index] - inverses[level_index] * solution[-1])
    return jnp.stack(solution[::-1])


def spanwise_derivative(values, sine_y):
    return -sine_y * jnp.roll(jnp.flip(values, axis=-1), 1, axis=-1)


def widened(values):
    return extended(values, (("gx", 1), ("gy", 2)), 1)


def disk_weights(turbine_cells, along_x, along_y, along_z, total_y):
    matches = (along_x[:, None] == turbine_cells[None, :, 0]).astype(jnp.float32)
    offset_y = (along_y[None, :] - turbine_cells[:, 1:2] + total_y // 2) % total_y - total_y // 2
    offset_z = along_z[None, :] - turbine_cells[:, 2:3]
    distance = (
        offset_z[:, :, None] * offset_z[:, :, None] + offset_y[:, None, :] * offset_y[:, None, :]
    )
    inside = (distance <= RADIUS * RADIUS).astype(jnp.float32)
    return jnp.einsum("xt,tzy->zxy", matches, inside, precision=HIGHEST)


def tendency(velocity_now, farm_flag, disk_weight):
    levels, cells_x, cells_y = (velocity_now.shape[1], velocity_now.shape[2], velocity_now.shape[3])
    border = widened(velocity_now.reshape(3 * levels, cells_x, cells_y)).reshape(
        3, levels, cells_x + 2, cells_y + 2
    )
    plus_x = border[:, :, 2:, 1:-1]
    minus_x = border[:, :, :-2, 1:-1]
    plus_y = border[:, :, 1:-1, 2:]
    minus_y = border[:, :, 1:-1, :-2]
    plus_z = shift_up(velocity_now)
    minus_z = shift_down(velocity_now)
    gradients = [0.5 * (plus_x - minus_x), 0.5 * (plus_y - minus_y), 0.5 * (plus_z - minus_z)]
    strain_squares = jnp.zeros_like(velocity_now[0])
    for component in range(3):
        strain_squares = (
            strain_squares + gradients[component][component] * gradients[component][component]
        )
        for direction in range(component + 1, 3):
            shear = 0.5 * (gradients[direction][component] + gradients[component][direction])
            strain_squares = strain_squares + 2.0 * shear * shear
    viscosity = SMAG_COEFF * jnp.sqrt(2.0 * strain_squares)
    visc_border = widened(viscosity)
    visc_plus_x = visc_border[:, 2:, 1:-1]
    visc_minus_x = visc_border[:, :-2, 1:-1]
    visc_plus_y = visc_border[:, 1:-1, 2:]
    visc_minus_y = visc_border[:, 1:-1, :-2]
    visc_plus_z = shift_up(viscosity)
    visc_minus_z = shift_down(viscosity)
    advection = 0.5 * (plus_x[0] * plus_x - minus_x[0] * minus_x)
    advection = advection + 0.5 * (plus_y[1] * plus_y - minus_y[1] * minus_y)
    advection = advection + 0.5 * (plus_z[2] * plus_z - minus_z[2] * minus_z)
    diffusion = 0.5 * (viscosity + visc_plus_x) * (plus_x - velocity_now) - 0.5 * (
        viscosity + visc_minus_x
    ) * (velocity_now - minus_x)
    diffusion = (
        diffusion
        + 0.5 * (viscosity + visc_plus_y) * (plus_y - velocity_now)
        - 0.5 * (viscosity + visc_minus_y) * (velocity_now - minus_y)
    )
    diffusion = (
        diffusion
        + 0.5 * (viscosity + visc_plus_z) * (plus_z - velocity_now)
        - 0.5 * (viscosity + visc_minus_z) * (velocity_now - minus_z)
    )
    changes = diffusion - advection
    streamwise = DRIVING_FORCE - THRUST_COEFF * farm_flag * disk_weight * velocity_now[0] * jnp.abs(
        velocity_now[0]
    )
    return jnp.concatenate([changes[:1] + streamwise[None], changes[1:]], axis=0)


def general_plan(velocity, turbine_cells, fringe_bounds):
    initial = velocity[0]
    levels, cells_x, cells_y = (initial.shape[1], initial.shape[2], initial.shape[3])
    total_y = cells_y * lax.axis_size("gy")
    x_anchor = lax.axis_index("gx") * cells_x
    y_anchor = lax.axis_index("gy") * cells_y
    farm_flag = lax.axis_index("sec").astype(jnp.float32)
    along_x = x_anchor + jnp.arange(cells_x, dtype=jnp.int32)
    along_y = y_anchor + jnp.arange(cells_y, dtype=jnp.int32)
    along_z = jnp.arange(levels, dtype=jnp.int32)
    disk_weight = disk_weights(turbine_cells, along_x, along_y, along_z, total_y)
    segment_one = initial + TIME_STEP * tendency(initial, farm_flag, disk_weight)
    segment_two = 0.75 * initial + 0.25 * (
        segment_one + TIME_STEP * tendency(segment_one, farm_flag, disk_weight)
    )
    segment_three = initial / 3.0 + 2.0 / 3.0 * (
        segment_two + TIME_STEP * tendency(segment_two, farm_flag, disk_weight)
    )
    regrouped = lax.all_to_all(segment_three, "gx", split_axis=1, concat_axis=2, tiled=True)
    count_x = regrouped.shape[2]
    quarter = count_x // 4
    cut_at = count_x - quarter
    outlet_part = regrouped[:, :, cut_at:, :]
    upstream = shifted(outlet_part, "sec", 1)
    columns = cut_at + jnp.arange(quarter, dtype=jnp.int32)
    inside = ((columns >= fringe_bounds[0]) & (columns < fringe_bounds[1])).astype(jnp.float32)
    weight = FRINGE_BLEND * farm_flag * inside
    blended_part = outlet_part + weight[:, None] * (upstream - outlet_part)
    regrouped = jnp.concatenate([regrouped[:, :, :cut_at, :], blended_part], axis=2)
    index_x = jnp.arange(count_x, dtype=jnp.int32)
    table_x = cas_table(index_x, index_x, count_x)
    gradient_u = 0.5 * (jnp.roll(regrouped[0], -1, axis=1) - jnp.roll(regrouped[0], 1, axis=1))
    fields = jnp.stack([gradient_u, regrouped[1], regrouped[2]])
    spectral_x = jnp.einsum("kx,czxy->czky", table_x, fields, precision=HIGHEST)
    columns_view = lax.all_to_all(
        lax.all_to_all(spectral_x, "gx", split_axis=2, concat_axis=1, tiled=True),
        "gy",
        split_axis=2,
        concat_axis=3,
        tiled=True,
    )
    slice_width = columns_view.shape[2]
    count_y = columns_view.shape[3]
    index_y = jnp.arange(count_y, dtype=jnp.int32)
    table_y = cas_table(index_y, index_y, count_y)
    spectrum = jnp.einsum("ly,czky->czkl", table_y, columns_view, precision=HIGHEST)
    sine_y = jnp.sin(index_y.astype(jnp.float32) * (2.0 * jnp.pi / count_y))
    source = (
        spectrum[0]
        + spanwise_derivative(spectrum[1], sine_y)
        + 0.5 * (shift_up(spectrum[2]) - shift_down(spectrum[2]))
    )
    wave_x = (
        lax.axis_index("gx") * cells_x
        + lax.axis_index("gy") * slice_width
        + jnp.arange(slice_width, dtype=jnp.int32)
    )
    eigen_value = 2.0 * jnp.cos(wave_x.astype(jnp.float32) * (2.0 * jnp.pi / count_x))[:, None]
    eigen_value = (
        eigen_value
        + 2.0 * jnp.cos(index_y.astype(jnp.float32) * (2.0 * jnp.pi / count_y))[None, :]
        - 4.0
    )
    solved = thomas(source, eigen_value)
    above_level = jnp.concatenate([solved[1:], -solved[-1:]], axis=0)
    below_level = jnp.concatenate([solved[:1], solved[:-1]], axis=0)
    coefficients = jnp.stack(
        [solved, spanwise_derivative(solved, sine_y), 0.5 * (above_level - below_level)]
    )
    physical_y = jnp.einsum("yl,czkl->czky", table_y, coefficients, precision=HIGHEST) * (
        1.0 / count_y
    )
    returned = lax.all_to_all(
        lax.all_to_all(physical_y, "gx", split_axis=1, concat_axis=2, tiled=True),
        "gy",
        split_axis=3,
        concat_axis=2,
        tiled=True,
    )
    group_size = count_x // lax.axis_size("gy")
    wave_back = (
        index_x // slice_width % lax.axis_size("gx") * cells_x
        + index_x // group_size * slice_width
        + index_x % slice_width
    )
    inverse_table = cas_table(index_x, wave_back, count_x)
    physical = jnp.einsum("xp,czpy->czxy", inverse_table, returned, precision=HIGHEST) * (
        1.0 / count_x
    )
    pressure = physical[0]
    gradient_p = 0.5 * (jnp.roll(pressure, -1, axis=1) - jnp.roll(pressure, 1, axis=1))
    velocity_next = regrouped - jnp.stack([gradient_p, physical[1], physical[2]])
    return (velocity_next[None], pressure[None])


def split(values):
    high = values.astype(jnp.bfloat16)
    low = values - high.astype(jnp.float32)
    return high, low.astype(jnp.bfloat16)


def dot(left, right):
    (a, da), (b, db) = split(left), split(right)

    def product(x, y):
        return jnp.dot(x, y, preferred_element_type=jnp.float32)

    return product(a, b) + (product(a, db) + product(da, b))


def swap_blocks(arrays, width):
    arrays = list(arrays)
    block = lax.broadcasted_iota(jnp.int32, arrays[0].shape, 1) // width
    step = 1
    while step < len(arrays):
        low = (block // step) % 2 == 0
        for index in range(len(arrays)):
            if (index // step) % 2 == 0:
                first, second = arrays[index], arrays[index + step]
                arrays[index] = jnp.where(low, first, pltpu.roll(second, step * width, 1))
                arrays[index + step] = jnp.where(
                    low, pltpu.roll(first, LANES - step * width, 1), second
                )
        step *= 2
    return arrays


def reordered(values, order):
    one = order.astype(jnp.bfloat16)
    high, rest = split(values)
    low = values - high.astype(jnp.float32) - rest.astype(jnp.float32)

    def product(x):
        return jnp.dot(x, one, preferred_element_type=jnp.float32)

    return (product(high) + product(rest)) + product(low.astype(jnp.bfloat16))


def parting(lanes, inverse=False):
    line = lax.broadcasted_iota(jnp.int32, (lanes, lanes), 1 if inverse else 0)
    spot = lax.broadcasted_iota(jnp.int32, (lanes, lanes), 0 if inverse else 1)
    later = jnp.where(spot >= lanes // 2, 1, 0)
    place = 2 * (spot - later * (lanes // 2)) + (later ^ lax.axis_index("gy"))
    return jnp.where(line == place, 1.0, 0.0)


def packed_columns(initial, columns, cells_x, tiles):
    total, lanes = initial.shape
    levels = total // (3 * cells_x)
    rows = levels // tiles
    picked = [
        initial[pl.ds((c * levels + t) * cells_x + x, rows, stride=tiles * cells_x), :]
        for x in columns
        for c in range(3)
        for t in range(tiles)
    ]
    values = reordered(jnp.concatenate(picked, axis=0), parting(lanes))
    return values.reshape(len(columns), 3, tiles, rows, lanes)


def pack_near_kernel(cells_x, initial, lower, upper):
    near, _, tiles, _, _ = lower.shape
    columns = list(range(near)) + list(range(cells_x - near, cells_x))
    values = packed_columns(initial, columns, cells_x, tiles)
    even = lax.axis_index("gx") % 2 == 0

    @pl.when(even)
    def _():
        lower[...] = values[:near]
        upper[...] = values[near:]

    @pl.when(jnp.logical_not(even))
    def _():
        lower[...] = values[near:]
        upper[...] = values[:near]


def pack_kernel(initial, own, same, other):
    cells_x, _, tiles, _, _ = own.shape
    far = same.shape[0]
    tail, head = cells_x - REACH, REACH - far
    values = packed_columns(initial, list(range(cells_x)), cells_x, tiles)
    own[...] = values
    is_first = lax.axis_index("gy") == 0

    @pl.when(is_first)
    def _():
        same[...] = values[tail : tail + far]
        other[...] = values[head : head + far]

    @pl.when(jnp.logical_not(is_first))
    def _():
        same[...] = values[head : head + far]
        other[...] = values[tail : tail + far]


class Stencil:
    def __init__(self, tiles, rows, width, viscosity, faces, thrust, start, beside):
        self.tiles, self.rows, self.width, self.beside = (tiles, rows, width, beside)
        self.viscosity, self.faces, self.thrust, self.start = (viscosity, faces, thrust, start)
        row = lax.broadcasted_iota(jnp.int32, (rows, width), 0)
        self.top = row == rows - 1
        self.bottom = row == 0

    def next_y(self, f):
        half = self.width // 2
        return jnp.concatenate([f[:, half:], pltpu.roll(f[:, :half], half - 1, 1)], axis=1)

    def last_y(self, f):
        half = self.width // 2
        return jnp.concatenate([pltpu.roll(f[:, half:], 1, 1), f[:, :half]], axis=1)

    def next_z(self, parts, t):
        if t < self.tiles - 1:
            return parts[t + 1]
        return jnp.where(self.top, 0.0, pltpu.roll(parts[0], self.rows - 1, 0))

    def last_z(self, parts, t):
        if t > 0:
            return parts[t - 1]
        return jnp.where(self.bottom, 0.0, pltpu.roll(parts[self.tiles - 1], 1, 0))

    def set_viscosity(self, now, first, count):
        tiles = self.tiles

        def column(n, carry):
            i = first + n
            here = [[now[i, c, t] for t in range(tiles)] for c in range(3)]
            found, sides = [], []
            for t in range(tiles):
                d_x = [now[i + 1, c, t] - now[i - 1, c, t] for c in range(3)]
                after_y = [self.next_y(f[t]) for f in here]
                sides.append(after_y)
                d_y = [a - self.last_y(f[t]) for a, f in zip(after_y, here)]
                d_z = [self.next_z(f, t) - self.last_z(f, t) for f in here]
                diagonal = d_x[0] * d_x[0] + d_y[1] * d_y[1] + d_z[2] * d_z[2]
                xy = d_x[1] + d_y[0]
                xz = d_x[2] + d_z[0]
                yz = d_y[2] + d_z[1]
                total = (diagonal + diagonal) + (xy * xy + xz * xz + yz * yz)
                root = total * lax.rsqrt(jnp.maximum(total, SMALLEST))
                found.append((0.5 * SMAG_COEFF) * root)
            for t in range(tiles):
                self.viscosity[i, t] = found[t]
                for c in range(3):
                    self.beside[i, c, t] = sides[t][c]
            return carry

        lax.fori_loop(0, count, column, 0, unroll=4 if count % 4 == 0 else 6)

    def face(self, both, here, after, lead):
        low = both + here[lead]
        high = both - after[lead]
        return [after[c] * high - here[c] * low for c in range(3)]

    def face_x(self, now, i, t):
        here = [now[i, c, t] for c in range(3)]
        after = [now[i + 1, c, t] for c in range(3)]
        return self.face(self.viscosity[i, t] + self.viscosity[i + 1, t], here, after, 0)

    def advance(self, now, then, first, count, keep, gain):
        tiles, scale = self.tiles, 0.5 * TIME_STEP * gain
        for t in range(tiles):
            for c, f in enumerate(self.face_x(now, first - 1, t)):
                self.faces[c, t] = f

        def column(n, carry):
            i = first + n
            eddy = [self.viscosity[i, t] for t in range(tiles)]
            field = [[now[i, c, t] for t in range(tiles)] for c in range(3)]

            def face_z(t):
                here = [f[t] for f in field]
                after = [self.next_z(f, t) for f in field]
                return self.face(eddy[t] + self.next_z(eddy, t), here, after, 2)

            last = face_z(tiles - 1)
            floor = eddy[0] - field[2][0]
            below = [
                jnp.where(self.bottom, field[c][0] * floor, pltpu.roll(last[c], 1, 0))
                for c in range(3)
            ]
            ahead_of = [self.face_x(now, i, t) for t in range(tiles)]
            before_of = [[self.faces[c, t] for c in range(3)] for t in range(tiles)]
            found = []
            for t in range(tiles):
                here = [f[t] for f in field]
                above = last if t == tiles - 1 else face_z(t)
                ahead, before = ahead_of[t], before_of[t]
                beside = [self.beside[i, c, t] for c in range(3)]
                side = self.face(eddy[t] + self.next_y(eddy[t]), here, beside, 1)
                for c in range(3):
                    change = (
                        (ahead[c] - before[c])
                        + (side[c] - self.last_y(side[c]))
                        + (above[c] - below[c])
                    )
                    if c == 0:
                        drag = self.thrust[i - 2, t] * here[0] * jnp.abs(here[0])
                        change = change + (2.0 * DRIVING_FORCE - drag)
                    if keep == 0.0:
                        found.append(here[c] + scale * change)
                    else:
                        found.append(keep * self.start[i, c, t] + gain * here[c] + scale * change)
                below = above
            for t in range(tiles):
                for c in range(3):
                    then[i, c, t] = found[3 * t + c]
                    self.faces[c, t] = ahead_of[t][c]
            return carry

        lax.fori_loop(0, count, column, 0, unroll=2)

    def stage(self, number, now, then, first, count):
        keep, gain = ((0.0, 1.0), (0.75, 0.25), (1.0 / 3.0, 2.0 / 3.0))[number]
        self.set_viscosity(now, first - 1, count + 2)
        self.advance(now, then, first, count, keep, gain)


def place_columns(start, runs_of):
    half = start.shape[-1] // 2
    front = lax.broadcasted_iota(jnp.int32, start.shape[-2:-1] + (half,), 1) < half // 2
    core = lax.axis_index("gy")
    odd = lax.axis_index("gx") % 2

    def copy(side, parity):
        for first, here, there, begin, count in runs_of(side, parity):
            low, high = (here, there) if side == 0 else (there, here)
            for n in range(count):
                for c in range(start.shape[1]):
                    for t in range(start.shape[2]):
                        a, b = low[begin + n, c, t], high[begin + n, c, t]
                        start[first + n, c, t, :, :half] = jnp.where(front, a, b)
                        start[first + n, c, t, :, half:] = pltpu.roll(
                            jnp.where(front, b, a), half // 2, 1
                        )

    for side in range(2):
        for parity in range(2):
            chosen = jnp.logical_and(core == side, odd == parity)
            pl.when(chosen)(functools.partial(copy, side, parity))


def near_kernel(
    own_here,
    own_there,
    across_here,
    across_there,
    around_here,
    around_there,
    thrust,
    first,
    second,
    third,
    start,
    stage_a,
    stage_b,
    viscosity,
    faces,
    beside,
):
    cells_x = own_here.shape[0]
    near = across_here.shape[0]
    _, _, tiles, rows, width = start.shape
    core = lax.axis_index("gy")

    def runs_of(side, parity):
        across, around = (across_here, across_there), (around_here, around_there)
        left, right = (around, across) if parity == 0 else (across, around)
        return (
            (0, *left, 0, near),
            (near, own_here, own_there, 0, cells_x),
            (near + cells_x, *right, 0, near),
        )

    place_columns(start, runs_of)
    stencil = Stencil(tiles, rows, width, viscosity, faces, thrust, start, beside)
    columns = start.shape[0]
    stencil.stage(0, start, stage_a, 2, columns - 4)
    stencil.stage(1, stage_a, stage_b, 4, columns - 8)
    first[...] = stage_a[pl.ds(2 + core * (columns - 8), 4)]
    second[...] = stage_b[pl.ds(4 + core * (columns - 12), 4)]
    stencil.stage(2, stage_b, stage_a, 6, columns - 12)
    third[...] = stage_a[pl.ds(6, columns - 12)]


def far_kernel(
    total_x,
    fringe,
    own_here,
    own_there,
    across_here,
    across_there,
    around_here,
    around_there,
    far_here,
    far_there,
    first,
    second,
    third,
    thrust,
    piece_here,
    piece_there,
    source,
    start,
    stage_a,
    stage_b,
    stage_c,
    viscosity,
    faces,
    beside,
    columns_here,
    columns_there,
):
    cells_x = own_here.shape[0]
    near, far = across_here.shape[0], far_here.shape[0]
    _, _, tiles, rows, width = start.shape
    half = width // 2
    share_x = cells_x // 2
    inner = share_x + 1
    core = lax.axis_index("gy")

    def runs_of(side, parity):
        across, around = (across_here, across_there), (around_here, around_there)
        if side == 0:
            return (
                (0, far_here, far_there, 0, far),
                (far, *(around if parity == 0 else across), 0, near),
                (far + near, own_here, own_there, 0, inner),
            )
        return (
            (0, own_here, own_there, cells_x - inner, inner),
            (inner, *(across if parity == 0 else around), 0, near),
            (inner + near, far_here, far_there, 0, far),
        )

    place_columns(start, runs_of)
    stencil = Stencil(tiles, rows, width, viscosity, faces, thrust, start, beside)
    stencil.stage(0, start, stage_a, 2 + 4 * core, 4)
    stage_a[pl.ds(6 - 4 * core, 4)] = first[...]
    stencil.stage(1, stage_a, stage_b, 4, 4)
    stage_b[pl.ds(8 - 8 * core, 4)] = second[...]
    stencil.stage(2, stage_b, stage_c, 6 - 4 * core, 4)
    stage_c[pl.ds(10 - 10 * core, 2)] = third[...]

    origin = REACH - core * (REACH - 1)
    pairs = 3 * tiles // 2
    front = lax.broadcasted_iota(jnp.int32, (rows, half), 1) < half // 2
    for x in range(share_x):
        for c in range(3):
            for t in range(tiles):
                n = c * tiles + t
                field = stage_c[origin + x, c, t]
                even, odd = field[:, :half], pltpu.roll(field[:, half:], half // 2, 1)
                low, high = jnp.where(front, even, odd), jnp.where(front, odd, even)
                spot = pl.ds((((n % 2) * share_x + x) * pairs + n // 2) * rows, rows)
                columns_here[spot, :] = jnp.where(core == 0, low, high)
                columns_there[spot, :] = jnp.where(core == 0, high, low)
    for s in range(rows):
        for m in range(pairs):
            spot = pl.ds(m * rows + s, 2 * share_x, stride=pairs * rows)
            piece_here[s, m] = columns_here[spot, :]
            piece_there[s, m] = columns_there[spot, :]

    is_farm = lax.axis_index("sec") == 1
    corner = lax.axis_index("gx") * cells_x + core * share_x

    def weight(offset, dest):
        place = lax.rem(corner + offset + total_x, total_x)
        inside = jnp.logical_and(place >= fringe[0], place < fringe[1])
        blend = jnp.where(inside, FRINGE_BLEND, 0.0)
        share = jnp.where(is_farm, 1.0 - blend, blend)
        if dest == 0:
            share = jnp.where(is_farm, 0.0, 1.0)
        return 0.5 * share

    for x in range(share_x):
        i = origin + x
        upright = [stage_c[i, 2, t] for t in range(tiles)]
        for t in range(tiles):
            cross = stage_c[i, 1, t]
            plane = (stencil.next_y(cross) - stencil.last_y(cross)) + (
                stencil.next_z(upright, t) - stencil.last_z(upright, t)
            )
            after, before = stage_c[i + 1, 0, t], stage_c[i - 1, 0, t]
            for dest in range(2):
                source[pl.ds(((dest * share_x + x) * tiles + t) * rows, rows), :] = (
                    weight(x + 1, dest) * after
                    - weight(x - 1, dest) * before
                    + weight(x, dest) * plane
                )


def spectra_kernel(source, table_y, table_z, spectra, modes):
    _, groups, _, parts, rows, lanes = spectra.shape
    levels = table_z.shape[0]
    count, total_y = source.shape
    columns = count // levels
    along_y = dot(source[...], table_y[...])
    beside = [along_y[n * levels : (n + 1) * levels] for n in range(columns)]
    both = dot(table_z[...], jnp.concatenate(beside, axis=1))
    for n in range(columns):
        for h in range(2):
            first = n * total_y + h * lanes
            modes[h, pl.ds(n * levels, levels), :] = both[:, first : first + lanes]
    for dest in range(2):
        for h in range(2):
            for p in range(parts):
                first = dest * count // 2 + p * groups
                picked = [
                    modes[h, pl.ds(first + b, rows, stride=levels // 2), :] for b in range(groups)
                ]
                for g, block in enumerate(swap_blocks(picked, lanes // groups)):
                    spectra[dest, g, h, p] = block


def arrange_kernel(piece_here, piece_there, *blocks):
    groups, pairs, rows, lanes = piece_here.shape
    half = rows // 2
    low = lax.broadcasted_iota(jnp.int32, (rows, lanes), 0) < half
    is_first = lax.axis_index("gy") == 0
    order = parting(lanes, inverse=True)
    for distance, block in enumerate(blocks):
        g = lax.axis_index("gx") ^ distance
        merged = []
        for m in range(pairs):
            here, there = piece_here[g, m], piece_there[g, m]
            before = jnp.where(is_first, here, there)
            after = jnp.where(is_first, there, here)
            merged.append(jnp.where(low, before, pltpu.roll(after, half, 0)))
            merged.append(jnp.where(low, pltpu.roll(before, half, 0), after))
        values = reordered(jnp.concatenate(merged, axis=0), order)
        block[...] = values.reshape(block.shape)


def pencil_kernel(received, waves, table, packed):
    _, groups, cores, parts, rows, lanes = received.shape
    total_x = groups * rows
    lane_width = lanes // groups
    wave, base = 2 * total_x, table.shape[1]
    spread_z = table[:base]
    pair_x = table[base : base + wave, :wave]
    table_x = table[base : base + total_x, wave : wave + total_x]
    along_x = table[base : base + total_x, 2 * wave : 2 * wave + lanes]
    along_zy = waves[lax.axis_index("gx"), lax.axis_index("gy")]
    spectrum = jnp.concatenate(
        [(received[0, :, :, p] + received[1, :, :, p]).reshape(-1, lanes) for p in range(parts)],
        axis=1,
    )
    solved = dot(pair_x, spectrum)
    pieces = []
    for a in range(2 * parts):
        p, side = a % parts, a // parts
        block = solved[side * total_x : (side + 1) * total_x, p * lanes : (p + 1) * lanes]
        pieces.append(block / (along_x + along_zy[a : a + 1]))
    field = dot(dot(table_x, jnp.concatenate(pieces, axis=1)), spread_z)
    levels_of = [field[:, a * lanes : (a + 1) * lanes] for a in range(2 * parts)]
    wide = lax.broadcasted_iota(jnp.int32, (total_x // 2, lanes), 1)
    left = wide < lanes // 2
    quarter = total_x // 4
    block = lax.broadcasted_iota(jnp.int32, (quarter, lanes), 1) // lane_width
    for g in range(groups):
        a, odd = divmod(g, 2)
        now = levels_of[a]
        front, rear = now[: total_x // 2], now[total_x // 2 :]
        if odd:
            main = jnp.where(left, pltpu.roll(front, lanes // 2, 1), rear)
            lower, lower_lane = now, lanes // 2 - lane_width
            upper, upper_lane = levels_of[min(a + 1, 2 * parts - 1)], 0
        else:
            main = jnp.where(left, front, pltpu.roll(rear, lanes // 2, 1))
            lower, lower_lane = levels_of[max(a - 1, 0)], lanes - lane_width
            upper, upper_lane = now, lanes // 2
        edge = None
        for q in range(4):
            for n, (whole, lane) in enumerate(((lower, lower_lane), (upper, upper_lane))):
                spot = 2 * q + n
                move = (spot * lane_width - lane) % lanes
                rolled = whole[q * quarter : (q + 1) * quarter]
                if move:
                    rolled = pltpu.roll(rolled, move, 1)
                edge = rolled if edge is None else jnp.where(block == spot, rolled, edge)
        packed[g, : total_x // 2] = main
        packed[g, total_x // 2 : 3 * quarter] = edge


def project_kernel(fringe, received, partner, table_y, moved, upstream, velocity_next, pressure):
    groups = received.shape[0]
    share, total_x, lanes = pressure.shape
    cells_x = total_x // groups
    width = lanes // groups
    place, core = lax.axis_index("gx"), lax.axis_index("gy")
    main_rows = total_x // 2
    rows = partner.shape[1]

    def levels_in(arrays):
        main = swap_blocks([arrays[s, :main_rows] for s in range(groups)], width)
        edge = swap_blocks([arrays[s, main_rows:rows] for s in range(groups)], width)
        inner = [jnp.concatenate([main[n], main[share + n]], axis=0) for n in range(share)]
        outer = [jnp.concatenate([edge[2 * q + n] for q in range(4)], axis=0) for n in range(2)]
        return [outer[0]] + inner + [outer[1]]

    here, there = levels_in(received), levels_in(partner)
    here, there = jnp.concatenate(here, axis=0), jnp.concatenate(there, axis=0)
    low = jnp.where(core == 0, here, there)
    high = jnp.where(core == 0, there, here)
    both = dot(jnp.concatenate([low, high], axis=1), table_y[core])
    fields = [both[n * total_x : (n + 1) * total_x] for n in range(share + 2)]
    values = [f[:, :lanes] for f in fields]
    values[0] = jnp.where(place == 0, values[1], values[0])
    values[-1] = jnp.where(place == groups - 1, -values[-2], values[-1])
    is_farm = lax.axis_index("sec") == 1
    outlet = upstream.shape[0]
    for z in range(share):
        now = values[z + 1]
        pressure[z] = now
        slopes = [
            0.5 * (pltpu.roll(now, total_x - 1, 0) - pltpu.roll(now, 1, 0)),
            fields[z + 1][:, lanes:],
            0.5 * (values[z + 2] - values[z]),
        ]
        for s in range(groups):
            distance = place ^ s
            columns = s * cells_x + lax.broadcasted_iota(jnp.int32, (cells_x, lanes), 0)
            inside = jnp.logical_and(columns >= fringe[0], columns < fringe[1])
            blend = jnp.where(jnp.logical_and(inside, is_farm), FRINGE_BLEND, 0.0)
            for c in range(3):
                own = moved[distance, c * share + z]
                if s >= groups - outlet:
                    own = own + blend * (upstream[s - groups + outlet, c * share + z] - own)
                spot = slice(s * cells_x, (s + 1) * cells_x)
                velocity_next[c, z, spot] = own - slopes[c][spot]


def cas(rows, columns, length):
    angle = (np.outer(rows, columns) % length) * (2.0 * np.pi / length)
    return np.cos(angle) + np.sin(angle)


def tables(levels, total_x, total_y, groups):
    half = total_y // 2
    lane_width = LANES // groups
    every_x = np.arange(total_x)
    every_y = np.arange(total_y)
    table_x = cas(every_x, every_x, total_x)
    table_y = cas(every_y, every_y, total_y)
    slope_y = 0.5 * (np.roll(table_y, -1, axis=1) - np.roll(table_y, 1, axis=1))
    level = np.arange(levels) + 0.5
    table_z = np.cos(np.outer(level, level) * (np.pi / levels))
    spread_z = np.kron(table_z, np.eye(lane_width))
    order = np.arange(levels).reshape(ROWS, levels // ROWS).T.reshape(levels)
    parted = np.concatenate([every_y[::2], every_y[1::2]])
    backward = [
        np.concatenate([table_y[:, here], slope_y[:, here]], axis=1)
        for here in (slice(0, half), slice(half, total_y))
    ]
    pair_x = np.einsum("kx,ab->akxb", table_x, np.eye(2)).reshape(2 * total_x, 2 * total_x)
    norm = levels / 2.0 * total_x * total_y
    wave_x = norm * (2.0 * np.cos(every_x * (2.0 * np.pi / total_x)) - 2.0)
    wave_y = norm * (2.0 * np.cos(every_y * (2.0 * np.pi / total_y)) - 2.0)
    wave_z = norm * (2.0 * np.cos(level * (np.pi / levels)) - 2.0)
    waves = wave_z.reshape(1, 1, -1, groups, 1) + wave_y.reshape(2, groups, 1, 1, lane_width)
    waves = waves.transpose(1, 0, 2, 3, 4).reshape(groups, 2, levels // groups, LANES)
    pencil = np.zeros((spread_z.shape[0] + 2 * total_x, spread_z.shape[1]))
    pencil[: spread_z.shape[0]] = spread_z
    pencil[spread_z.shape[0] :, : 2 * total_x] = pair_x
    pencil[spread_z.shape[0] : -total_x, 2 * total_x : 3 * total_x] = table_x
    pencil[spread_z.shape[0] : -total_x, 4 * total_x : 4 * total_x + LANES] = wave_x[:, None]
    return [
        jnp.asarray(t, jnp.float32)
        for t in (
            pencil,
            table_y[parted],
            np.stack(backward),
            table_z[:, order],
            waves,
        )
    ]


def call(kernel, out_shapes, scratch, *operands):
    in_specs = [
        pl.BlockSpec(memory_space=pltpu.SMEM if o.dtype == jnp.int32 else pltpu.VMEM)
        for o in operands
    ]
    return pl.pallas_call(
        kernel,
        out_shape=out_shapes,
        in_specs=in_specs,
        out_specs=jax.tree.map(lambda _: pl.BlockSpec(memory_space=pltpu.VMEM), out_shapes),
        scratch_shapes=scratch,
        compiler_params=pltpu.CompilerParams(vmem_limit_bytes=VMEM_BYTES),
    )(*operands)


def thrust_weights(turbine_cells, along_x, along_y, along_z, total_y, strength):
    matches = (along_x[:, None] == turbine_cells[None, :, 0]).astype(jnp.bfloat16)
    offset_y = (along_y[None, :] - turbine_cells[:, 1:2] + total_y // 2) % total_y - total_y // 2
    offset_z = along_z[None, :] - turbine_cells[:, 2:3]
    distance = (
        offset_z[:, :, None] * offset_z[:, :, None] + offset_y[:, None, :] * offset_y[:, None, :]
    )
    inside = (distance <= RADIUS * RADIUS).astype(jnp.bfloat16)
    count = jnp.einsum("xt,tzy->xzy", matches, inside, preferred_element_type=jnp.float32)
    return strength * count


def paired_plan(velocity, turbine_cells, fringe_bounds):
    groups = lax.axis_size("gx")
    initial = velocity[0]
    _, levels, cells_x, cells_y = initial.shape
    total_x, total_y = cells_x * groups, 2 * cells_y
    share, share_x = levels // ROWS, cells_x // 2
    section, place, core = (lax.axis_index("sec"), lax.axis_index("gx"), lax.axis_index("gy"))
    pencil, table_y, backward, table_z, waves = tables(levels, total_x, total_y, groups)

    near, far = REACH - 4, 4
    up = [(i, (i + 1) % groups) for i in range(groups)]
    down = [(j, i) for i, j in up]
    swap = [(0, 1), (1, 0)]
    straight = [(2 * i, 2 * j) for i, j in up] + [(2 * j + 1, 2 * i + 1) for i, j in up]
    crossed = [(2 * i + 1, 2 * j) for i, j in up] + [(2 * j, 2 * i + 1) for i, j in up]
    pairs_across = [(i, i ^ 1) for i in range(groups)]
    pairs_around = [(i, (i - 1 if i % 2 == 0 else i + 1) % groups) for i in range(groups)]
    f32 = jnp.float32
    flat = initial.reshape(-1, cells_y)

    def narrow(count):
        return jax.ShapeDtypeStruct((count, 3, share, ROWS, cells_y), f32)

    lower, upper = call(
        functools.partial(pack_near_kernel, cells_x), [narrow(near)] * 2, [], flat
    )
    around = lax.ppermute(lower, "gx", pairs_around)
    across = lax.ppermute(upper, "gx", pairs_across)
    own, same, other = call(
        pack_kernel, [narrow(cells_x), narrow(far), narrow(far)], [], flat
    )
    own_there = lax.ppermute(own, "gy", swap)
    other, across = lax.optimization_barrier((other, across))
    far_there = lax.ppermute(other, ("gx", "gy"), crossed)
    across_there = lax.ppermute(across, "gy", swap)
    around_there = lax.ppermute(around, "gy", swap)

    strength = 2.0 * THRUST_COEFF * section.astype(jnp.float32)
    along_z = jnp.arange(levels).reshape(ROWS, share).T.reshape(levels)
    along_y = jnp.arange(total_y).reshape(cells_y, 2).T.reshape(total_y)

    def thrust_on(offset, count):
        along_x = (place * cells_x + offset + jnp.arange(count) + total_x) % total_x
        weights = thrust_weights(
            turbine_cells, along_x, along_y, along_z, total_y, strength
        )
        return weights.reshape(count, share, ROWS, total_y)

    near_thrust = thrust_on(2 - near, cells_x + 2 * near - 4)
    far_thrust = thrust_on((2 - REACH) * (1 - core) + (share_x + 1) * core, far + near + share_x - 3)
    far_here = lax.ppermute(same, ("gx", "gy"), straight)
    body = (3, share, ROWS, total_y)

    def columns(count):
        return pltpu.VMEM((count,) + body, f32)

    reached = cells_x + 2 * near
    shapes = [jax.ShapeDtypeStruct((n,) + body, f32) for n in (4, 4, reached - 12)]
    first, second, third = call(
        near_kernel,
        shapes,
        [columns(reached)] * 3
        + [pltpu.VMEM((reached,) + body[1:], f32), pltpu.VMEM(body, f32), columns(reached)],
        own,
        own_there,
        across,
        across_there,
        around,
        around_there,
        near_thrust,
    )
    window = far + near + share_x + 1
    pairs = 3 * share // 2
    piece = jax.ShapeDtypeStruct((ROWS, pairs, 2 * share_x, cells_y), f32)
    parts = levels // (2 * groups)
    piece_here, piece_send, source = call(
        functools.partial(far_kernel, total_x),
        [piece, piece, jax.ShapeDtypeStruct((2 * share_x * levels, total_y), f32)],
        [columns(window)] * 4
        + [
            pltpu.VMEM((window,) + body[1:], f32),
            pltpu.VMEM(body, f32),
            columns(window),
            pltpu.VMEM((share_x * 3 * levels, cells_y), f32),
            pltpu.VMEM((share_x * 3 * levels, cells_y), f32),
        ],
        fringe_bounds,
        own,
        own_there,
        across,
        across_there,
        around,
        around_there,
        far_here,
        far_there,
        first,
        second,
        third,
        far_thrust,
    )
    piece_there = lax.ppermute(piece_send, "gy", swap)
    spectra = call(
        spectra_kernel,
        jax.ShapeDtypeStruct((2, groups, 2, parts, 2 * share_x, LANES), f32),
        [pltpu.VMEM((2, 2 * share_x * levels, LANES), f32)],
        source,
        table_y,
        table_z,
    )
    received = lax.all_to_all(
        spectra.reshape((4 * groups,) + spectra.shape[3:]), ("sec", "gx", "gy"), 0, 0, tiled=True
    ).reshape(spectra.shape)
    blocks = call(
        arrange_kernel,
        [jax.ShapeDtypeStruct((3 * share, cells_x, cells_y), f32)] * groups,
        [],
        piece_here,
        piece_there,
    )
    moved = [blocks[0]] + [
        lax.ppermute(block, "gx", [(i, i ^ d) for i in range(groups)])
        for d, block in enumerate(blocks)
        if d
    ]
    packed = call(
        pencil_kernel,
        jax.ShapeDtypeStruct((groups, 3 * total_x // 4, LANES), f32),
        [],
        received,
        waves,
        pencil,
    )
    packed, *moved = lax.optimization_barrier([packed] + moved)
    moved = jnp.stack(moved)
    outlet = groups // 4
    leaving = jnp.stack(
        [
            lax.dynamic_index_in_dim(moved, place ^ s, 0, keepdims=False)
            for s in range(groups - outlet, groups)
        ]
    )
    upstream = lax.ppermute(leaving, "sec", [(0, 1)])
    returned = lax.all_to_all(packed, "gx", 0, 0, tiled=True)
    returned, upstream = lax.optimization_barrier((returned, upstream))
    partner = lax.ppermute(returned, "gy", swap)
    velocity_next, pressure = call(
        project_kernel,
        [
            jax.ShapeDtypeStruct((3, share, total_x, cells_y), f32),
            jax.ShapeDtypeStruct((share, total_x, cells_y), f32),
        ],
        [],
        fringe_bounds,
        returned,
        partner,
        backward,
        moved,
        upstream,
    )
    return (velocity_next[None], pressure[None])


def on_device(velocity, turbine_cells, fringe_bounds):
    groups = lax.axis_size("gx")
    _, _, levels, cells_x, cells_y = velocity.shape
    paired = (
        lax.axis_size("gy") == 2
        and lax.axis_size("sec") == 2
        and cells_y == LANES
        and cells_x == ROWS
        and groups == ROWS
        and 2 * levels == groups * groups
    )
    plan = paired_plan if paired else general_plan
    return plan(velocity, turbine_cells, fringe_bounds)


def solution(mesh):
    return jax.shard_map(
        on_device,
        mesh=mesh,
        in_specs=(P("sec", None, None, "gx", "gy"), P(), P()),
        out_specs=(P("sec", None, "gx", None, "gy"), P("sec", "gx", None, "gy")),
        check_vma=False,
    )
```

```python
import functools

import jax
import jax.numpy as jnp
import numpy as np
from jax import lax
from jax.experimental import pallas as pl
from jax.experimental.pallas import tpu as pltpu
from jax.sharding import PartitionSpec as P

RADIUS = 4


TIME_STEP = 0.05
SMAG_COEFF = 0.1
THRUST_COEFF = 4.0
DRIVING_FORCE = 0.1
FRINGE_BLEND = 0.5
HIGHEST = lax.Precision.HIGHEST
STAGES = 3
REACH = 2 * STAGES + 1
LANES = 128
SMALLEST = float(np.finfo(np.float32).tiny)
ROWS = 8
VMEM_BYTES = 20 * 1024 * 1024


def extended(x, sides, width):
    for axis, dim in sides:
        count, length = (lax.axis_size(axis), x.shape[dim])
        up = [(i, (i + 1) % count) for i in range(count)]
        down = [(j, i) for i, j in up]
        last = lax.slice_in_dim(x, length - width, length, axis=dim)
        initial = lax.slice_in_dim(x, 0, width, axis=dim)
        before = lax.ppermute(last, axis, up)
        after = lax.ppermute(initial, axis, down)
        x = jnp.concatenate([before, x, after], axis=dim)
    return x


def shifted(block, axis, distance):
    devices = range(lax.axis_size(axis))
    route = [(i - distance, i) for i in devices if i - distance in devices]
    return lax.ppermute(block, axis, route)


def cas_table(row_index, column_index, length):
    product = row_index[:, None] * column_index[None, :] % length
    angle = product.astype(jnp.float32) * (2.0 * jnp.pi / length)
    return jnp.cos(angle) + jnp.sin(angle)


def shift_up(values):
    zeros = jnp.zeros_like(values[..., :1, :, :])
    return jnp.concatenate([values[..., 1:, :, :], zeros], axis=-3)


def shift_down(values):
    zeros = jnp.zeros_like(values[..., :1, :, :])
    return jnp.concatenate([zeros, values[..., :-1, :, :]], axis=-3)


def thomas(right_side, eigen_value):
    length = right_side.shape[0]
    inverses = []
    reduced = []
    for level_index in range(length):
        if level_index == 0:
            diagonal = eigen_value - 1.0
        elif level_index == length - 1:
            diagonal = eigen_value - 3.0
        else:
            diagonal = eigen_value - 2.0
        if level_index == 0:
            pivot_now = diagonal
            current = right_side[0] / pivot_now
        else:
            pivot_now = diagonal - inverses[-1]
            current = (right_side[level_index] - reduced[-1]) / pivot_now
        inverses.append(1.0 / pivot_now)
        reduced.append(current)
    solution = [reduced[-1]]
    for level_index in range(length - 2, -1, -1):
        solution.append(reduced[level_index] - inverses[level_index] * solution[-1])
    return jnp.stack(solution[::-1])


def spanwise_derivative(values, sine_y):
    return -sine_y * jnp.roll(jnp.flip(values, axis=-1), 1, axis=-1)


def widened(values):
    return extended(values, (("gx", 1), ("gy", 2)), 1)


def disk_weights(turbine_cells, along_x, along_y, along_z, total_y):
    matches = (along_x[:, None] == turbine_cells[None, :, 0]).astype(jnp.float32)
    offset_y = (along_y[None, :] - turbine_cells[:, 1:2] + total_y // 2) % total_y - total_y // 2
    offset_z = along_z[None, :] - turbine_cells[:, 2:3]
    distance = (
        offset_z[:, :, None] * offset_z[:, :, None] + offset_y[:, None, :] * offset_y[:, None, :]
    )
    inside = (distance <= RADIUS * RADIUS).astype(jnp.float32)
    return jnp.einsum("xt,tzy->zxy", matches, inside, precision=HIGHEST)


def tendency(velocity_now, farm_flag, disk_weight):
    levels, cells_x, cells_y = (velocity_now.shape[1], velocity_now.shape[2], velocity_now.shape[3])
    border = widened(velocity_now.reshape(3 * levels, cells_x, cells_y)).reshape(
        3, levels, cells_x + 2, cells_y + 2
    )
    plus_x = border[:, :, 2:, 1:-1]
    minus_x = border[:, :, :-2, 1:-1]
    plus_y = border[:, :, 1:-1, 2:]
    minus_y = border[:, :, 1:-1, :-2]
    plus_z = shift_up(velocity_now)
    minus_z = shift_down(velocity_now)
    gradients = [0.5 * (plus_x - minus_x), 0.5 * (plus_y - minus_y), 0.5 * (plus_z - minus_z)]
    strain_squares = jnp.zeros_like(velocity_now[0])
    for component in range(3):
        strain_squares = (
            strain_squares + gradients[component][component] * gradients[component][component]
        )
        for direction in range(component + 1, 3):
            shear = 0.5 * (gradients[direction][component] + gradients[component][direction])
            strain_squares = strain_squares + 2.0 * shear * shear
    viscosity = SMAG_COEFF * jnp.sqrt(2.0 * strain_squares)
    visc_border = widened(viscosity)
    visc_plus_x = visc_border[:, 2:, 1:-1]
    visc_minus_x = visc_border[:, :-2, 1:-1]
    visc_plus_y = visc_border[:, 1:-1, 2:]
    visc_minus_y = visc_border[:, 1:-1, :-2]
    visc_plus_z = shift_up(viscosity)
    visc_minus_z = shift_down(viscosity)
    advection = 0.5 * (plus_x[0] * plus_x - minus_x[0] * minus_x)
    advection = advection + 0.5 * (plus_y[1] * plus_y - minus_y[1] * minus_y)
    advection = advection + 0.5 * (plus_z[2] * plus_z - minus_z[2] * minus_z)
    diffusion = 0.5 * (viscosity + visc_plus_x) * (plus_x - velocity_now) - 0.5 * (
        viscosity + visc_minus_x
    ) * (velocity_now - minus_x)
    diffusion = (
        diffusion
        + 0.5 * (viscosity + visc_plus_y) * (plus_y - velocity_now)
        - 0.5 * (viscosity + visc_minus_y) * (velocity_now - minus_y)
    )
    diffusion = (
        diffusion
        + 0.5 * (viscosity + visc_plus_z) * (plus_z - velocity_now)
        - 0.5 * (viscosity + visc_minus_z) * (velocity_now - minus_z)
    )
    changes = diffusion - advection
    streamwise = DRIVING_FORCE - THRUST_COEFF * farm_flag * disk_weight * velocity_now[0] * jnp.abs(
        velocity_now[0]
    )
    return jnp.concatenate([changes[:1] + streamwise[None], changes[1:]], axis=0)


def general_plan(velocity, turbine_cells, fringe_bounds):
    initial = velocity[0]
    levels, cells_x, cells_y = (initial.shape[1], initial.shape[2], initial.shape[3])
    total_y = cells_y * lax.axis_size("gy")
    x_anchor = lax.axis_index("gx") * cells_x
    y_anchor = lax.axis_index("gy") * cells_y
    farm_flag = lax.axis_index("sec").astype(jnp.float32)
    along_x = x_anchor + jnp.arange(cells_x, dtype=jnp.int32)
    along_y = y_anchor + jnp.arange(cells_y, dtype=jnp.int32)
    along_z = jnp.arange(levels, dtype=jnp.int32)
    disk_weight = disk_weights(turbine_cells, along_x, along_y, along_z, total_y)
    segment_one = initial + TIME_STEP * tendency(initial, farm_flag, disk_weight)
    segment_two = 0.75 * initial + 0.25 * (
        segment_one + TIME_STEP * tendency(segment_one, farm_flag, disk_weight)
    )
    segment_three = initial / 3.0 + 2.0 / 3.0 * (
        segment_two + TIME_STEP * tendency(segment_two, farm_flag, disk_weight)
    )
    regrouped = lax.all_to_all(segment_three, "gx", split_axis=1, concat_axis=2, tiled=True)
    count_x = regrouped.shape[2]
    quarter = count_x // 4
    cut_at = count_x - quarter
    outlet_part = regrouped[:, :, cut_at:, :]
    upstream = shifted(outlet_part, "sec", 1)
    columns = cut_at + jnp.arange(quarter, dtype=jnp.int32)
    inside = ((columns >= fringe_bounds[0]) & (columns < fringe_bounds[1])).astype(jnp.float32)
    weight = FRINGE_BLEND * farm_flag * inside
    blended_part = outlet_part + weight[:, None] * (upstream - outlet_part)
    regrouped = jnp.concatenate([regrouped[:, :, :cut_at, :], blended_part], axis=2)
    index_x = jnp.arange(count_x, dtype=jnp.int32)
    table_x = cas_table(index_x, index_x, count_x)
    gradient_u = 0.5 * (jnp.roll(regrouped[0], -1, axis=1) - jnp.roll(regrouped[0], 1, axis=1))
    fields = jnp.stack([gradient_u, regrouped[1], regrouped[2]])
    spectral_x = jnp.einsum("kx,czxy->czky", table_x, fields, precision=HIGHEST)
    columns_view = lax.all_to_all(
        lax.all_to_all(spectral_x, "gx", split_axis=2, concat_axis=1, tiled=True),
        "gy",
        split_axis=2,
        concat_axis=3,
        tiled=True,
    )
    slice_width = columns_view.shape[2]
    count_y = columns_view.shape[3]
    index_y = jnp.arange(count_y, dtype=jnp.int32)
    table_y = cas_table(index_y, index_y, count_y)
    spectrum = jnp.einsum("ly,czky->czkl", table_y, columns_view, precision=HIGHEST)
    sine_y = jnp.sin(index_y.astype(jnp.float32) * (2.0 * jnp.pi / count_y))
    source = (
        spectrum[0]
        + spanwise_derivative(spectrum[1], sine_y)
        + 0.5 * (shift_up(spectrum[2]) - shift_down(spectrum[2]))
    )
    wave_x = (
        lax.axis_index("gx") * cells_x
        + lax.axis_index("gy") * slice_width
        + jnp.arange(slice_width, dtype=jnp.int32)
    )
    eigen_value = 2.0 * jnp.cos(wave_x.astype(jnp.float32) * (2.0 * jnp.pi / count_x))[:, None]
    eigen_value = (
        eigen_value
        + 2.0 * jnp.cos(index_y.astype(jnp.float32) * (2.0 * jnp.pi / count_y))[None, :]
        - 4.0
    )
    solved = thomas(source, eigen_value)
    above_level = jnp.concatenate([solved[1:], -solved[-1:]], axis=0)
    below_level = jnp.concatenate([solved[:1], solved[:-1]], axis=0)
    coefficients = jnp.stack(
        [solved, spanwise_derivative(solved, sine_y), 0.5 * (above_level - below_level)]
    )
    physical_y = jnp.einsum("yl,czkl->czky", table_y, coefficients, precision=HIGHEST) * (
        1.0 / count_y
    )
    returned = lax.all_to_all(
        lax.all_to_all(physical_y, "gx", split_axis=1, concat_axis=2, tiled=True),
        "gy",
        split_axis=3,
        concat_axis=2,
        tiled=True,
    )
    group_size = count_x // lax.axis_size("gy")
    wave_back = (
        index_x // slice_width % lax.axis_size("gx") * cells_x
        + index_x // group_size * slice_width
        + index_x % slice_width
    )
    inverse_table = cas_table(index_x, wave_back, count_x)
    physical = jnp.einsum("xp,czpy->czxy", inverse_table, returned, precision=HIGHEST) * (
        1.0 / count_x
    )
    pressure = physical[0]
    gradient_p = 0.5 * (jnp.roll(pressure, -1, axis=1) - jnp.roll(pressure, 1, axis=1))
    velocity_next = regrouped - jnp.stack([gradient_p, physical[1], physical[2]])
    return (velocity_next[None], pressure[None])


def split(values):
    high = values.astype(jnp.bfloat16)
    low = values - high.astype(jnp.float32)
    return high, low.astype(jnp.bfloat16)


def dot(left, right):
    (a, da), (b, db) = split(left), split(right)

    def product(x, y):
        return jnp.dot(x, y, preferred_element_type=jnp.float32)

    return product(a, b) + (product(a, db) + product(da, b))


def swap_blocks(arrays, width):
    arrays = list(arrays)
    block = lax.broadcasted_iota(jnp.int32, arrays[0].shape, 1) // width
    step = 1
    while step < len(arrays):
        low = (block // step) % 2 == 0
        for index in range(len(arrays)):
            if (index // step) % 2 == 0:
                first, second = arrays[index], arrays[index + step]
                arrays[index] = jnp.where(low, first, pltpu.roll(second, step * width, 1))
                arrays[index + step] = jnp.where(
                    low, pltpu.roll(first, LANES - step * width, 1), second
                )
        step *= 2
    return arrays


def reordered(values, order):
    one = order.astype(jnp.bfloat16)
    high, rest = split(values)
    low = values - high.astype(jnp.float32) - rest.astype(jnp.float32)

    def product(x):
        return jnp.dot(x, one, preferred_element_type=jnp.float32)

    return (product(high) + product(rest)) + product(low.astype(jnp.bfloat16))


def parting(lanes, inverse=False):
    line = lax.broadcasted_iota(jnp.int32, (lanes, lanes), 1 if inverse else 0)
    spot = lax.broadcasted_iota(jnp.int32, (lanes, lanes), 0 if inverse else 1)
    later = jnp.where(spot >= lanes // 2, 1, 0)
    place = 2 * (spot - later * (lanes // 2)) + (later ^ lax.axis_index("gy"))
    return jnp.where(line == place, 1.0, 0.0)


def packed_columns(initial, columns, cells_x, tiles):
    total, lanes = initial.shape
    levels = total // (3 * cells_x)
    rows = levels // tiles
    picked = [
        initial[pl.ds((c * levels + t) * cells_x + x, rows, stride=tiles * cells_x), :]
        for x in columns
        for c in range(3)
        for t in range(tiles)
    ]
    values = reordered(jnp.concatenate(picked, axis=0), parting(lanes))
    return values.reshape(len(columns), 3, tiles, rows, lanes)


def pack_near_kernel(cells_x, initial, lower, upper):
    near, _, tiles, _, _ = lower.shape
    columns = list(range(near)) + list(range(cells_x - near, cells_x))
    values = packed_columns(initial, columns, cells_x, tiles)
    even = lax.axis_index("gx") % 2 == 0

    @pl.when(even)
    def _():
        lower[...] = values[:near]
        upper[...] = values[near:]

    @pl.when(jnp.logical_not(even))
    def _():
        lower[...] = values[near:]
        upper[...] = values[:near]


def pack_kernel(initial, own, same, other):
    cells_x, _, tiles, _, _ = own.shape
    far = same.shape[0]
    tail, head = cells_x - REACH, REACH - far
    values = packed_columns(initial, list(range(cells_x)), cells_x, tiles)
    own[...] = values
    is_first = lax.axis_index("gy") == 0

    @pl.when(is_first)
    def _():
        same[...] = values[tail : tail + far]
        other[...] = values[head : head + far]

    @pl.when(jnp.logical_not(is_first))
    def _():
        same[...] = values[head : head + far]
        other[...] = values[tail : tail + far]


class Stencil:
    def __init__(self, tiles, rows, width, viscosity, faces, thrust, start, beside):
        self.tiles, self.rows, self.width, self.beside = (tiles, rows, width, beside)
        self.viscosity, self.faces, self.thrust, self.start = (viscosity, faces, thrust, start)
        row = lax.broadcasted_iota(jnp.int32, (rows, width), 0)
        self.top = row == rows - 1
        self.bottom = row == 0

    def next_y(self, f):
        half = self.width // 2
        return jnp.concatenate([f[:, half:], pltpu.roll(f[:, :half], half - 1, 1)], axis=1)

    def last_y(self, f):
        half = self.width // 2
        return jnp.concatenate([pltpu.roll(f[:, half:], 1, 1), f[:, :half]], axis=1)

    def next_z(self, parts, t):
        if t < self.tiles - 1:
            return parts[t + 1]
        return jnp.where(self.top, 0.0, pltpu.roll(parts[0], self.rows - 1, 0))

    def last_z(self, parts, t):
        if t > 0:
            return parts[t - 1]
        return jnp.where(self.bottom, 0.0, pltpu.roll(parts[self.tiles - 1], 1, 0))

    def set_viscosity(self, now, first, count):
        tiles = self.tiles

        def column(n, carry):
            i = first + n
            here = [[now[i, c, t] for t in range(tiles)] for c in range(3)]
            found, sides = [], []
            for t in range(tiles):
                d_x = [now[i + 1, c, t] - now[i - 1, c, t] for c in range(3)]
                after_y = [self.next_y(f[t]) for f in here]
                sides.append(after_y)
                d_y = [a - self.last_y(f[t]) for a, f in zip(after_y, here)]
                d_z = [self.next_z(f, t) - self.last_z(f, t) for f in here]
                diagonal = d_x[0] * d_x[0] + d_y[1] * d_y[1] + d_z[2] * d_z[2]
                xy = d_x[1] + d_y[0]
                xz = d_x[2] + d_z[0]
                yz = d_y[2] + d_z[1]
                total = (diagonal + diagonal) + (xy * xy + xz * xz + yz * yz)
                root = total * lax.rsqrt(jnp.maximum(total, SMALLEST))
                found.append((0.5 * SMAG_COEFF) * root)
            for t in range(tiles):
                self.viscosity[i, t] = found[t]
                for c in range(3):
                    self.beside[i, c, t] = sides[t][c]
            return carry

        lax.fori_loop(0, count, column, 0, unroll=4 if count % 4 == 0 else 6)

    def face(self, both, here, after, lead):
        low = both + here[lead]
        high = both - after[lead]
        return [after[c] * high - here[c] * low for c in range(3)]

    def face_x(self, now, i, t):
        here = [now[i, c, t] for c in range(3)]
        after = [now[i + 1, c, t] for c in range(3)]
        return self.face(self.viscosity[i, t] + self.viscosity[i + 1, t], here, after, 0)

    def advance(self, now, then, first, count, keep, gain):
        tiles, scale = self.tiles, 0.5 * TIME_STEP * gain
        for t in range(tiles):
            for c, f in enumerate(self.face_x(now, first - 1, t)):
                self.faces[c, t] = f

        def column(n, carry):
            i = first + n
            eddy = [self.viscosity[i, t] for t in range(tiles)]
            field = [[now[i, c, t] for t in range(tiles)] for c in range(3)]

            def face_z(t):
                here = [f[t] for f in field]
                after = [self.next_z(f, t) for f in field]
                return self.face(eddy[t] + self.next_z(eddy, t), here, after, 2)

            last = face_z(tiles - 1)
            floor = eddy[0] - field[2][0]
            below = [
                jnp.where(self.bottom, field[c][0] * floor, pltpu.roll(last[c], 1, 0))
                for c in range(3)
            ]
            ahead_of = [self.face_x(now, i, t) for t in range(tiles)]
            before_of = [[self.faces[c, t] for c in range(3)] for t in range(tiles)]
            found = []
            for t in range(tiles):
                here = [f[t] for f in field]
                above = last if t == tiles - 1 else face_z(t)
                ahead, before = ahead_of[t], before_of[t]
                beside = [self.beside[i, c, t] for c in range(3)]
                side = self.face(eddy[t] + self.next_y(eddy[t]), here, beside, 1)
                for c in range(3):
                    change = (
                        (ahead[c] - before[c])
                        + (side[c] - self.last_y(side[c]))
                        + (above[c] - below[c])
                    )
                    if c == 0:
                        drag = self.thrust[i - 2, t] * here[0] * jnp.abs(here[0])
                        change = change + (2.0 * DRIVING_FORCE - drag)
                    if keep == 0.0:
                        found.append(here[c] + scale * change)
                    else:
                        found.append(keep * self.start[i, c, t] + gain * here[c] + scale * change)
                below = above
            for t in range(tiles):
                for c in range(3):
                    then[i, c, t] = found[3 * t + c]
                    self.faces[c, t] = ahead_of[t][c]
            return carry

        lax.fori_loop(0, count, column, 0, unroll=2)

    def stage(self, number, now, then, first, count):
        keep, gain = ((0.0, 1.0), (0.75, 0.25), (1.0 / 3.0, 2.0 / 3.0))[number]
        self.set_viscosity(now, first - 1, count + 2)
        self.advance(now, then, first, count, keep, gain)


def place_columns(start, runs_of):
    half = start.shape[-1] // 2
    front = lax.broadcasted_iota(jnp.int32, start.shape[-2:-1] + (half,), 1) < half // 2
    core = lax.axis_index("gy")
    odd = lax.axis_index("gx") % 2

    def copy(side, parity):
        for first, here, there, begin, count in runs_of(side, parity):
            low, high = (here, there) if side == 0 else (there, here)
            for n in range(count):
                for c in range(start.shape[1]):
                    for t in range(start.shape[2]):
                        a, b = low[begin + n, c, t], high[begin + n, c, t]
                        start[first + n, c, t, :, :half] = jnp.where(front, a, b)
                        start[first + n, c, t, :, half:] = pltpu.roll(
                            jnp.where(front, b, a), half // 2, 1
                        )

    for side in range(2):
        for parity in range(2):
            chosen = jnp.logical_and(core == side, odd == parity)
            pl.when(chosen)(functools.partial(copy, side, parity))


def near_kernel(
    own_here,
    own_there,
    across_here,
    across_there,
    around_here,
    around_there,
    thrust,
    first,
    second,
    third,
    start,
    stage_a,
    stage_b,
    viscosity,
    faces,
    beside,
):
    cells_x = own_here.shape[0]
    near = across_here.shape[0]
    _, _, tiles, rows, width = start.shape
    core = lax.axis_index("gy")

    def runs_of(side, parity):
        across, around = (across_here, across_there), (around_here, around_there)
        left, right = (around, across) if parity == 0 else (across, around)
        return (
            (0, *left, 0, near),
            (near, own_here, own_there, 0, cells_x),
            (near + cells_x, *right, 0, near),
        )

    place_columns(start, runs_of)
    stencil = Stencil(tiles, rows, width, viscosity, faces, thrust, start, beside)
    columns = start.shape[0]
    stencil.stage(0, start, stage_a, 2, columns - 4)
    stencil.stage(1, stage_a, stage_b, 4, columns - 8)
    first[...] = stage_a[pl.ds(2 + core * (columns - 8), 4)]
    second[...] = stage_b[pl.ds(4 + core * (columns - 12), 4)]
    stencil.stage(2, stage_b, stage_a, 6, columns - 12)
    third[...] = stage_a[pl.ds(6, columns - 12)]


def far_kernel(
    total_x,
    fringe,
    own_here,
    own_there,
    across_here,
    across_there,
    around_here,
    around_there,
    far_here,
    far_there,
    first,
    second,
    third,
    thrust,
    piece_here,
    piece_there,
    source,
    start,
    stage_a,
    stage_b,
    stage_c,
    viscosity,
    faces,
    beside,
    columns_here,
    columns_there,
):
    cells_x = own_here.shape[0]
    near, far = across_here.shape[0], far_here.shape[0]
    _, _, tiles, rows, width = start.shape
    half = width // 2
    share_x = cells_x // 2
    inner = share_x + 1
    core = lax.axis_index("gy")

    def runs_of(side, parity):
        across, around = (across_here, across_there), (around_here, around_there)
        if side == 0:
            return (
                (0, far_here, far_there, 0, far),
                (far, *(around if parity == 0 else across), 0, near),
                (far + near, own_here, own_there, 0, inner),
            )
        return (
            (0, own_here, own_there, cells_x - inner, inner),
            (inner, *(across if parity == 0 else around), 0, near),
            (inner + near, far_here, far_there, 0, far),
        )

    place_columns(start, runs_of)
    stencil = Stencil(tiles, rows, width, viscosity, faces, thrust, start, beside)
    stencil.stage(0, start, stage_a, 2 + 4 * core, 4)
    stage_a[pl.ds(6 - 4 * core, 4)] = first[...]
    stencil.stage(1, stage_a, stage_b, 4, 4)
    stage_b[pl.ds(8 - 8 * core, 4)] = second[...]
    stencil.stage(2, stage_b, stage_c, 6 - 4 * core, 4)
    stage_c[pl.ds(10 - 10 * core, 2)] = third[...]

    origin = REACH - core * (REACH - 1)
    pairs = 3 * tiles // 2
    front = lax.broadcasted_iota(jnp.int32, (rows, half), 1) < half // 2
    for x in range(share_x):
        for c in range(3):
            for t in range(tiles):
                n = c * tiles + t
                field = stage_c[origin + x, c, t]
                even, odd = field[:, :half], pltpu.roll(field[:, half:], half // 2, 1)
                low, high = jnp.where(front, even, odd), jnp.where(front, odd, even)
                spot = pl.ds((((n % 2) * share_x + x) * pairs + n // 2) * rows, rows)
                columns_here[spot, :] = jnp.where(core == 0, low, high)
                columns_there[spot, :] = jnp.where(core == 0, high, low)
    for s in range(rows):
        for m in range(pairs):
            spot = pl.ds(m * rows + s, 2 * share_x, stride=pairs * rows)
            piece_here[s, m] = columns_here[spot, :]
            piece_there[s, m] = columns_there[spot, :]

    is_farm = lax.axis_index("sec") == 1
    corner = lax.axis_index("gx") * cells_x + core * share_x

    def weight(offset, dest):
        place = lax.rem(corner + offset + total_x, total_x)
        inside = jnp.logical_and(place >= fringe[0], place < fringe[1])
        blend = jnp.where(inside, FRINGE_BLEND, 0.0)
        share = jnp.where(is_farm, 1.0 - blend, blend)
        if dest == 0:
            share = jnp.where(is_farm, 0.0, 1.0)
        return 0.5 * share

    for x in range(share_x):
        i = origin + x
        upright = [stage_c[i, 2, t] for t in range(tiles)]
        for t in range(tiles):
            cross = stage_c[i, 1, t]
            plane = (stencil.next_y(cross) - stencil.last_y(cross)) + (
                stencil.next_z(upright, t) - stencil.last_z(upright, t)
            )
            after, before = stage_c[i + 1, 0, t], stage_c[i - 1, 0, t]
            for dest in range(2):
                source[pl.ds(((dest * share_x + x) * tiles + t) * rows, rows), :] = (
                    weight(x + 1, dest) * after
                    - weight(x - 1, dest) * before
                    + weight(x, dest) * plane
                )


def spectra_kernel(source, table_y, table_z, spectra, modes):
    _, groups, _, parts, rows, lanes = spectra.shape
    levels = table_z.shape[0]
    count, total_y = source.shape
    columns = count // levels
    along_y = dot(source[...], table_y[...])
    beside = [along_y[n * levels : (n + 1) * levels] for n in range(columns)]
    both = dot(table_z[...], jnp.concatenate(beside, axis=1))
    for n in range(columns):
        for h in range(2):
            first = n * total_y + h * lanes
            modes[h, pl.ds(n * levels, levels), :] = both[:, first : first + lanes]
    for dest in range(2):
        for h in range(2):
            for p in range(parts):
                first = dest * count // 2 + p * groups
                picked = [
                    modes[h, pl.ds(first + b, rows, stride=levels // 2), :] for b in range(groups)
                ]
                for g, block in enumerate(swap_blocks(picked, lanes // groups)):
                    spectra[dest, g, h, p] = block


def arrange_kernel(piece_here, piece_there, *blocks):
    groups, pairs, rows, lanes = piece_here.shape
    half = rows // 2
    low = lax.broadcasted_iota(jnp.int32, (rows, lanes), 0) < half
    is_first = lax.axis_index("gy") == 0
    order = parting(lanes, inverse=True)
    for distance, block in enumerate(blocks):
        g = lax.axis_index("gx") ^ distance
        merged = []
        for m in range(pairs):
            here, there = piece_here[g, m], piece_there[g, m]
            before = jnp.where(is_first, here, there)
            after = jnp.where(is_first, there, here)
            merged.append(jnp.where(low, before, pltpu.roll(after, half, 0)))
            merged.append(jnp.where(low, pltpu.roll(before, half, 0), after))
        values = reordered(jnp.concatenate(merged, axis=0), order)
        block[...] = values.reshape(block.shape)


def pencil_kernel(received, waves, table, packed):
    _, groups, cores, parts, rows, lanes = received.shape
    total_x = groups * rows
    lane_width = lanes // groups
    wave, base = 2 * total_x, table.shape[1]
    spread_z = table[:base]
    pair_x = table[base : base + wave, :wave]
    table_x = table[base : base + total_x, wave : wave + total_x]
    along_x = table[base : base + total_x, 2 * wave : 2 * wave + lanes]
    along_zy = waves[lax.axis_index("gx"), lax.axis_index("gy")]
    spectrum = jnp.concatenate(
        [(received[0, :, :, p] + received[1, :, :, p]).reshape(-1, lanes) for p in range(parts)],
        axis=1,
    )
    solved = dot(pair_x, spectrum)
    pieces = []
    for a in range(2 * parts):
        p, side = a % parts, a // parts
        block = solved[side * total_x : (side + 1) * total_x, p * lanes : (p + 1) * lanes]
        pieces.append(block / (along_x + along_zy[a : a + 1]))
    field = dot(dot(table_x, jnp.concatenate(pieces, axis=1)), spread_z)
    levels_of = [field[:, a * lanes : (a + 1) * lanes] for a in range(2 * parts)]
    wide = lax.broadcasted_iota(jnp.int32, (total_x // 2, lanes), 1)
    left = wide < lanes // 2
    quarter = total_x // 4
    block = lax.broadcasted_iota(jnp.int32, (quarter, lanes), 1) // lane_width
    for g in range(groups):
        a, odd = divmod(g, 2)
        now = levels_of[a]
        front, rear = now[: total_x // 2], now[total_x // 2 :]
        if odd:
            main = jnp.where(left, pltpu.roll(front, lanes // 2, 1), rear)
            lower, lower_lane = now, lanes // 2 - lane_width
            upper, upper_lane = levels_of[min(a + 1, 2 * parts - 1)], 0
        else:
            main = jnp.where(left, front, pltpu.roll(rear, lanes // 2, 1))
            lower, lower_lane = levels_of[max(a - 1, 0)], lanes - lane_width
            upper, upper_lane = now, lanes // 2
        edge = None
        for q in range(4):
            for n, (whole, lane) in enumerate(((lower, lower_lane), (upper, upper_lane))):
                spot = 2 * q + n
                move = (spot * lane_width - lane) % lanes
                rolled = whole[q * quarter : (q + 1) * quarter]
                if move:
                    rolled = pltpu.roll(rolled, move, 1)
                edge = rolled if edge is None else jnp.where(block == spot, rolled, edge)
        packed[g, : total_x // 2] = main
        packed[g, total_x // 2 : 3 * quarter] = edge


def project_kernel(fringe, received, partner, table_y, moved, upstream, velocity_next, pressure):
    groups = received.shape[0]
    share, total_x, lanes = pressure.shape
    cells_x = total_x // groups
    width = lanes // groups
    place, core = lax.axis_index("gx"), lax.axis_index("gy")
    main_rows = total_x // 2
    rows = partner.shape[1]

    def levels_in(arrays):
        main = swap_blocks([arrays[s, :main_rows] for s in range(groups)], width)
        edge = swap_blocks([arrays[s, main_rows:rows] for s in range(groups)], width)
        inner = [jnp.concatenate([main[n], main[share + n]], axis=0) for n in range(share)]
        outer = [jnp.concatenate([edge[2 * q + n] for q in range(4)], axis=0) for n in range(2)]
        return [outer[0]] + inner + [outer[1]]

    here, there = levels_in(received), levels_in(partner)
    here, there = jnp.concatenate(here, axis=0), jnp.concatenate(there, axis=0)
    low = jnp.where(core == 0, here, there)
    high = jnp.where(core == 0, there, here)
    both = dot(jnp.concatenate([low, high], axis=1), table_y[core])
    fields = [both[n * total_x : (n + 1) * total_x] for n in range(share + 2)]
    values = [f[:, :lanes] for f in fields]
    values[0] = jnp.where(place == 0, values[1], values[0])
    values[-1] = jnp.where(place == groups - 1, -values[-2], values[-1])
    is_farm = lax.axis_index("sec") == 1
    outlet = upstream.shape[0]
    for z in range(share):
        now = values[z + 1]
        pressure[z] = now
        slopes = [
            0.5 * (pltpu.roll(now, total_x - 1, 0) - pltpu.roll(now, 1, 0)),
            fields[z + 1][:, lanes:],
            0.5 * (values[z + 2] - values[z]),
        ]
        for s in range(groups):
            distance = place ^ s
            columns = s * cells_x + lax.broadcasted_iota(jnp.int32, (cells_x, lanes), 0)
            inside = jnp.logical_and(columns >= fringe[0], columns < fringe[1])
            blend = jnp.where(jnp.logical_and(inside, is_farm), FRINGE_BLEND, 0.0)
            for c in range(3):
                own = moved[distance, c * share + z]
                if s >= groups - outlet:
                    own = own + blend * (upstream[s - groups + outlet, c * share + z] - own)
                spot = slice(s * cells_x, (s + 1) * cells_x)
                velocity_next[c, z, spot] = own - slopes[c][spot]


def cas(rows, columns, length):
    angle = (np.outer(rows, columns) % length) * (2.0 * np.pi / length)
    return np.cos(angle) + np.sin(angle)


def tables(levels, total_x, total_y, groups):
    half = total_y // 2
    lane_width = LANES // groups
    every_x = np.arange(total_x)
    every_y = np.arange(total_y)
    table_x = cas(every_x, every_x, total_x)
    table_y = cas(every_y, every_y, total_y)
    slope_y = 0.5 * (np.roll(table_y, -1, axis=1) - np.roll(table_y, 1, axis=1))
    level = np.arange(levels) + 0.5
    table_z = np.cos(np.outer(level, level) * (np.pi / levels))
    spread_z = np.kron(table_z, np.eye(lane_width))
    order = np.arange(levels).reshape(ROWS, levels // ROWS).T.reshape(levels)
    parted = np.concatenate([every_y[::2], every_y[1::2]])
    backward = [
        np.concatenate([table_y[:, here], slope_y[:, here]], axis=1)
        for here in (slice(0, half), slice(half, total_y))
    ]
    pair_x = np.einsum("kx,ab->akxb", table_x, np.eye(2)).reshape(2 * total_x, 2 * total_x)
    norm = levels / 2.0 * total_x * total_y
    wave_x = norm * (2.0 * np.cos(every_x * (2.0 * np.pi / total_x)) - 2.0)
    wave_y = norm * (2.0 * np.cos(every_y * (2.0 * np.pi / total_y)) - 2.0)
    wave_z = norm * (2.0 * np.cos(level * (np.pi / levels)) - 2.0)
    waves = wave_z.reshape(1, 1, -1, groups, 1) + wave_y.reshape(2, groups, 1, 1, lane_width)
    waves = waves.transpose(1, 0, 2, 3, 4).reshape(groups, 2, levels // groups, LANES)
    pencil = np.zeros((spread_z.shape[0] + 2 * total_x, spread_z.shape[1]))
    pencil[: spread_z.shape[0]] = spread_z
    pencil[spread_z.shape[0] :, : 2 * total_x] = pair_x
    pencil[spread_z.shape[0] : -total_x, 2 * total_x : 3 * total_x] = table_x
    pencil[spread_z.shape[0] : -total_x, 4 * total_x : 4 * total_x + LANES] = wave_x[:, None]
    return [
        jnp.asarray(t, jnp.float32)
        for t in (
            pencil,
            table_y[parted],
            np.stack(backward),
            table_z[:, order],
            waves,
        )
    ]


def call(kernel, out_shapes, scratch, *operands):
    in_specs = [
        pl.BlockSpec(memory_space=pltpu.SMEM if o.dtype == jnp.int32 else pltpu.VMEM)
        for o in operands
    ]
    return pl.pallas_call(
        kernel,
        out_shape=out_shapes,
        in_specs=in_specs,
        out_specs=jax.tree.map(lambda _: pl.BlockSpec(memory_space=pltpu.VMEM), out_shapes),
        scratch_shapes=scratch,
        compiler_params=pltpu.CompilerParams(vmem_limit_bytes=VMEM_BYTES),
    )(*operands)


def thrust_weights(turbine_cells, along_x, along_y, along_z, total_y, strength):
    matches = (along_x[:, None] == turbine_cells[None, :, 0]).astype(jnp.bfloat16)
    offset_y = (along_y[None, :] - turbine_cells[:, 1:2] + total_y // 2) % total_y - total_y // 2
    offset_z = along_z[None, :] - turbine_cells[:, 2:3]
    distance = (
        offset_z[:, :, None] * offset_z[:, :, None] + offset_y[:, None, :] * offset_y[:, None, :]
    )
    inside = (distance <= RADIUS * RADIUS).astype(jnp.bfloat16)
    count = jnp.einsum("xt,tzy->xzy", matches, inside, preferred_element_type=jnp.float32)
    return strength * count


def paired_plan(velocity, turbine_cells, fringe_bounds):
    groups = lax.axis_size("gx")
    initial = velocity[0]
    _, levels, cells_x, cells_y = initial.shape
    total_x, total_y = cells_x * groups, 2 * cells_y
    share, share_x = levels // ROWS, cells_x // 2
    section, place, core = (lax.axis_index("sec"), lax.axis_index("gx"), lax.axis_index("gy"))
    pencil, table_y, backward, table_z, waves = tables(levels, total_x, total_y, groups)

    near, far = REACH - 4, 4
    up = [(i, (i + 1) % groups) for i in range(groups)]
    down = [(j, i) for i, j in up]
    swap = [(0, 1), (1, 0)]
    straight = [(2 * i, 2 * j) for i, j in up] + [(2 * j + 1, 2 * i + 1) for i, j in up]
    crossed = [(2 * i + 1, 2 * j) for i, j in up] + [(2 * j, 2 * i + 1) for i, j in up]
    pairs_across = [(i, i ^ 1) for i in range(groups)]
    pairs_around = [(i, (i - 1 if i % 2 == 0 else i + 1) % groups) for i in range(groups)]
    f32 = jnp.float32
    flat = initial.reshape(-1, cells_y)

    def narrow(count):
        return jax.ShapeDtypeStruct((count, 3, share, ROWS, cells_y), f32)

    lower, upper = call(
        functools.partial(pack_near_kernel, cells_x), [narrow(near)] * 2, [], flat
    )
    around = lax.ppermute(lower, "gx", pairs_around)
    across = lax.ppermute(upper, "gx", pairs_across)
    own, same, other = call(
        pack_kernel, [narrow(cells_x), narrow(far), narrow(far)], [], flat
    )
    own_there = lax.ppermute(own, "gy", swap)
    other, across = lax.optimization_barrier((other, across))
    far_there = lax.ppermute(other, ("gx", "gy"), crossed)
    across_there = lax.ppermute(across, "gy", swap)
    around_there = lax.ppermute(around, "gy", swap)

    strength = 2.0 * THRUST_COEFF * section.astype(jnp.float32)
    along_z = jnp.arange(levels).reshape(ROWS, share).T.reshape(levels)
    along_y = jnp.arange(total_y).reshape(cells_y, 2).T.reshape(total_y)

    def thrust_on(offset, count):
        along_x = (place * cells_x + offset + jnp.arange(count) + total_x) % total_x
        weights = thrust_weights(
            turbine_cells, along_x, along_y, along_z, total_y, strength
        )
        return weights.reshape(count, share, ROWS, total_y)

    near_thrust = thrust_on(2 - near, cells_x + 2 * near - 4)
    far_thrust = thrust_on((2 - REACH) * (1 - core) + (share_x + 1) * core, far + near + share_x - 3)
    far_here = lax.ppermute(same, ("gx", "gy"), straight)
    body = (3, share, ROWS, total_y)

    def columns(count):
        return pltpu.VMEM((count,) + body, f32)

    reached = cells_x + 2 * near
    shapes = [jax.ShapeDtypeStruct((n,) + body, f32) for n in (4, 4, reached - 12)]
    first, second, third = call(
        near_kernel,
        shapes,
        [columns(reached)] * 3
        + [pltpu.VMEM((reached,) + body[1:], f32), pltpu.VMEM(body, f32), columns(reached)],
        own,
        own_there,
        across,
        across_there,
        around,
        around_there,
        near_thrust,
    )
    window = far + near + share_x + 1
    pairs = 3 * share // 2
    piece = jax.ShapeDtypeStruct((ROWS, pairs, 2 * share_x, cells_y), f32)
    parts = levels // (2 * groups)
    piece_here, piece_send, source = call(
        functools.partial(far_kernel, total_x),
        [piece, piece, jax.ShapeDtypeStruct((2 * share_x * levels, total_y), f32)],
        [columns(window)] * 4
        + [
            pltpu.VMEM((window,) + body[1:], f32),
            pltpu.VMEM(body, f32),
            columns(window),
            pltpu.VMEM((share_x * 3 * levels, cells_y), f32),
            pltpu.VMEM((share_x * 3 * levels, cells_y), f32),
        ],
        fringe_bounds,
        own,
        own_there,
        across,
        across_there,
        around,
        around_there,
        far_here,
        far_there,
        first,
        second,
        third,
        far_thrust,
    )
    piece_there = lax.ppermute(piece_send, "gy", swap)
    spectra = call(
        spectra_kernel,
        jax.ShapeDtypeStruct((2, groups, 2, parts, 2 * share_x, LANES), f32),
        [pltpu.VMEM((2, 2 * share_x * levels, LANES), f32)],
        source,
        table_y,
        table_z,
    )
    received = lax.all_to_all(
        spectra.reshape((4 * groups,) + spectra.shape[3:]), ("sec", "gx", "gy"), 0, 0, tiled=True
    ).reshape(spectra.shape)
    blocks = call(
        arrange_kernel,
        [jax.ShapeDtypeStruct((3 * share, cells_x, cells_y), f32)] * groups,
        [],
        piece_here,
        piece_there,
    )
    moved = [blocks[0]] + [
        lax.ppermute(block, "gx", [(i, i ^ d) for i in range(groups)])
        for d, block in enumerate(blocks)
        if d
    ]
    packed = call(
        pencil_kernel,
        jax.ShapeDtypeStruct((groups, 3 * total_x // 4, LANES), f32),
        [],
        received,
        waves,
        pencil,
    )
    tied = [3, 4, 5]
    packed, *some = lax.optimization_barrier([packed] + [moved[d] for d in tied])
    for d, block in zip(tied, some):
        moved[d] = block
    moved = jnp.stack(moved)
    outlet = groups // 4
    leaving = jnp.stack(
        [
            lax.dynamic_index_in_dim(moved, place ^ s, 0, keepdims=False)
            for s in range(groups - outlet, groups)
        ]
    )
    upstream = lax.ppermute(leaving, "sec", [(0, 1)])
    returned = lax.all_to_all(packed, "gx", 0, 0, tiled=True)
    returned, upstream = lax.optimization_barrier((returned, upstream))
    partner = lax.ppermute(returned, "gy", swap)
    velocity_next, pressure = call(
        project_kernel,
        [
            jax.ShapeDtypeStruct((3, share, total_x, cells_y), f32),
            jax.ShapeDtypeStruct((share, total_x, cells_y), f32),
        ],
        [],
        fringe_bounds,
        returned,
        partner,
        backward,
        moved,
        upstream,
    )
    return (velocity_next[None], pressure[None])


def on_device(velocity, turbine_cells, fringe_bounds):
    groups = lax.axis_size("gx")
    _, _, levels, cells_x, cells_y = velocity.shape
    paired = (
        lax.axis_size("gy") == 2
        and lax.axis_size("sec") == 2
        and cells_y == LANES
        and cells_x == ROWS
        and groups == ROWS
        and 2 * levels == groups * groups
    )
    plan = paired_plan if paired else general_plan
    return plan(velocity, turbine_cells, fringe_bounds)


def solution(mesh):
    return jax.shard_map(
        on_device,
        mesh=mesh,
        in_specs=(P("sec", None, None, "gx", "gy"), P(), P()),
        out_specs=(P("sec", None, "gx", None, "gy"), P("sec", "gx", None, "gy")),
        check_vma=False,
    )
```

```python
import functools

import jax
import jax.numpy as jnp
import numpy as np
from jax import lax
from jax.experimental import pallas as pl
from jax.experimental.pallas import tpu as pltpu
from jax.sharding import PartitionSpec as P

RADIUS = 4


TIME_STEP = 0.05
SMAG_COEFF = 0.1
THRUST_COEFF = 4.0
DRIVING_FORCE = 0.1
FRINGE_BLEND = 0.5
HIGHEST = lax.Precision.HIGHEST
STAGES = 3
REACH = 2 * STAGES + 1
LANES = 128
SMALLEST = float(np.finfo(np.float32).tiny)
ROWS = 8
VMEM_BYTES = 20 * 1024 * 1024


def extended(x, sides, width):
    for axis, dim in sides:
        count, length = (lax.axis_size(axis), x.shape[dim])
        up = [(i, (i + 1) % count) for i in range(count)]
        down = [(j, i) for i, j in up]
        last = lax.slice_in_dim(x, length - width, length, axis=dim)
        initial = lax.slice_in_dim(x, 0, width, axis=dim)
        before = lax.ppermute(last, axis, up)
        after = lax.ppermute(initial, axis, down)
        x = jnp.concatenate([before, x, after], axis=dim)
    return x


def shifted(block, axis, distance):
    devices = range(lax.axis_size(axis))
    route = [(i - distance, i) for i in devices if i - distance in devices]
    return lax.ppermute(block, axis, route)


def cas_table(row_index, column_index, length):
    product = row_index[:, None] * column_index[None, :] % length
    angle = product.astype(jnp.float32) * (2.0 * jnp.pi / length)
    return jnp.cos(angle) + jnp.sin(angle)


def shift_up(values):
    zeros = jnp.zeros_like(values[..., :1, :, :])
    return jnp.concatenate([values[..., 1:, :, :], zeros], axis=-3)


def shift_down(values):
    zeros = jnp.zeros_like(values[..., :1, :, :])
    return jnp.concatenate([zeros, values[..., :-1, :, :]], axis=-3)


def thomas(right_side, eigen_value):
    length = right_side.shape[0]
    inverses = []
    reduced = []
    for level_index in range(length):
        if level_index == 0:
            diagonal = eigen_value - 1.0
        elif level_index == length - 1:
            diagonal = eigen_value - 3.0
        else:
            diagonal = eigen_value - 2.0
        if level_index == 0:
            pivot_now = diagonal
            current = right_side[0] / pivot_now
        else:
            pivot_now = diagonal - inverses[-1]
            current = (right_side[level_index] - reduced[-1]) / pivot_now
        inverses.append(1.0 / pivot_now)
        reduced.append(current)
    solution = [reduced[-1]]
    for level_index in range(length - 2, -1, -1):
        solution.append(reduced[level_index] - inverses[level_index] * solution[-1])
    return jnp.stack(solution[::-1])


def spanwise_derivative(values, sine_y):
    return -sine_y * jnp.roll(jnp.flip(values, axis=-1), 1, axis=-1)


def widened(values):
    return extended(values, (("gx", 1), ("gy", 2)), 1)


def disk_weights(turbine_cells, along_x, along_y, along_z, total_y):
    matches = (along_x[:, None] == turbine_cells[None, :, 0]).astype(jnp.float32)
    offset_y = (along_y[None, :] - turbine_cells[:, 1:2] + total_y // 2) % total_y - total_y // 2
    offset_z = along_z[None, :] - turbine_cells[:, 2:3]
    distance = (
        offset_z[:, :, None] * offset_z[:, :, None] + offset_y[:, None, :] * offset_y[:, None, :]
    )
    inside = (distance <= RADIUS * RADIUS).astype(jnp.float32)
    return jnp.einsum("xt,tzy->zxy", matches, inside, precision=HIGHEST)


def tendency(velocity_now, farm_flag, disk_weight):
    levels, cells_x, cells_y = (velocity_now.shape[1], velocity_now.shape[2], velocity_now.shape[3])
    border = widened(velocity_now.reshape(3 * levels, cells_x, cells_y)).reshape(
        3, levels, cells_x + 2, cells_y + 2
    )
    plus_x = border[:, :, 2:, 1:-1]
    minus_x = border[:, :, :-2, 1:-1]
    plus_y = border[:, :, 1:-1, 2:]
    minus_y = border[:, :, 1:-1, :-2]
    plus_z = shift_up(velocity_now)
    minus_z = shift_down(velocity_now)
    gradients = [0.5 * (plus_x - minus_x), 0.5 * (plus_y - minus_y), 0.5 * (plus_z - minus_z)]
    strain_squares = jnp.zeros_like(velocity_now[0])
    for component in range(3):
        strain_squares = (
            strain_squares + gradients[component][component] * gradients[component][component]
        )
        for direction in range(component + 1, 3):
            shear = 0.5 * (gradients[direction][component] + gradients[component][direction])
            strain_squares = strain_squares + 2.0 * shear * shear
    viscosity = SMAG_COEFF * jnp.sqrt(2.0 * strain_squares)
    visc_border = widened(viscosity)
    visc_plus_x = visc_border[:, 2:, 1:-1]
    visc_minus_x = visc_border[:, :-2, 1:-1]
    visc_plus_y = visc_border[:, 1:-1, 2:]
    visc_minus_y = visc_border[:, 1:-1, :-2]
    visc_plus_z = shift_up(viscosity)
    visc_minus_z = shift_down(viscosity)
    advection = 0.5 * (plus_x[0] * plus_x - minus_x[0] * minus_x)
    advection = advection + 0.5 * (plus_y[1] * plus_y - minus_y[1] * minus_y)
    advection = advection + 0.5 * (plus_z[2] * plus_z - minus_z[2] * minus_z)
    diffusion = 0.5 * (viscosity + visc_plus_x) * (plus_x - velocity_now) - 0.5 * (
        viscosity + visc_minus_x
    ) * (velocity_now - minus_x)
    diffusion = (
        diffusion
        + 0.5 * (viscosity + visc_plus_y) * (plus_y - velocity_now)
        - 0.5 * (viscosity + visc_minus_y) * (velocity_now - minus_y)
    )
    diffusion = (
        diffusion
        + 0.5 * (viscosity + visc_plus_z) * (plus_z - velocity_now)
        - 0.5 * (viscosity + visc_minus_z) * (velocity_now - minus_z)
    )
    changes = diffusion - advection
    streamwise = DRIVING_FORCE - THRUST_COEFF * farm_flag * disk_weight * velocity_now[0] * jnp.abs(
        velocity_now[0]
    )
    return jnp.concatenate([changes[:1] + streamwise[None], changes[1:]], axis=0)


def general_plan(velocity, turbine_cells, fringe_bounds):
    initial = velocity[0]
    levels, cells_x, cells_y = (initial.shape[1], initial.shape[2], initial.shape[3])
    total_y = cells_y * lax.axis_size("gy")
    x_anchor = lax.axis_index("gx") * cells_x
    y_anchor = lax.axis_index("gy") * cells_y
    farm_flag = lax.axis_index("sec").astype(jnp.float32)
    along_x = x_anchor + jnp.arange(cells_x, dtype=jnp.int32)
    along_y = y_anchor + jnp.arange(cells_y, dtype=jnp.int32)
    along_z = jnp.arange(levels, dtype=jnp.int32)
    disk_weight = disk_weights(turbine_cells, along_x, along_y, along_z, total_y)
    segment_one = initial + TIME_STEP * tendency(initial, farm_flag, disk_weight)
    segment_two = 0.75 * initial + 0.25 * (
        segment_one + TIME_STEP * tendency(segment_one, farm_flag, disk_weight)
    )
    segment_three = initial / 3.0 + 2.0 / 3.0 * (
        segment_two + TIME_STEP * tendency(segment_two, farm_flag, disk_weight)
    )
    regrouped = lax.all_to_all(segment_three, "gx", split_axis=1, concat_axis=2, tiled=True)
    count_x = regrouped.shape[2]
    quarter = count_x // 4
    cut_at = count_x - quarter
    outlet_part = regrouped[:, :, cut_at:, :]
    upstream = shifted(outlet_part, "sec", 1)
    columns = cut_at + jnp.arange(quarter, dtype=jnp.int32)
    inside = ((columns >= fringe_bounds[0]) & (columns < fringe_bounds[1])).astype(jnp.float32)
    weight = FRINGE_BLEND * farm_flag * inside
    blended_part = outlet_part + weight[:, None] * (upstream - outlet_part)
    regrouped = jnp.concatenate([regrouped[:, :, :cut_at, :], blended_part], axis=2)
    index_x = jnp.arange(count_x, dtype=jnp.int32)
    table_x = cas_table(index_x, index_x, count_x)
    gradient_u = 0.5 * (jnp.roll(regrouped[0], -1, axis=1) - jnp.roll(regrouped[0], 1, axis=1))
    fields = jnp.stack([gradient_u, regrouped[1], regrouped[2]])
    spectral_x = jnp.einsum("kx,czxy->czky", table_x, fields, precision=HIGHEST)
    columns_view = lax.all_to_all(
        lax.all_to_all(spectral_x, "gx", split_axis=2, concat_axis=1, tiled=True),
        "gy",
        split_axis=2,
        concat_axis=3,
        tiled=True,
    )
    slice_width = columns_view.shape[2]
    count_y = columns_view.shape[3]
    index_y = jnp.arange(count_y, dtype=jnp.int32)
    table_y = cas_table(index_y, index_y, count_y)
    spectrum = jnp.einsum("ly,czky->czkl", table_y, columns_view, precision=HIGHEST)
    sine_y = jnp.sin(index_y.astype(jnp.float32) * (2.0 * jnp.pi / count_y))
    source = (
        spectrum[0]
        + spanwise_derivative(spectrum[1], sine_y)
        + 0.5 * (shift_up(spectrum[2]) - shift_down(spectrum[2]))
    )
    wave_x = (
        lax.axis_index("gx") * cells_x
        + lax.axis_index("gy") * slice_width
        + jnp.arange(slice_width, dtype=jnp.int32)
    )
    eigen_value = 2.0 * jnp.cos(wave_x.astype(jnp.float32) * (2.0 * jnp.pi / count_x))[:, None]
    eigen_value = (
        eigen_value
        + 2.0 * jnp.cos(index_y.astype(jnp.float32) * (2.0 * jnp.pi / count_y))[None, :]
        - 4.0
    )
    solved = thomas(source, eigen_value)
    above_level = jnp.concatenate([solved[1:], -solved[-1:]], axis=0)
    below_level = jnp.concatenate([solved[:1], solved[:-1]], axis=0)
    coefficients = jnp.stack(
        [solved, spanwise_derivative(solved, sine_y), 0.5 * (above_level - below_level)]
    )
    physical_y = jnp.einsum("yl,czkl->czky", table_y, coefficients, precision=HIGHEST) * (
        1.0 / count_y
    )
    returned = lax.all_to_all(
        lax.all_to_all(physical_y, "gx", split_axis=1, concat_axis=2, tiled=True),
        "gy",
        split_axis=3,
        concat_axis=2,
        tiled=True,
    )
    group_size = count_x // lax.axis_size("gy")
    wave_back = (
        index_x // slice_width % lax.axis_size("gx") * cells_x
        + index_x // group_size * slice_width
        + index_x % slice_width
    )
    inverse_table = cas_table(index_x, wave_back, count_x)
    physical = jnp.einsum("xp,czpy->czxy", inverse_table, returned, precision=HIGHEST) * (
        1.0 / count_x
    )
    pressure = physical[0]
    gradient_p = 0.5 * (jnp.roll(pressure, -1, axis=1) - jnp.roll(pressure, 1, axis=1))
    velocity_next = regrouped - jnp.stack([gradient_p, physical[1], physical[2]])
    return (velocity_next[None], pressure[None])


def split(values):
    high = values.astype(jnp.bfloat16)
    low = values - high.astype(jnp.float32)
    return high, low.astype(jnp.bfloat16)


def dot(left, right):
    (a, da), (b, db) = split(left), split(right)

    def product(x, y):
        return jnp.dot(x, y, preferred_element_type=jnp.float32)

    return product(a, b) + (product(a, db) + product(da, b))


def swap_blocks(arrays, width):
    arrays = list(arrays)
    block = lax.broadcasted_iota(jnp.int32, arrays[0].shape, 1) // width
    step = 1
    while step < len(arrays):
        low = (block // step) % 2 == 0
        for index in range(len(arrays)):
            if (index // step) % 2 == 0:
                first, second = arrays[index], arrays[index + step]
                arrays[index] = jnp.where(low, first, pltpu.roll(second, step * width, 1))
                arrays[index + step] = jnp.where(
                    low, pltpu.roll(first, LANES - step * width, 1), second
                )
        step *= 2
    return arrays


def reordered(values, order):
    one = order.astype(jnp.bfloat16)
    high, rest = split(values)
    low = values - high.astype(jnp.float32) - rest.astype(jnp.float32)

    def product(x):
        return jnp.dot(x, one, preferred_element_type=jnp.float32)

    return (product(high) + product(rest)) + product(low.astype(jnp.bfloat16))


def parting(lanes, inverse=False):
    line = lax.broadcasted_iota(jnp.int32, (lanes, lanes), 1 if inverse else 0)
    spot = lax.broadcasted_iota(jnp.int32, (lanes, lanes), 0 if inverse else 1)
    later = jnp.where(spot >= lanes // 2, 1, 0)
    place = 2 * (spot - later * (lanes // 2)) + (later ^ lax.axis_index("gy"))
    return jnp.where(line == place, 1.0, 0.0)


def packed_columns(initial, columns, cells_x, tiles):
    total, lanes = initial.shape
    levels = total // (3 * cells_x)
    rows = levels // tiles
    picked = [
        initial[pl.ds((c * levels + t) * cells_x + x, rows, stride=tiles * cells_x), :]
        for x in columns
        for c in range(3)
        for t in range(tiles)
    ]
    values = reordered(jnp.concatenate(picked, axis=0), parting(lanes))
    return values.reshape(len(columns), 3, tiles, rows, lanes)


def pack_near_kernel(cells_x, initial, lower, upper):
    near, _, tiles, _, _ = lower.shape
    columns = list(range(near)) + list(range(cells_x - near, cells_x))
    values = packed_columns(initial, columns, cells_x, tiles)
    even = lax.axis_index("gx") % 2 == 0

    @pl.when(even)
    def _():
        lower[...] = values[:near]
        upper[...] = values[near:]

    @pl.when(jnp.logical_not(even))
    def _():
        lower[...] = values[near:]
        upper[...] = values[:near]


def pack_kernel(initial, own, same, other):
    cells_x, _, tiles, _, _ = own.shape
    far = same.shape[0]
    tail, head = cells_x - REACH, REACH - far
    values = packed_columns(initial, list(range(cells_x)), cells_x, tiles)
    own[...] = values
    is_first = lax.axis_index("gy") == 0

    @pl.when(is_first)
    def _():
        same[...] = values[tail : tail + far]
        other[...] = values[head : head + far]

    @pl.when(jnp.logical_not(is_first))
    def _():
        same[...] = values[head : head + far]
        other[...] = values[tail : tail + far]


class Stencil:
    def __init__(self, tiles, rows, width, viscosity, faces, thrust, start, beside):
        self.tiles, self.rows, self.width, self.beside = (tiles, rows, width, beside)
        self.viscosity, self.faces, self.thrust, self.start = (viscosity, faces, thrust, start)
        row = lax.broadcasted_iota(jnp.int32, (rows, width), 0)
        self.top = row == rows - 1
        self.bottom = row == 0

    def next_y(self, f):
        half = self.width // 2
        return jnp.concatenate([f[:, half:], pltpu.roll(f[:, :half], half - 1, 1)], axis=1)

    def last_y(self, f):
        half = self.width // 2
        return jnp.concatenate([pltpu.roll(f[:, half:], 1, 1), f[:, :half]], axis=1)

    def next_z(self, parts, t):
        if t < self.tiles - 1:
            return parts[t + 1]
        return jnp.where(self.top, 0.0, pltpu.roll(parts[0], self.rows - 1, 0))

    def last_z(self, parts, t):
        if t > 0:
            return parts[t - 1]
        return jnp.where(self.bottom, 0.0, pltpu.roll(parts[self.tiles - 1], 1, 0))

    def set_viscosity(self, now, first, count):
        tiles = self.tiles

        def column(n, carry):
            i = first + n
            here = [[now[i, c, t] for t in range(tiles)] for c in range(3)]
            found, sides = [], []
            for t in range(tiles):
                d_x = [now[i + 1, c, t] - now[i - 1, c, t] for c in range(3)]
                after_y = [self.next_y(f[t]) for f in here]
                sides.append(after_y)
                d_y = [a - self.last_y(f[t]) for a, f in zip(after_y, here)]
                d_z = [self.next_z(f, t) - self.last_z(f, t) for f in here]
                diagonal = d_x[0] * d_x[0] + d_y[1] * d_y[1] + d_z[2] * d_z[2]
                xy = d_x[1] + d_y[0]
                xz = d_x[2] + d_z[0]
                yz = d_y[2] + d_z[1]
                total = (diagonal + diagonal) + (xy * xy + xz * xz + yz * yz)
                root = total * lax.rsqrt(jnp.maximum(total, SMALLEST))
                found.append((0.5 * SMAG_COEFF) * root)
            for t in range(tiles):
                self.viscosity[i, t] = found[t]
                for c in range(3):
                    self.beside[i, c, t] = sides[t][c]
            return carry

        lax.fori_loop(0, count, column, 0, unroll=4 if count % 4 == 0 else 6)

    def face(self, both, here, after, lead):
        low = both + here[lead]
        high = both - after[lead]
        return [after[c] * high - here[c] * low for c in range(3)]

    def face_x(self, now, i, t):
        here = [now[i, c, t] for c in range(3)]
        after = [now[i + 1, c, t] for c in range(3)]
        return self.face(self.viscosity[i, t] + self.viscosity[i + 1, t], here, after, 0)

    def advance(self, now, then, first, count, keep, gain):
        tiles, scale = self.tiles, 0.5 * TIME_STEP * gain
        for t in range(tiles):
            for c, f in enumerate(self.face_x(now, first - 1, t)):
                self.faces[c, t] = f

        def column(n, carry):
            i = first + n
            eddy = [self.viscosity[i, t] for t in range(tiles)]
            field = [[now[i, c, t] for t in range(tiles)] for c in range(3)]

            def face_z(t):
                here = [f[t] for f in field]
                after = [self.next_z(f, t) for f in field]
                return self.face(eddy[t] + self.next_z(eddy, t), here, after, 2)

            last = face_z(tiles - 1)
            floor = eddy[0] - field[2][0]
            below = [
                jnp.where(self.bottom, field[c][0] * floor, pltpu.roll(last[c], 1, 0))
                for c in range(3)
            ]
            ahead_of = [self.face_x(now, i, t) for t in range(tiles)]
            before_of = [[self.faces[c, t] for c in range(3)] for t in range(tiles)]
            found = []
            for t in range(tiles):
                here = [f[t] for f in field]
                above = last if t == tiles - 1 else face_z(t)
                ahead, before = ahead_of[t], before_of[t]
                beside = [self.beside[i, c, t] for c in range(3)]
                side = self.face(eddy[t] + self.next_y(eddy[t]), here, beside, 1)
                for c in range(3):
                    change = (
                        (ahead[c] - before[c])
                        + (side[c] - self.last_y(side[c]))
                        + (above[c] - below[c])
                    )
                    if c == 0:
                        drag = self.thrust[i - 2, t] * here[0] * jnp.abs(here[0])
                        change = change + (2.0 * DRIVING_FORCE - drag)
                    if keep == 0.0:
                        found.append(here[c] + scale * change)
                    else:
                        found.append(keep * self.start[i, c, t] + gain * here[c] + scale * change)
                below = above
            for t in range(tiles):
                for c in range(3):
                    then[i, c, t] = found[3 * t + c]
                    self.faces[c, t] = ahead_of[t][c]
            return carry

        lax.fori_loop(0, count, column, 0, unroll=2)

    def stage(self, number, now, then, first, count):
        keep, gain = ((0.0, 1.0), (0.75, 0.25), (1.0 / 3.0, 2.0 / 3.0))[number]
        self.set_viscosity(now, first - 1, count + 2)
        self.advance(now, then, first, count, keep, gain)


def place_columns(start, runs_of):
    half = start.shape[-1] // 2
    front = lax.broadcasted_iota(jnp.int32, start.shape[-2:-1] + (half,), 1) < half // 2
    core = lax.axis_index("gy")
    odd = lax.axis_index("gx") % 2

    def copy(side, parity):
        for first, here, there, begin, count in runs_of(side, parity):
            low, high = (here, there) if side == 0 else (there, here)
            for n in range(count):
                for c in range(start.shape[1]):
                    for t in range(start.shape[2]):
                        a, b = low[begin + n, c, t], high[begin + n, c, t]
                        start[first + n, c, t, :, :half] = jnp.where(front, a, b)
                        start[first + n, c, t, :, half:] = pltpu.roll(
                            jnp.where(front, b, a), half // 2, 1
                        )

    for side in range(2):
        for parity in range(2):
            chosen = jnp.logical_and(core == side, odd == parity)
            pl.when(chosen)(functools.partial(copy, side, parity))


def near_kernel(
    own_here,
    own_there,
    across_here,
    across_there,
    around_here,
    around_there,
    thrust,
    first,
    second,
    third,
    start,
    stage_a,
    stage_b,
    viscosity,
    faces,
    beside,
):
    cells_x = own_here.shape[0]
    near = across_here.shape[0]
    _, _, tiles, rows, width = start.shape
    core = lax.axis_index("gy")

    def runs_of(side, parity):
        across, around = (across_here, across_there), (around_here, around_there)
        left, right = (around, across) if parity == 0 else (across, around)
        return (
            (0, *left, 0, near),
            (near, own_here, own_there, 0, cells_x),
            (near + cells_x, *right, 0, near),
        )

    place_columns(start, runs_of)
    stencil = Stencil(tiles, rows, width, viscosity, faces, thrust, start, beside)
    columns = start.shape[0]
    stencil.stage(0, start, stage_a, 2, columns - 4)
    stencil.stage(1, stage_a, stage_b, 4, columns - 8)
    first[...] = stage_a[pl.ds(2 + core * (columns - 8), 4)]
    second[...] = stage_b[pl.ds(4 + core * (columns - 12), 4)]
    stencil.stage(2, stage_b, stage_a, 6, columns - 12)
    third[...] = stage_a[pl.ds(6, columns - 12)]


def far_kernel(
    total_x,
    fringe,
    own_here,
    own_there,
    across_here,
    across_there,
    around_here,
    around_there,
    far_here,
    far_there,
    first,
    second,
    third,
    thrust,
    piece_here,
    piece_there,
    source,
    start,
    stage_a,
    stage_b,
    stage_c,
    viscosity,
    faces,
    beside,
    columns_here,
    columns_there,
):
    cells_x = own_here.shape[0]
    near, far = across_here.shape[0], far_here.shape[0]
    _, _, tiles, rows, width = start.shape
    half = width // 2
    share_x = cells_x // 2
    inner = share_x + 1
    core = lax.axis_index("gy")

    def runs_of(side, parity):
        across, around = (across_here, across_there), (around_here, around_there)
        if side == 0:
            return (
                (0, far_here, far_there, 0, far),
                (far, *(around if parity == 0 else across), 0, near),
                (far + near, own_here, own_there, 0, inner),
            )
        return (
            (0, own_here, own_there, cells_x - inner, inner),
            (inner, *(across if parity == 0 else around), 0, near),
            (inner + near, far_here, far_there, 0, far),
        )

    place_columns(start, runs_of)
    stencil = Stencil(tiles, rows, width, viscosity, faces, thrust, start, beside)
    stencil.stage(0, start, stage_a, 2 + 4 * core, 4)
    stage_a[pl.ds(6 - 4 * core, 4)] = first[...]
    stencil.stage(1, stage_a, stage_b, 4, 4)
    stage_b[pl.ds(8 - 8 * core, 4)] = second[...]
    stencil.stage(2, stage_b, stage_c, 6 - 4 * core, 4)
    stage_c[pl.ds(10 - 10 * core, 2)] = third[...]

    origin = REACH - core * (REACH - 1)
    pairs = 3 * tiles // 2
    front = lax.broadcasted_iota(jnp.int32, (rows, half), 1) < half // 2
    for x in range(share_x):
        for c in range(3):
            for t in range(tiles):
                n = c * tiles + t
                field = stage_c[origin + x, c, t]
                even, odd = field[:, :half], pltpu.roll(field[:, half:], half // 2, 1)
                low, high = jnp.where(front, even, odd), jnp.where(front, odd, even)
                spot = pl.ds((((n % 2) * share_x + x) * pairs + n // 2) * rows, rows)
                columns_here[spot, :] = jnp.where(core == 0, low, high)
                columns_there[spot, :] = jnp.where(core == 0, high, low)
    for s in range(rows):
        for m in range(pairs):
            spot = pl.ds(m * rows + s, 2 * share_x, stride=pairs * rows)
            piece_here[s, m] = columns_here[spot, :]
            piece_there[s, m] = columns_there[spot, :]

    is_farm = lax.axis_index("sec") == 1
    corner = lax.axis_index("gx") * cells_x + core * share_x

    def weight(offset, dest):
        place = lax.rem(corner + offset + total_x, total_x)
        inside = jnp.logical_and(place >= fringe[0], place < fringe[1])
        blend = jnp.where(inside, FRINGE_BLEND, 0.0)
        share = jnp.where(is_farm, 1.0 - blend, blend)
        if dest == 0:
            share = jnp.where(is_farm, 0.0, 1.0)
        return 0.5 * share

    for x in range(share_x):
        i = origin + x
        upright = [stage_c[i, 2, t] for t in range(tiles)]
        for t in range(tiles):
            cross = stage_c[i, 1, t]
            plane = (stencil.next_y(cross) - stencil.last_y(cross)) + (
                stencil.next_z(upright, t) - stencil.last_z(upright, t)
            )
            after, before = stage_c[i + 1, 0, t], stage_c[i - 1, 0, t]
            for dest in range(2):
                source[pl.ds(((dest * share_x + x) * tiles + t) * rows, rows), :] = (
                    weight(x + 1, dest) * after
                    - weight(x - 1, dest) * before
                    + weight(x, dest) * plane
                )


def spectra_kernel(source, table_y, table_z, spectra, modes):
    _, groups, _, parts, rows, lanes = spectra.shape
    levels = table_z.shape[0]
    count, total_y = source.shape
    columns = count // levels
    along_y = dot(source[...], table_y[...])
    beside = [along_y[n * levels : (n + 1) * levels] for n in range(columns)]
    both = dot(table_z[...], jnp.concatenate(beside, axis=1))
    for n in range(columns):
        for h in range(2):
            first = n * total_y + h * lanes
            modes[h, pl.ds(n * levels, levels), :] = both[:, first : first + lanes]
    for dest in range(2):
        for h in range(2):
            for p in range(parts):
                first = dest * count // 2 + p * groups
                picked = [
                    modes[h, pl.ds(first + b, rows, stride=levels // 2), :] for b in range(groups)
                ]
                for g, block in enumerate(swap_blocks(picked, lanes // groups)):
                    spectra[dest, g, h, p] = block


def arrange_kernel(piece_here, piece_there, *blocks):
    groups, pairs, rows, lanes = piece_here.shape
    half = rows // 2
    low = lax.broadcasted_iota(jnp.int32, (rows, lanes), 0) < half
    is_first = lax.axis_index("gy") == 0
    order = parting(lanes, inverse=True)
    for distance, block in enumerate(blocks):
        g = lax.axis_index("gx") ^ distance
        merged = []
        for m in range(pairs):
            here, there = piece_here[g, m], piece_there[g, m]
            before = jnp.where(is_first, here, there)
            after = jnp.where(is_first, there, here)
            merged.append(jnp.where(low, before, pltpu.roll(after, half, 0)))
            merged.append(jnp.where(low, pltpu.roll(before, half, 0), after))
        values = reordered(jnp.concatenate(merged, axis=0), order)
        block[...] = values.reshape(block.shape)


def pencil_kernel(received, waves, table, packed):
    _, groups, cores, parts, rows, lanes = received.shape
    total_x = groups * rows
    lane_width = lanes // groups
    wave, base = 2 * total_x, table.shape[1]
    spread_z = table[:base]
    pair_x = table[base : base + wave, :wave]
    table_x = table[base : base + total_x, wave : wave + total_x]
    along_x = table[base : base + total_x, 2 * wave : 2 * wave + lanes]
    along_zy = waves[lax.axis_index("gx"), lax.axis_index("gy")]
    spectrum = jnp.concatenate(
        [(received[0, :, :, p] + received[1, :, :, p]).reshape(-1, lanes) for p in range(parts)],
        axis=1,
    )
    solved = dot(pair_x, spectrum)
    pieces = []
    for a in range(2 * parts):
        p, side = a % parts, a // parts
        block = solved[side * total_x : (side + 1) * total_x, p * lanes : (p + 1) * lanes]
        pieces.append(block / (along_x + along_zy[a : a + 1]))
    field = dot(dot(table_x, jnp.concatenate(pieces, axis=1)), spread_z)
    levels_of = [field[:, a * lanes : (a + 1) * lanes] for a in range(2 * parts)]
    wide = lax.broadcasted_iota(jnp.int32, (total_x // 2, lanes), 1)
    left = wide < lanes // 2
    quarter = total_x // 4
    block = lax.broadcasted_iota(jnp.int32, (quarter, lanes), 1) // lane_width
    for g in range(groups):
        a, odd = divmod(g, 2)
        now = levels_of[a]
        front, rear = now[: total_x // 2], now[total_x // 2 :]
        if odd:
            main = jnp.where(left, pltpu.roll(front, lanes // 2, 1), rear)
            lower, lower_lane = now, lanes // 2 - lane_width
            upper, upper_lane = levels_of[min(a + 1, 2 * parts - 1)], 0
        else:
            main = jnp.where(left, front, pltpu.roll(rear, lanes // 2, 1))
            lower, lower_lane = levels_of[max(a - 1, 0)], lanes - lane_width
            upper, upper_lane = now, lanes // 2
        edge = None
        for q in range(4):
            for n, (whole, lane) in enumerate(((lower, lower_lane), (upper, upper_lane))):
                spot = 2 * q + n
                move = (spot * lane_width - lane) % lanes
                rolled = whole[q * quarter : (q + 1) * quarter]
                if move:
                    rolled = pltpu.roll(rolled, move, 1)
                edge = rolled if edge is None else jnp.where(block == spot, rolled, edge)
        packed[g, : total_x // 2] = main
        packed[g, total_x // 2 : 3 * quarter] = edge


def project_kernel(received, partner, table_y, blended, velocity_next, pressure):
    groups = received.shape[0]
    share, total_x, lanes = pressure.shape
    cells_x = total_x // groups
    width = lanes // groups
    place, core = lax.axis_index("gx"), lax.axis_index("gy")
    main_rows = total_x // 2
    rows = partner.shape[1]

    def levels_in(arrays):
        main = swap_blocks([arrays[s, :main_rows] for s in range(groups)], width)
        edge = swap_blocks([arrays[s, main_rows:rows] for s in range(groups)], width)
        inner = [jnp.concatenate([main[n], main[share + n]], axis=0) for n in range(share)]
        outer = [jnp.concatenate([edge[2 * q + n] for q in range(4)], axis=0) for n in range(2)]
        return [outer[0]] + inner + [outer[1]]

    here, there = levels_in(received), levels_in(partner)
    here, there = jnp.concatenate(here, axis=0), jnp.concatenate(there, axis=0)
    low = jnp.where(core == 0, here, there)
    high = jnp.where(core == 0, there, here)
    both = dot(jnp.concatenate([low, high], axis=1), table_y[core])
    fields = [both[n * total_x : (n + 1) * total_x] for n in range(share + 2)]
    values = [f[:, :lanes] for f in fields]
    values[0] = jnp.where(place == 0, values[1], values[0])
    values[-1] = jnp.where(place == groups - 1, -values[-2], values[-1])
    for z in range(share):
        now = values[z + 1]
        pressure[z] = now
        slopes = [
            0.5 * (pltpu.roll(now, total_x - 1, 0) - pltpu.roll(now, 1, 0)),
            fields[z + 1][:, lanes:],
            0.5 * (values[z + 2] - values[z]),
        ]
        for c in range(3):
            velocity_next[c, z] = blended[c, z] - slopes[c]


def blend_kernel(fringe, moved, upstream, blended):
    _, share, total_x, lanes = blended.shape
    groups, _, cells_x, _ = moved.shape
    outlet = upstream.shape[0]
    is_farm = lax.axis_index("sec") == 1
    for s in range(groups):
        distance = lax.axis_index("gx") ^ s
        columns = s * cells_x + lax.broadcasted_iota(jnp.int32, (cells_x, lanes), 0)
        inside = jnp.logical_and(columns >= fringe[0], columns < fringe[1])
        blend = jnp.where(jnp.logical_and(inside, is_farm), FRINGE_BLEND, 0.0)
        for c in range(3):
            for z in range(share):
                own = moved[distance, c * share + z]
                if s >= groups - outlet:
                    own = own + blend * (upstream[s - groups + outlet, c * share + z] - own)
                blended[c, z, s * cells_x : (s + 1) * cells_x] = own


def cas(rows, columns, length):
    angle = (np.outer(rows, columns) % length) * (2.0 * np.pi / length)
    return np.cos(angle) + np.sin(angle)


def tables(levels, total_x, total_y, groups):
    half = total_y // 2
    lane_width = LANES // groups
    every_x = np.arange(total_x)
    every_y = np.arange(total_y)
    table_x = cas(every_x, every_x, total_x)
    table_y = cas(every_y, every_y, total_y)
    slope_y = 0.5 * (np.roll(table_y, -1, axis=1) - np.roll(table_y, 1, axis=1))
    level = np.arange(levels) + 0.5
    table_z = np.cos(np.outer(level, level) * (np.pi / levels))
    spread_z = np.kron(table_z, np.eye(lane_width))
    order = np.arange(levels).reshape(ROWS, levels // ROWS).T.reshape(levels)
    parted = np.concatenate([every_y[::2], every_y[1::2]])
    backward = [
        np.concatenate([table_y[:, here], slope_y[:, here]], axis=1)
        for here in (slice(0, half), slice(half, total_y))
    ]
    pair_x = np.einsum("kx,ab->akxb", table_x, np.eye(2)).reshape(2 * total_x, 2 * total_x)
    norm = levels / 2.0 * total_x * total_y
    wave_x = norm * (2.0 * np.cos(every_x * (2.0 * np.pi / total_x)) - 2.0)
    wave_y = norm * (2.0 * np.cos(every_y * (2.0 * np.pi / total_y)) - 2.0)
    wave_z = norm * (2.0 * np.cos(level * (np.pi / levels)) - 2.0)
    waves = wave_z.reshape(1, 1, -1, groups, 1) + wave_y.reshape(2, groups, 1, 1, lane_width)
    waves = waves.transpose(1, 0, 2, 3, 4).reshape(groups, 2, levels // groups, LANES)
    pencil = np.zeros((spread_z.shape[0] + 2 * total_x, spread_z.shape[1]))
    pencil[: spread_z.shape[0]] = spread_z
    pencil[spread_z.shape[0] :, : 2 * total_x] = pair_x
    pencil[spread_z.shape[0] : -total_x, 2 * total_x : 3 * total_x] = table_x
    pencil[spread_z.shape[0] : -total_x, 4 * total_x : 4 * total_x + LANES] = wave_x[:, None]
    return [
        jnp.asarray(t, jnp.float32)
        for t in (
            pencil,
            table_y[parted],
            np.stack(backward),
            table_z[:, order],
            waves,
        )
    ]


def call(kernel, out_shapes, scratch, *operands):
    in_specs = [
        pl.BlockSpec(memory_space=pltpu.SMEM if o.dtype == jnp.int32 else pltpu.VMEM)
        for o in operands
    ]
    return pl.pallas_call(
        kernel,
        out_shape=out_shapes,
        in_specs=in_specs,
        out_specs=jax.tree.map(lambda _: pl.BlockSpec(memory_space=pltpu.VMEM), out_shapes),
        scratch_shapes=scratch,
        compiler_params=pltpu.CompilerParams(vmem_limit_bytes=VMEM_BYTES),
    )(*operands)


def thrust_weights(turbine_cells, along_x, along_y, along_z, total_y, strength):
    matches = (along_x[:, None] == turbine_cells[None, :, 0]).astype(jnp.bfloat16)
    offset_y = (along_y[None, :] - turbine_cells[:, 1:2] + total_y // 2) % total_y - total_y // 2
    offset_z = along_z[None, :] - turbine_cells[:, 2:3]
    distance = (
        offset_z[:, :, None] * offset_z[:, :, None] + offset_y[:, None, :] * offset_y[:, None, :]
    )
    inside = (distance <= RADIUS * RADIUS).astype(jnp.bfloat16)
    count = jnp.einsum("xt,tzy->xzy", matches, inside, preferred_element_type=jnp.float32)
    return strength * count


def paired_plan(velocity, turbine_cells, fringe_bounds):
    groups = lax.axis_size("gx")
    initial = velocity[0]
    _, levels, cells_x, cells_y = initial.shape
    total_x, total_y = cells_x * groups, 2 * cells_y
    share, share_x = levels // ROWS, cells_x // 2
    section, place, core = (lax.axis_index("sec"), lax.axis_index("gx"), lax.axis_index("gy"))
    pencil, table_y, backward, table_z, waves = tables(levels, total_x, total_y, groups)

    near, far = REACH - 4, 4
    up = [(i, (i + 1) % groups) for i in range(groups)]
    down = [(j, i) for i, j in up]
    swap = [(0, 1), (1, 0)]
    straight = [(2 * i, 2 * j) for i, j in up] + [(2 * j + 1, 2 * i + 1) for i, j in up]
    crossed = [(2 * i + 1, 2 * j) for i, j in up] + [(2 * j, 2 * i + 1) for i, j in up]
    pairs_across = [(i, i ^ 1) for i in range(groups)]
    pairs_around = [(i, (i - 1 if i % 2 == 0 else i + 1) % groups) for i in range(groups)]
    f32 = jnp.float32
    flat = initial.reshape(-1, cells_y)

    def narrow(count):
        return jax.ShapeDtypeStruct((count, 3, share, ROWS, cells_y), f32)

    lower, upper = call(
        functools.partial(pack_near_kernel, cells_x), [narrow(near)] * 2, [], flat
    )
    around = lax.ppermute(lower, "gx", pairs_around)
    across = lax.ppermute(upper, "gx", pairs_across)
    own, same, other = call(
        pack_kernel, [narrow(cells_x), narrow(far), narrow(far)], [], flat
    )
    own_there = lax.ppermute(own, "gy", swap)
    other, across = lax.optimization_barrier((other, across))
    far_there = lax.ppermute(other, ("gx", "gy"), crossed)
    across_there = lax.ppermute(across, "gy", swap)
    around_there = lax.ppermute(around, "gy", swap)

    strength = 2.0 * THRUST_COEFF * section.astype(jnp.float32)
    along_z = jnp.arange(levels).reshape(ROWS, share).T.reshape(levels)
    along_y = jnp.arange(total_y).reshape(cells_y, 2).T.reshape(total_y)

    def thrust_on(offset, count):
        along_x = (place * cells_x + offset + jnp.arange(count) + total_x) % total_x
        weights = thrust_weights(
            turbine_cells, along_x, along_y, along_z, total_y, strength
        )
        return weights.reshape(count, share, ROWS, total_y)

    near_thrust = thrust_on(2 - near, cells_x + 2 * near - 4)
    far_thrust = thrust_on((2 - REACH) * (1 - core) + (share_x + 1) * core, far + near + share_x - 3)
    far_here = lax.ppermute(same, ("gx", "gy"), straight)
    body = (3, share, ROWS, total_y)

    def columns(count):
        return pltpu.VMEM((count,) + body, f32)

    reached = cells_x + 2 * near
    shapes = [jax.ShapeDtypeStruct((n,) + body, f32) for n in (4, 4, reached - 12)]
    first, second, third = call(
        near_kernel,
        shapes,
        [columns(reached)] * 3
        + [pltpu.VMEM((reached,) + body[1:], f32), pltpu.VMEM(body, f32), columns(reached)],
        own,
        own_there,
        across,
        across_there,
        around,
        around_there,
        near_thrust,
    )
    window = far + near + share_x + 1
    pairs = 3 * share // 2
    piece = jax.ShapeDtypeStruct((ROWS, pairs, 2 * share_x, cells_y), f32)
    parts = levels // (2 * groups)
    piece_here, piece_send, source = call(
        functools.partial(far_kernel, total_x),
        [piece, piece, jax.ShapeDtypeStruct((2 * share_x * levels, total_y), f32)],
        [columns(window)] * 4
        + [
            pltpu.VMEM((window,) + body[1:], f32),
            pltpu.VMEM(body, f32),
            columns(window),
            pltpu.VMEM((share_x * 3 * levels, cells_y), f32),
            pltpu.VMEM((share_x * 3 * levels, cells_y), f32),
        ],
        fringe_bounds,
        own,
        own_there,
        across,
        across_there,
        around,
        around_there,
        far_here,
        far_there,
        first,
        second,
        third,
        far_thrust,
    )
    piece_there = lax.ppermute(piece_send, "gy", swap)
    spectra = call(
        spectra_kernel,
        jax.ShapeDtypeStruct((2, groups, 2, parts, 2 * share_x, LANES), f32),
        [pltpu.VMEM((2, 2 * share_x * levels, LANES), f32)],
        source,
        table_y,
        table_z,
    )
    received = lax.all_to_all(
        spectra.reshape((4 * groups,) + spectra.shape[3:]), ("sec", "gx", "gy"), 0, 0, tiled=True
    ).reshape(spectra.shape)
    blocks = call(
        arrange_kernel,
        [jax.ShapeDtypeStruct((3 * share, cells_x, cells_y), f32)] * groups,
        [],
        piece_here,
        piece_there,
    )
    moved = [blocks[0]] + [
        lax.ppermute(block, "gx", [(i, i ^ d) for i in range(groups)])
        for d, block in enumerate(blocks)
        if d
    ]
    packed = call(
        pencil_kernel,
        jax.ShapeDtypeStruct((groups, 3 * total_x // 4, LANES), f32),
        [],
        received,
        waves,
        pencil,
    )
    tied = [3, 4, 5]
    packed, *some = lax.optimization_barrier([packed] + [moved[d] for d in tied])
    for d, block in zip(tied, some):
        moved[d] = block
    moved = jnp.stack(moved)
    outlet = groups // 4
    leaving = jnp.stack(
        [
            lax.dynamic_index_in_dim(moved, place ^ s, 0, keepdims=False)
            for s in range(groups - outlet, groups)
        ]
    )
    upstream = lax.ppermute(leaving, "sec", [(0, 1)])
    returned = lax.all_to_all(packed, "gx", 0, 0, tiled=True)
    returned, upstream = lax.optimization_barrier((returned, upstream))
    partner = lax.ppermute(returned, "gy", swap)
    blended = call(
        blend_kernel,
        jax.ShapeDtypeStruct((3, share, total_x, cells_y), f32),
        [],
        fringe_bounds,
        moved,
        upstream,
    )
    velocity_next, pressure = call(
        project_kernel,
        [
            jax.ShapeDtypeStruct((3, share, total_x, cells_y), f32),
            jax.ShapeDtypeStruct((share, total_x, cells_y), f32),
        ],
        [],
        returned,
        partner,
        backward,
        blended,
    )
    return (velocity_next[None], pressure[None])


def on_device(velocity, turbine_cells, fringe_bounds):
    groups = lax.axis_size("gx")
    _, _, levels, cells_x, cells_y = velocity.shape
    paired = (
        lax.axis_size("gy") == 2
        and lax.axis_size("sec") == 2
        and cells_y == LANES
        and cells_x == ROWS
        and groups == ROWS
        and 2 * levels == groups * groups
    )
    plan = paired_plan if paired else general_plan
    return plan(velocity, turbine_cells, fringe_bounds)


def solution(mesh):
    return jax.shard_map(
        on_device,
        mesh=mesh,
        in_specs=(P("sec", None, None, "gx", "gy"), P(), P()),
        out_specs=(P("sec", None, "gx", None, "gy"), P("sec", "gx", None, "gy")),
        check_vma=False,
    )
```

```python
import functools

import jax
import jax.numpy as jnp
import numpy as np
from jax import lax
from jax.experimental import pallas as pl
from jax.experimental.pallas import tpu as pltpu
from jax.sharding import PartitionSpec as P

RADIUS = 4


TIME_STEP = 0.05
SMAG_COEFF = 0.1
THRUST_COEFF = 4.0
DRIVING_FORCE = 0.1
FRINGE_BLEND = 0.5
HIGHEST = lax.Precision.HIGHEST
STAGES = 3
REACH = 2 * STAGES + 1
LANES = 128
SMALLEST = float(np.finfo(np.float32).tiny)
ROWS = 8
VMEM_BYTES = 20 * 1024 * 1024


def extended(x, sides, width):
    for axis, dim in sides:
        count, length = (lax.axis_size(axis), x.shape[dim])
        up = [(i, (i + 1) % count) for i in range(count)]
        down = [(j, i) for i, j in up]
        last = lax.slice_in_dim(x, length - width, length, axis=dim)
        initial = lax.slice_in_dim(x, 0, width, axis=dim)
        before = lax.ppermute(last, axis, up)
        after = lax.ppermute(initial, axis, down)
        x = jnp.concatenate([before, x, after], axis=dim)
    return x


def shifted(block, axis, distance):
    devices = range(lax.axis_size(axis))
    route = [(i - distance, i) for i in devices if i - distance in devices]
    return lax.ppermute(block, axis, route)


def cas_table(row_index, column_index, length):
    product = row_index[:, None] * column_index[None, :] % length
    angle = product.astype(jnp.float32) * (2.0 * jnp.pi / length)
    return jnp.cos(angle) + jnp.sin(angle)


def shift_up(values):
    zeros = jnp.zeros_like(values[..., :1, :, :])
    return jnp.concatenate([values[..., 1:, :, :], zeros], axis=-3)


def shift_down(values):
    zeros = jnp.zeros_like(values[..., :1, :, :])
    return jnp.concatenate([zeros, values[..., :-1, :, :]], axis=-3)


def thomas(right_side, eigen_value):
    length = right_side.shape[0]
    inverses = []
    reduced = []
    for level_index in range(length):
        if level_index == 0:
            diagonal = eigen_value - 1.0
        elif level_index == length - 1:
            diagonal = eigen_value - 3.0
        else:
            diagonal = eigen_value - 2.0
        if level_index == 0:
            pivot_now = diagonal
            current = right_side[0] / pivot_now
        else:
            pivot_now = diagonal - inverses[-1]
            current = (right_side[level_index] - reduced[-1]) / pivot_now
        inverses.append(1.0 / pivot_now)
        reduced.append(current)
    solution = [reduced[-1]]
    for level_index in range(length - 2, -1, -1):
        solution.append(reduced[level_index] - inverses[level_index] * solution[-1])
    return jnp.stack(solution[::-1])


def spanwise_derivative(values, sine_y):
    return -sine_y * jnp.roll(jnp.flip(values, axis=-1), 1, axis=-1)


def widened(values):
    return extended(values, (("gx", 1), ("gy", 2)), 1)


def disk_weights(turbine_cells, along_x, along_y, along_z, total_y):
    matches = (along_x[:, None] == turbine_cells[None, :, 0]).astype(jnp.float32)
    offset_y = (along_y[None, :] - turbine_cells[:, 1:2] + total_y // 2) % total_y - total_y // 2
    offset_z = along_z[None, :] - turbine_cells[:, 2:3]
    distance = (
        offset_z[:, :, None] * offset_z[:, :, None] + offset_y[:, None, :] * offset_y[:, None, :]
    )
    inside = (distance <= RADIUS * RADIUS).astype(jnp.float32)
    return jnp.einsum("xt,tzy->zxy", matches, inside, precision=HIGHEST)


def tendency(velocity_now, farm_flag, disk_weight):
    levels, cells_x, cells_y = (velocity_now.shape[1], velocity_now.shape[2], velocity_now.shape[3])
    border = widened(velocity_now.reshape(3 * levels, cells_x, cells_y)).reshape(
        3, levels, cells_x + 2, cells_y + 2
    )
    plus_x = border[:, :, 2:, 1:-1]
    minus_x = border[:, :, :-2, 1:-1]
    plus_y = border[:, :, 1:-1, 2:]
    minus_y = border[:, :, 1:-1, :-2]
    plus_z = shift_up(velocity_now)
    minus_z = shift_down(velocity_now)
    gradients = [0.5 * (plus_x - minus_x), 0.5 * (plus_y - minus_y), 0.5 * (plus_z - minus_z)]
    strain_squares = jnp.zeros_like(velocity_now[0])
    for component in range(3):
        strain_squares = (
            strain_squares + gradients[component][component] * gradients[component][component]
        )
        for direction in range(component + 1, 3):
            shear = 0.5 * (gradients[direction][component] + gradients[component][direction])
            strain_squares = strain_squares + 2.0 * shear * shear
    viscosity = SMAG_COEFF * jnp.sqrt(2.0 * strain_squares)
    visc_border = widened(viscosity)
    visc_plus_x = visc_border[:, 2:, 1:-1]
    visc_minus_x = visc_border[:, :-2, 1:-1]
    visc_plus_y = visc_border[:, 1:-1, 2:]
    visc_minus_y = visc_border[:, 1:-1, :-2]
    visc_plus_z = shift_up(viscosity)
    visc_minus_z = shift_down(viscosity)
    advection = 0.5 * (plus_x[0] * plus_x - minus_x[0] * minus_x)
    advection = advection + 0.5 * (plus_y[1] * plus_y - minus_y[1] * minus_y)
    advection = advection + 0.5 * (plus_z[2] * plus_z - minus_z[2] * minus_z)
    diffusion = 0.5 * (viscosity + visc_plus_x) * (plus_x - velocity_now) - 0.5 * (
        viscosity + visc_minus_x
    ) * (velocity_now - minus_x)
    diffusion = (
        diffusion
        + 0.5 * (viscosity + visc_plus_y) * (plus_y - velocity_now)
        - 0.5 * (viscosity + visc_minus_y) * (velocity_now - minus_y)
    )
    diffusion = (
        diffusion
        + 0.5 * (viscosity + visc_plus_z) * (plus_z - velocity_now)
        - 0.5 * (viscosity + visc_minus_z) * (velocity_now - minus_z)
    )
    changes = diffusion - advection
    streamwise = DRIVING_FORCE - THRUST_COEFF * farm_flag * disk_weight * velocity_now[0] * jnp.abs(
        velocity_now[0]
    )
    return jnp.concatenate([changes[:1] + streamwise[None], changes[1:]], axis=0)


def general_plan(velocity, turbine_cells, fringe_bounds):
    initial = velocity[0]
    levels, cells_x, cells_y = (initial.shape[1], initial.shape[2], initial.shape[3])
    total_y = cells_y * lax.axis_size("gy")
    x_anchor = lax.axis_index("gx") * cells_x
    y_anchor = lax.axis_index("gy") * cells_y
    farm_flag = lax.axis_index("sec").astype(jnp.float32)
    along_x = x_anchor + jnp.arange(cells_x, dtype=jnp.int32)
    along_y = y_anchor + jnp.arange(cells_y, dtype=jnp.int32)
    along_z = jnp.arange(levels, dtype=jnp.int32)
    disk_weight = disk_weights(turbine_cells, along_x, along_y, along_z, total_y)
    segment_one = initial + TIME_STEP * tendency(initial, farm_flag, disk_weight)
    segment_two = 0.75 * initial + 0.25 * (
        segment_one + TIME_STEP * tendency(segment_one, farm_flag, disk_weight)
    )
    segment_three = initial / 3.0 + 2.0 / 3.0 * (
        segment_two + TIME_STEP * tendency(segment_two, farm_flag, disk_weight)
    )
    regrouped = lax.all_to_all(segment_three, "gx", split_axis=1, concat_axis=2, tiled=True)
    count_x = regrouped.shape[2]
    quarter = count_x // 4
    cut_at = count_x - quarter
    outlet_part = regrouped[:, :, cut_at:, :]
    upstream = shifted(outlet_part, "sec", 1)
    columns = cut_at + jnp.arange(quarter, dtype=jnp.int32)
    inside = ((columns >= fringe_bounds[0]) & (columns < fringe_bounds[1])).astype(jnp.float32)
    weight = FRINGE_BLEND * farm_flag * inside
    blended_part = outlet_part + weight[:, None] * (upstream - outlet_part)
    regrouped = jnp.concatenate([regrouped[:, :, :cut_at, :], blended_part], axis=2)
    index_x = jnp.arange(count_x, dtype=jnp.int32)
    table_x = cas_table(index_x, index_x, count_x)
    gradient_u = 0.5 * (jnp.roll(regrouped[0], -1, axis=1) - jnp.roll(regrouped[0], 1, axis=1))
    fields = jnp.stack([gradient_u, regrouped[1], regrouped[2]])
    spectral_x = jnp.einsum("kx,czxy->czky", table_x, fields, precision=HIGHEST)
    columns_view = lax.all_to_all(
        lax.all_to_all(spectral_x, "gx", split_axis=2, concat_axis=1, tiled=True),
        "gy",
        split_axis=2,
        concat_axis=3,
        tiled=True,
    )
    slice_width = columns_view.shape[2]
    count_y = columns_view.shape[3]
    index_y = jnp.arange(count_y, dtype=jnp.int32)
    table_y = cas_table(index_y, index_y, count_y)
    spectrum = jnp.einsum("ly,czky->czkl", table_y, columns_view, precision=HIGHEST)
    sine_y = jnp.sin(index_y.astype(jnp.float32) * (2.0 * jnp.pi / count_y))
    source = (
        spectrum[0]
        + spanwise_derivative(spectrum[1], sine_y)
        + 0.5 * (shift_up(spectrum[2]) - shift_down(spectrum[2]))
    )
    wave_x = (
        lax.axis_index("gx") * cells_x
        + lax.axis_index("gy") * slice_width
        + jnp.arange(slice_width, dtype=jnp.int32)
    )
    eigen_value = 2.0 * jnp.cos(wave_x.astype(jnp.float32) * (2.0 * jnp.pi / count_x))[:, None]
    eigen_value = (
        eigen_value
        + 2.0 * jnp.cos(index_y.astype(jnp.float32) * (2.0 * jnp.pi / count_y))[None, :]
        - 4.0
    )
    solved = thomas(source, eigen_value)
    above_level = jnp.concatenate([solved[1:], -solved[-1:]], axis=0)
    below_level = jnp.concatenate([solved[:1], solved[:-1]], axis=0)
    coefficients = jnp.stack(
        [solved, spanwise_derivative(solved, sine_y), 0.5 * (above_level - below_level)]
    )
    physical_y = jnp.einsum("yl,czkl->czky", table_y, coefficients, precision=HIGHEST) * (
        1.0 / count_y
    )
    returned = lax.all_to_all(
        lax.all_to_all(physical_y, "gx", split_axis=1, concat_axis=2, tiled=True),
        "gy",
        split_axis=3,
        concat_axis=2,
        tiled=True,
    )
    group_size = count_x // lax.axis_size("gy")
    wave_back = (
        index_x // slice_width % lax.axis_size("gx") * cells_x
        + index_x // group_size * slice_width
        + index_x % slice_width
    )
    inverse_table = cas_table(index_x, wave_back, count_x)
    physical = jnp.einsum("xp,czpy->czxy", inverse_table, returned, precision=HIGHEST) * (
        1.0 / count_x
    )
    pressure = physical[0]
    gradient_p = 0.5 * (jnp.roll(pressure, -1, axis=1) - jnp.roll(pressure, 1, axis=1))
    velocity_next = regrouped - jnp.stack([gradient_p, physical[1], physical[2]])
    return (velocity_next[None], pressure[None])


def split(values):
    high = values.astype(jnp.bfloat16)
    low = values - high.astype(jnp.float32)
    return high, low.astype(jnp.bfloat16)


def dot(left, right):
    (a, da), (b, db) = split(left), split(right)

    def product(x, y):
        return jnp.dot(x, y, preferred_element_type=jnp.float32)

    return product(a, b) + (product(a, db) + product(da, b))


def swap_blocks(arrays, width):
    arrays = list(arrays)
    block = lax.broadcasted_iota(jnp.int32, arrays[0].shape, 1) // width
    step = 1
    while step < len(arrays):
        low = (block // step) % 2 == 0
        for index in range(len(arrays)):
            if (index // step) % 2 == 0:
                first, second = arrays[index], arrays[index + step]
                arrays[index] = jnp.where(low, first, pltpu.roll(second, step * width, 1))
                arrays[index + step] = jnp.where(
                    low, pltpu.roll(first, LANES - step * width, 1), second
                )
        step *= 2
    return arrays


def reordered(values, order):
    one = order.astype(jnp.bfloat16)
    high, rest = split(values)
    low = values - high.astype(jnp.float32) - rest.astype(jnp.float32)

    def product(x):
        return jnp.dot(x, one, preferred_element_type=jnp.float32)

    return (product(high) + product(rest)) + product(low.astype(jnp.bfloat16))


def parting(lanes, inverse=False):
    line = lax.broadcasted_iota(jnp.int32, (lanes, lanes), 1 if inverse else 0)
    spot = lax.broadcasted_iota(jnp.int32, (lanes, lanes), 0 if inverse else 1)
    later = jnp.where(spot >= lanes // 2, 1, 0)
    place = 2 * (spot - later * (lanes // 2)) + (later ^ lax.axis_index("gy"))
    return jnp.where(line == place, 1.0, 0.0)


def packed_columns(initial, columns, cells_x, tiles):
    total, lanes = initial.shape
    levels = total // (3 * cells_x)
    rows = levels // tiles
    picked = [
        initial[pl.ds((c * levels + t) * cells_x + x, rows, stride=tiles * cells_x), :]
        for x in columns
        for c in range(3)
        for t in range(tiles)
    ]
    values = reordered(jnp.concatenate(picked, axis=0), parting(lanes))
    return values.reshape(len(columns), 3, tiles, rows, lanes)


def pack_near_kernel(cells_x, initial, lower, upper):
    near, _, tiles, _, _ = lower.shape
    columns = list(range(near)) + list(range(cells_x - near, cells_x))
    values = packed_columns(initial, columns, cells_x, tiles)
    even = lax.axis_index("gx") % 2 == 0

    @pl.when(even)
    def _():
        lower[...] = values[:near]
        upper[...] = values[near:]

    @pl.when(jnp.logical_not(even))
    def _():
        lower[...] = values[near:]
        upper[...] = values[:near]


def pack_kernel(initial, own, same, other):
    cells_x, _, tiles, _, _ = own.shape
    far = same.shape[0]
    tail, head = cells_x - REACH, REACH - far
    values = packed_columns(initial, list(range(cells_x)), cells_x, tiles)
    own[...] = values
    is_first = lax.axis_index("gy") == 0

    @pl.when(is_first)
    def _():
        same[...] = values[tail : tail + far]
        other[...] = values[head : head + far]

    @pl.when(jnp.logical_not(is_first))
    def _():
        same[...] = values[head : head + far]
        other[...] = values[tail : tail + far]


class Stencil:
    def __init__(self, tiles, rows, width, viscosity, faces, thrust, start, beside):
        self.tiles, self.rows, self.width, self.beside = (tiles, rows, width, beside)
        self.viscosity, self.faces, self.thrust, self.start = (viscosity, faces, thrust, start)
        row = lax.broadcasted_iota(jnp.int32, (rows, width), 0)
        self.top = row == rows - 1
        self.bottom = row == 0

    def next_y(self, f):
        half = self.width // 2
        return jnp.concatenate([f[:, half:], pltpu.roll(f[:, :half], half - 1, 1)], axis=1)

    def last_y(self, f):
        half = self.width // 2
        return jnp.concatenate([pltpu.roll(f[:, half:], 1, 1), f[:, :half]], axis=1)

    def next_z(self, parts, t):
        if t < self.tiles - 1:
            return parts[t + 1]
        return jnp.where(self.top, 0.0, pltpu.roll(parts[0], self.rows - 1, 0))

    def last_z(self, parts, t):
        if t > 0:
            return parts[t - 1]
        return jnp.where(self.bottom, 0.0, pltpu.roll(parts[self.tiles - 1], 1, 0))

    def set_viscosity(self, now, first, count):
        tiles = self.tiles

        def column(n, carry):
            i = first + n
            here = [[now[i, c, t] for t in range(tiles)] for c in range(3)]
            found, sides = [], []
            for t in range(tiles):
                d_x = [now[i + 1, c, t] - now[i - 1, c, t] for c in range(3)]
                after_y = [self.next_y(f[t]) for f in here]
                sides.append(after_y)
                d_y = [a - self.last_y(f[t]) for a, f in zip(after_y, here)]
                d_z = [self.next_z(f, t) - self.last_z(f, t) for f in here]
                diagonal = d_x[0] * d_x[0] + d_y[1] * d_y[1] + d_z[2] * d_z[2]
                xy = d_x[1] + d_y[0]
                xz = d_x[2] + d_z[0]
                yz = d_y[2] + d_z[1]
                total = (diagonal + diagonal) + (xy * xy + xz * xz + yz * yz)
                root = total * lax.rsqrt(jnp.maximum(total, SMALLEST))
                found.append((0.5 * SMAG_COEFF) * root)
            for t in range(tiles):
                self.viscosity[i, t] = found[t]
                for c in range(3):
                    self.beside[i, c, t] = sides[t][c]
            return carry

        lax.fori_loop(0, count, column, 0, unroll=4 if count % 4 == 0 else 6)

    def face(self, both, here, after, lead):
        low = both + here[lead]
        high = both - after[lead]
        return [after[c] * high - here[c] * low for c in range(3)]

    def face_x(self, now, i, t):
        here = [now[i, c, t] for c in range(3)]
        after = [now[i + 1, c, t] for c in range(3)]
        return self.face(self.viscosity[i, t] + self.viscosity[i + 1, t], here, after, 0)

    def advance(self, now, then, first, count, keep, gain):
        tiles, scale = self.tiles, 0.5 * TIME_STEP * gain
        for t in range(tiles):
            for c, f in enumerate(self.face_x(now, first - 1, t)):
                self.faces[c, t] = f

        def column(n, carry):
            i = first + n
            eddy = [self.viscosity[i, t] for t in range(tiles)]
            field = [[now[i, c, t] for t in range(tiles)] for c in range(3)]

            def face_z(t):
                here = [f[t] for f in field]
                after = [self.next_z(f, t) for f in field]
                return self.face(eddy[t] + self.next_z(eddy, t), here, after, 2)

            last = face_z(tiles - 1)
            floor = eddy[0] - field[2][0]
            below = [
                jnp.where(self.bottom, field[c][0] * floor, pltpu.roll(last[c], 1, 0))
                for c in range(3)
            ]
            ahead_of = [self.face_x(now, i, t) for t in range(tiles)]
            before_of = [[self.faces[c, t] for c in range(3)] for t in range(tiles)]
            found = []
            for t in range(tiles):
                here = [f[t] for f in field]
                above = last if t == tiles - 1 else face_z(t)
                ahead, before = ahead_of[t], before_of[t]
                beside = [self.beside[i, c, t] for c in range(3)]
                side = self.face(eddy[t] + self.next_y(eddy[t]), here, beside, 1)
                for c in range(3):
                    change = (
                        (ahead[c] - before[c])
                        + (side[c] - self.last_y(side[c]))
                        + (above[c] - below[c])
                    )
                    if c == 0:
                        drag = self.thrust[i - 2, t] * here[0] * jnp.abs(here[0])
                        change = change + (2.0 * DRIVING_FORCE - drag)
                    if keep == 0.0:
                        found.append(here[c] + scale * change)
                    else:
                        found.append(keep * self.start[i, c, t] + gain * here[c] + scale * change)
                below = above
            for t in range(tiles):
                for c in range(3):
                    then[i, c, t] = found[3 * t + c]
                    self.faces[c, t] = ahead_of[t][c]
            return carry

        lax.fori_loop(0, count, column, 0, unroll=2)

    def stage(self, number, now, then, first, count):
        keep, gain = ((0.0, 1.0), (0.75, 0.25), (1.0 / 3.0, 2.0 / 3.0))[number]
        self.set_viscosity(now, first - 1, count + 2)
        self.advance(now, then, first, count, keep, gain)


def place_columns(start, runs_of):
    half = start.shape[-1] // 2
    front = lax.broadcasted_iota(jnp.int32, start.shape[-2:-1] + (half,), 1) < half // 2
    core = lax.axis_index("gy")
    odd = lax.axis_index("gx") % 2

    def copy(side, parity):
        for first, here, there, begin, count in runs_of(side, parity):
            low, high = (here, there) if side == 0 else (there, here)
            for n in range(count):
                for c in range(start.shape[1]):
                    for t in range(start.shape[2]):
                        a, b = low[begin + n, c, t], high[begin + n, c, t]
                        start[first + n, c, t, :, :half] = jnp.where(front, a, b)
                        start[first + n, c, t, :, half:] = pltpu.roll(
                            jnp.where(front, b, a), half // 2, 1
                        )

    for side in range(2):
        for parity in range(2):
            chosen = jnp.logical_and(core == side, odd == parity)
            pl.when(chosen)(functools.partial(copy, side, parity))


def near_kernel(
    own_here,
    own_there,
    across_here,
    across_there,
    around_here,
    around_there,
    thrust,
    first,
    second,
    third,
    start,
    stage_a,
    stage_b,
    viscosity,
    faces,
    beside,
):
    cells_x = own_here.shape[0]
    near = across_here.shape[0]
    _, _, tiles, rows, width = start.shape
    core = lax.axis_index("gy")

    def runs_of(side, parity):
        across, around = (across_here, across_there), (around_here, around_there)
        left, right = (around, across) if parity == 0 else (across, around)
        return (
            (0, *left, 0, near),
            (near, own_here, own_there, 0, cells_x),
            (near + cells_x, *right, 0, near),
        )

    place_columns(start, runs_of)
    stencil = Stencil(tiles, rows, width, viscosity, faces, thrust, start, beside)
    columns = start.shape[0]
    stencil.stage(0, start, stage_a, 2, columns - 4)
    stencil.stage(1, stage_a, stage_b, 4, columns - 8)
    first[...] = stage_a[pl.ds(2 + core * (columns - 8), 4)]
    second[...] = stage_b[pl.ds(4 + core * (columns - 12), 4)]
    stencil.stage(2, stage_b, stage_a, 6, columns - 12)
    third[...] = stage_a[pl.ds(6, columns - 12)]


def far_kernel(
    total_x,
    fringe,
    own_here,
    own_there,
    across_here,
    across_there,
    around_here,
    around_there,
    far_here,
    far_there,
    first,
    second,
    third,
    thrust,
    piece_here,
    piece_there,
    source,
    start,
    stage_a,
    stage_b,
    stage_c,
    viscosity,
    faces,
    beside,
    columns_here,
    columns_there,
):
    cells_x = own_here.shape[0]
    near, far = across_here.shape[0], far_here.shape[0]
    _, _, tiles, rows, width = start.shape
    half = width // 2
    share_x = cells_x // 2
    inner = share_x + 1
    core = lax.axis_index("gy")

    def runs_of(side, parity):
        across, around = (across_here, across_there), (around_here, around_there)
        if side == 0:
            return (
                (0, far_here, far_there, 0, far),
                (far, *(around if parity == 0 else across), 0, near),
                (far + near, own_here, own_there, 0, inner),
            )
        return (
            (0, own_here, own_there, cells_x - inner, inner),
            (inner, *(across if parity == 0 else around), 0, near),
            (inner + near, far_here, far_there, 0, far),
        )

    place_columns(start, runs_of)
    stencil = Stencil(tiles, rows, width, viscosity, faces, thrust, start, beside)
    stencil.stage(0, start, stage_a, 2 + 4 * core, 4)
    stage_a[pl.ds(6 - 4 * core, 4)] = first[...]
    stencil.stage(1, stage_a, stage_b, 4, 4)
    stage_b[pl.ds(8 - 8 * core, 4)] = second[...]
    stencil.stage(2, stage_b, stage_c, 6 - 4 * core, 4)
    stage_c[pl.ds(10 - 10 * core, 2)] = third[...]

    origin = REACH - core * (REACH - 1)
    pairs = 3 * tiles // 2
    front = lax.broadcasted_iota(jnp.int32, (rows, half), 1) < half // 2
    for x in range(share_x):
        for c in range(3):
            for t in range(tiles):
                n = c * tiles + t
                field = stage_c[origin + x, c, t]
                even, odd = field[:, :half], pltpu.roll(field[:, half:], half // 2, 1)
                low, high = jnp.where(front, even, odd), jnp.where(front, odd, even)
                spot = pl.ds((((n % 2) * share_x + x) * pairs + n // 2) * rows, rows)
                columns_here[spot, :] = jnp.where(core == 0, low, high)
                columns_there[spot, :] = jnp.where(core == 0, high, low)
    for s in range(rows):
        for m in range(pairs):
            spot = pl.ds(m * rows + s, 2 * share_x, stride=pairs * rows)
            piece_here[s, m] = columns_here[spot, :]
            piece_there[s, m] = columns_there[spot, :]

    is_farm = lax.axis_index("sec") == 1
    corner = lax.axis_index("gx") * cells_x + core * share_x

    def weight(offset, dest):
        place = lax.rem(corner + offset + total_x, total_x)
        inside = jnp.logical_and(place >= fringe[0], place < fringe[1])
        blend = jnp.where(inside, FRINGE_BLEND, 0.0)
        share = jnp.where(is_farm, 1.0 - blend, blend)
        if dest == 0:
            share = jnp.where(is_farm, 0.0, 1.0)
        return 0.5 * share

    for x in range(share_x):
        i = origin + x
        upright = [stage_c[i, 2, t] for t in range(tiles)]
        for t in range(tiles):
            cross = stage_c[i, 1, t]
            plane = (stencil.next_y(cross) - stencil.last_y(cross)) + (
                stencil.next_z(upright, t) - stencil.last_z(upright, t)
            )
            after, before = stage_c[i + 1, 0, t], stage_c[i - 1, 0, t]
            for dest in range(2):
                source[pl.ds(((dest * share_x + x) * tiles + t) * rows, rows), :] = (
                    weight(x + 1, dest) * after
                    - weight(x - 1, dest) * before
                    + weight(x, dest) * plane
                )


def spectra_kernel(source, table_y, table_z, spectra, modes):
    _, groups, _, parts, rows, lanes = spectra.shape
    levels = table_z.shape[0]
    count, total_y = source.shape
    columns = count // levels
    along_y = dot(source[...], table_y[...])
    beside = [along_y[n * levels : (n + 1) * levels] for n in range(columns)]
    both = dot(table_z[...], jnp.concatenate(beside, axis=1))
    for n in range(columns):
        for h in range(2):
            first = n * total_y + h * lanes
            modes[h, pl.ds(n * levels, levels), :] = both[:, first : first + lanes]
    for dest in range(2):
        for h in range(2):
            for p in range(parts):
                first = dest * count // 2 + p * groups
                picked = [
                    modes[h, pl.ds(first + b, rows, stride=levels // 2), :] for b in range(groups)
                ]
                for g, block in enumerate(swap_blocks(picked, lanes // groups)):
                    spectra[dest, g, h, p] = block


def arrange_kernel(piece_here, piece_there, *blocks):
    groups, pairs, rows, lanes = piece_here.shape
    half = rows // 2
    low = lax.broadcasted_iota(jnp.int32, (rows, lanes), 0) < half
    is_first = lax.axis_index("gy") == 0
    order = parting(lanes, inverse=True)
    for distance, block in enumerate(blocks):
        g = lax.axis_index("gx") ^ distance
        merged = []
        for m in range(pairs):
            here, there = piece_here[g, m], piece_there[g, m]
            before = jnp.where(is_first, here, there)
            after = jnp.where(is_first, there, here)
            merged.append(jnp.where(low, before, pltpu.roll(after, half, 0)))
            merged.append(jnp.where(low, pltpu.roll(before, half, 0), after))
        values = reordered(jnp.concatenate(merged, axis=0), order)
        block[...] = values.reshape(block.shape)


def pencil_kernel(received, waves, table, packed):
    _, groups, cores, parts, rows, lanes = received.shape
    total_x = groups * rows
    lane_width = lanes // groups
    wave, base = 2 * total_x, table.shape[1]
    spread_z = table[:base]
    pair_x = table[base : base + wave, :wave]
    table_x = table[base : base + total_x, wave : wave + total_x]
    along_x = table[base : base + total_x, 2 * wave : 2 * wave + lanes]
    along_zy = waves[lax.axis_index("gx"), lax.axis_index("gy")]
    spectrum = jnp.concatenate(
        [(received[0, :, :, p] + received[1, :, :, p]).reshape(-1, lanes) for p in range(parts)],
        axis=1,
    )
    solved = dot(pair_x, spectrum)
    pieces = []
    for a in range(2 * parts):
        p, side = a % parts, a // parts
        block = solved[side * total_x : (side + 1) * total_x, p * lanes : (p + 1) * lanes]
        pieces.append(block / (along_x + along_zy[a : a + 1]))
    field = dot(dot(table_x, jnp.concatenate(pieces, axis=1)), spread_z)
    levels_of = [field[:, a * lanes : (a + 1) * lanes] for a in range(2 * parts)]
    wide = lax.broadcasted_iota(jnp.int32, (total_x // 2, lanes), 1)
    left = wide < lanes // 2
    quarter = total_x // 4
    block = lax.broadcasted_iota(jnp.int32, (quarter, lanes), 1) // lane_width
    for g in range(groups):
        a, odd = divmod(g, 2)
        now = levels_of[a]
        front, rear = now[: total_x // 2], now[total_x // 2 :]
        if odd:
            main = jnp.where(left, pltpu.roll(front, lanes // 2, 1), rear)
            lower, lower_lane = now, lanes // 2 - lane_width
            upper, upper_lane = levels_of[min(a + 1, 2 * parts - 1)], 0
        else:
            main = jnp.where(left, front, pltpu.roll(rear, lanes // 2, 1))
            lower, lower_lane = levels_of[max(a - 1, 0)], lanes - lane_width
            upper, upper_lane = now, lanes // 2
        edge = None
        for q in range(4):
            for n, (whole, lane) in enumerate(((lower, lower_lane), (upper, upper_lane))):
                spot = 2 * q + n
                move = (spot * lane_width - lane) % lanes
                rolled = whole[q * quarter : (q + 1) * quarter]
                if move:
                    rolled = pltpu.roll(rolled, move, 1)
                edge = rolled if edge is None else jnp.where(block == spot, rolled, edge)
        packed[g, : total_x // 2] = main
        packed[g, total_x // 2 : 3 * quarter] = edge


def levels_in(arrays, total_x, share):
    groups, rows, lanes = arrays.shape
    width, main_rows = lanes // groups, total_x // 2
    main = swap_blocks([arrays[s, :main_rows] for s in range(groups)], width)
    edge = swap_blocks([arrays[s, main_rows:rows] for s in range(groups)], width)
    inner = [x for n in range(share) for x in (main[n], main[share + n])]
    outer = [[edge[2 * q + n] for q in range(4)] for n in range(2)]
    return jnp.concatenate(outer[0] + inner + outer[1], axis=0)


def half_kernel(received, table_y, partial):
    groups, rows, lanes = received.shape
    total_x = 4 * rows // 3
    core = lax.axis_index("gy")
    share = partial.shape[0] // total_x - 2
    table = table_y[core, pl.ds(pl.multiple_of(core * lanes, lanes), lanes), :]
    partial[...] = dot(levels_in(received, total_x, share), table)


def project_kernel(partial, partner, table_y, blended, velocity_next, pressure):
    groups = partner.shape[0]
    share, total_x, lanes = pressure.shape
    place, core = lax.axis_index("gx"), lax.axis_index("gy")
    table = table_y[core, pl.ds(pl.multiple_of((1 - core) * lanes, lanes), lanes), :]
    both = partial[...] + dot(levels_in(partner, total_x, share), table)
    fields = [both[n * total_x : (n + 1) * total_x] for n in range(share + 2)]
    values = [f[:, :lanes] for f in fields]
    values[0] = jnp.where(place == 0, values[1], values[0])
    values[-1] = jnp.where(place == groups - 1, -values[-2], values[-1])
    for z in range(share):
        now = values[z + 1]
        pressure[z] = now
        slopes = [
            0.5 * (pltpu.roll(now, total_x - 1, 0) - pltpu.roll(now, 1, 0)),
            fields[z + 1][:, lanes:],
            0.5 * (values[z + 2] - values[z]),
        ]
        for c in range(3):
            velocity_next[c, z] = blended[c, z] - slopes[c]


def blend_kernel(fringe, moved, upstream, blended):
    _, share, total_x, lanes = blended.shape
    groups, _, cells_x, _ = moved.shape
    outlet = upstream.shape[0]
    is_farm = lax.axis_index("sec") == 1
    for s in range(groups):
        distance = lax.axis_index("gx") ^ s
        columns = s * cells_x + lax.broadcasted_iota(jnp.int32, (cells_x, lanes), 0)
        inside = jnp.logical_and(columns >= fringe[0], columns < fringe[1])
        blend = jnp.where(jnp.logical_and(inside, is_farm), FRINGE_BLEND, 0.0)
        for c in range(3):
            for z in range(share):
                own = moved[distance, c * share + z]
                if s >= groups - outlet:
                    own = own + blend * (upstream[s - groups + outlet, c * share + z] - own)
                blended[c, z, s * cells_x : (s + 1) * cells_x] = own


def cas(rows, columns, length):
    angle = (np.outer(rows, columns) % length) * (2.0 * np.pi / length)
    return np.cos(angle) + np.sin(angle)


def tables(levels, total_x, total_y, groups):
    half = total_y // 2
    lane_width = LANES // groups
    every_x = np.arange(total_x)
    every_y = np.arange(total_y)
    table_x = cas(every_x, every_x, total_x)
    table_y = cas(every_y, every_y, total_y)
    slope_y = 0.5 * (np.roll(table_y, -1, axis=1) - np.roll(table_y, 1, axis=1))
    level = np.arange(levels) + 0.5
    table_z = np.cos(np.outer(level, level) * (np.pi / levels))
    spread_z = np.kron(table_z, np.eye(lane_width))
    order = np.arange(levels).reshape(ROWS, levels // ROWS).T.reshape(levels)
    parted = np.concatenate([every_y[::2], every_y[1::2]])
    backward = [
        np.concatenate([table_y[:, here], slope_y[:, here]], axis=1)
        for here in (slice(0, half), slice(half, total_y))
    ]
    pair_x = np.einsum("kx,ab->akxb", table_x, np.eye(2)).reshape(2 * total_x, 2 * total_x)
    norm = levels / 2.0 * total_x * total_y
    wave_x = norm * (2.0 * np.cos(every_x * (2.0 * np.pi / total_x)) - 2.0)
    wave_y = norm * (2.0 * np.cos(every_y * (2.0 * np.pi / total_y)) - 2.0)
    wave_z = norm * (2.0 * np.cos(level * (np.pi / levels)) - 2.0)
    waves = wave_z.reshape(1, 1, -1, groups, 1) + wave_y.reshape(2, groups, 1, 1, lane_width)
    waves = waves.transpose(1, 0, 2, 3, 4).reshape(groups, 2, levels // groups, LANES)
    pencil = np.zeros((spread_z.shape[0] + 2 * total_x, spread_z.shape[1]))
    pencil[: spread_z.shape[0]] = spread_z
    pencil[spread_z.shape[0] :, : 2 * total_x] = pair_x
    pencil[spread_z.shape[0] : -total_x, 2 * total_x : 3 * total_x] = table_x
    pencil[spread_z.shape[0] : -total_x, 4 * total_x : 4 * total_x + LANES] = wave_x[:, None]
    return [
        jnp.asarray(t, jnp.float32)
        for t in (
            pencil,
            table_y[parted],
            np.stack(backward),
            table_z[:, order],
            waves,
        )
    ]


def call(kernel, out_shapes, scratch, *operands):
    in_specs = [
        pl.BlockSpec(memory_space=pltpu.SMEM if o.dtype == jnp.int32 else pltpu.VMEM)
        for o in operands
    ]
    return pl.pallas_call(
        kernel,
        out_shape=out_shapes,
        in_specs=in_specs,
        out_specs=jax.tree.map(lambda _: pl.BlockSpec(memory_space=pltpu.VMEM), out_shapes),
        scratch_shapes=scratch,
        compiler_params=pltpu.CompilerParams(vmem_limit_bytes=VMEM_BYTES),
    )(*operands)


def thrust_weights(turbine_cells, along_x, along_y, along_z, total_y, strength):
    matches = (along_x[:, None] == turbine_cells[None, :, 0]).astype(jnp.bfloat16)
    offset_y = (along_y[None, :] - turbine_cells[:, 1:2] + total_y // 2) % total_y - total_y // 2
    offset_z = along_z[None, :] - turbine_cells[:, 2:3]
    distance = (
        offset_z[:, :, None] * offset_z[:, :, None] + offset_y[:, None, :] * offset_y[:, None, :]
    )
    inside = (distance <= RADIUS * RADIUS).astype(jnp.bfloat16)
    count = jnp.einsum("xt,tzy->xzy", matches, inside, preferred_element_type=jnp.float32)
    return strength * count


def paired_plan(velocity, turbine_cells, fringe_bounds):
    groups = lax.axis_size("gx")
    initial = velocity[0]
    _, levels, cells_x, cells_y = initial.shape
    total_x, total_y = cells_x * groups, 2 * cells_y
    share, share_x = levels // ROWS, cells_x // 2
    section, place, core = (lax.axis_index("sec"), lax.axis_index("gx"), lax.axis_index("gy"))
    pencil, table_y, backward, table_z, waves = tables(levels, total_x, total_y, groups)

    near, far = REACH - 4, 4
    up = [(i, (i + 1) % groups) for i in range(groups)]
    down = [(j, i) for i, j in up]
    swap = [(0, 1), (1, 0)]
    straight = [(2 * i, 2 * j) for i, j in up] + [(2 * j + 1, 2 * i + 1) for i, j in up]
    crossed = [(2 * i + 1, 2 * j) for i, j in up] + [(2 * j, 2 * i + 1) for i, j in up]
    pairs_across = [(i, i ^ 1) for i in range(groups)]
    pairs_around = [(i, (i - 1 if i % 2 == 0 else i + 1) % groups) for i in range(groups)]
    f32 = jnp.float32
    flat = initial.reshape(-1, cells_y)

    def narrow(count):
        return jax.ShapeDtypeStruct((count, 3, share, ROWS, cells_y), f32)

    lower, upper = call(
        functools.partial(pack_near_kernel, cells_x), [narrow(near)] * 2, [], flat
    )
    around = lax.ppermute(lower, "gx", pairs_around)
    across = lax.ppermute(upper, "gx", pairs_across)
    own, same, other = call(
        pack_kernel, [narrow(cells_x), narrow(far), narrow(far)], [], flat
    )
    own_there = lax.ppermute(own, "gy", swap)
    other, across = lax.optimization_barrier((other, across))
    far_there = lax.ppermute(other, ("gx", "gy"), crossed)
    across_there = lax.ppermute(across, "gy", swap)
    around_there = lax.ppermute(around, "gy", swap)

    strength = 2.0 * THRUST_COEFF * section.astype(jnp.float32)
    along_z = jnp.arange(levels).reshape(ROWS, share).T.reshape(levels)
    along_y = jnp.arange(total_y).reshape(cells_y, 2).T.reshape(total_y)

    def thrust_on(offset, count):
        along_x = (place * cells_x + offset + jnp.arange(count) + total_x) % total_x
        weights = thrust_weights(
            turbine_cells, along_x, along_y, along_z, total_y, strength
        )
        return weights.reshape(count, share, ROWS, total_y)

    near_thrust = thrust_on(2 - near, cells_x + 2 * near - 4)
    far_thrust = thrust_on((2 - REACH) * (1 - core) + (share_x + 1) * core, far + near + share_x - 3)
    far_here = lax.ppermute(same, ("gx", "gy"), straight)
    body = (3, share, ROWS, total_y)

    def columns(count):
        return pltpu.VMEM((count,) + body, f32)

    reached = cells_x + 2 * near
    shapes = [jax.ShapeDtypeStruct((n,) + body, f32) for n in (4, 4, reached - 12)]
    first, second, third = call(
        near_kernel,
        shapes,
        [columns(reached)] * 3
        + [pltpu.VMEM((reached,) + body[1:], f32), pltpu.VMEM(body, f32), columns(reached)],
        own,
        own_there,
        across,
        across_there,
        around,
        around_there,
        near_thrust,
    )
    window = far + near + share_x + 1
    pairs = 3 * share // 2
    piece = jax.ShapeDtypeStruct((ROWS, pairs, 2 * share_x, cells_y), f32)
    parts = levels // (2 * groups)
    piece_here, piece_send, source = call(
        functools.partial(far_kernel, total_x),
        [piece, piece, jax.ShapeDtypeStruct((2 * share_x * levels, total_y), f32)],
        [columns(window)] * 4
        + [
            pltpu.VMEM((window,) + body[1:], f32),
            pltpu.VMEM(body, f32),
            columns(window),
            pltpu.VMEM((share_x * 3 * levels, cells_y), f32),
            pltpu.VMEM((share_x * 3 * levels, cells_y), f32),
        ],
        fringe_bounds,
        own,
        own_there,
        across,
        across_there,
        around,
        around_there,
        far_here,
        far_there,
        first,
        second,
        third,
        far_thrust,
    )
    piece_there = lax.ppermute(piece_send, "gy", swap)
    spectra = call(
        spectra_kernel,
        jax.ShapeDtypeStruct((2, groups, 2, parts, 2 * share_x, LANES), f32),
        [pltpu.VMEM((2, 2 * share_x * levels, LANES), f32)],
        source,
        table_y,
        table_z,
    )
    received = lax.all_to_all(
        spectra.reshape((4 * groups,) + spectra.shape[3:]), ("sec", "gx", "gy"), 0, 0, tiled=True
    ).reshape(spectra.shape)
    blocks = call(
        arrange_kernel,
        [jax.ShapeDtypeStruct((3 * share, cells_x, cells_y), f32)] * groups,
        [],
        piece_here,
        piece_there,
    )
    moved = [blocks[0]] + [
        lax.ppermute(block, "gx", [(i, i ^ d) for i in range(groups)])
        for d, block in enumerate(blocks)
        if d
    ]
    packed = call(
        pencil_kernel,
        jax.ShapeDtypeStruct((groups, 3 * total_x // 4, LANES), f32),
        [],
        received,
        waves,
        pencil,
    )
    tied = [3, 4, 5]
    packed, *some = lax.optimization_barrier([packed] + [moved[d] for d in tied])
    for d, block in zip(tied, some):
        moved[d] = block
    moved = jnp.stack(moved)
    outlet = groups // 4
    leaving = jnp.stack(
        [
            lax.dynamic_index_in_dim(moved, place ^ s, 0, keepdims=False)
            for s in range(groups - outlet, groups)
        ]
    )
    upstream = lax.ppermute(leaving, "sec", [(0, 1)])
    returned = lax.all_to_all(packed, "gx", 0, 0, tiled=True)
    returned, upstream = lax.optimization_barrier((returned, upstream))
    partner = lax.ppermute(returned, "gy", swap)
    blended = call(
        blend_kernel,
        jax.ShapeDtypeStruct((3, share, total_x, cells_y), f32),
        [],
        fringe_bounds,
        moved,
        upstream,
    )
    partial = call(
        half_kernel,
        jax.ShapeDtypeStruct(((share + 2) * total_x, 2 * cells_y), f32),
        [],
        returned,
        backward,
    )
    velocity_next, pressure = call(
        project_kernel,
        [
            jax.ShapeDtypeStruct((3, share, total_x, cells_y), f32),
            jax.ShapeDtypeStruct((share, total_x, cells_y), f32),
        ],
        [],
        partial,
        partner,
        backward,
        blended,
    )
    return (velocity_next[None], pressure[None])


def on_device(velocity, turbine_cells, fringe_bounds):
    groups = lax.axis_size("gx")
    _, _, levels, cells_x, cells_y = velocity.shape
    paired = (
        lax.axis_size("gy") == 2
        and lax.axis_size("sec") == 2
        and cells_y == LANES
        and cells_x == ROWS
        and groups == ROWS
        and 2 * levels == groups * groups
    )
    plan = paired_plan if paired else general_plan
    return plan(velocity, turbine_cells, fringe_bounds)


def solution(mesh):
    return jax.shard_map(
        on_device,
        mesh=mesh,
        in_specs=(P("sec", None, None, "gx", "gy"), P(), P()),
        out_specs=(P("sec", None, "gx", None, "gy"), P("sec", "gx", None, "gy")),
        check_vma=False,
    )
```
